32 devices in a mesh: rep: 2 (over x), dom: 16 (over z, y, core).
Axes of the slice: x: 2, y: 2, z: 4, core: 2. Of those that a mesh axis runs over, the one named last changes fastest.
Arguments:
- positions: float32 [3, 32768], P(None, ('rep', 'dom')), parts along dimension 1, may hold values from -6 to 6
- species: int32 [32768], P(('rep', 'dom')), parts along dimension 0, may hold values from 0 to 7
- live_bins: int32 [32], P(('rep', 'dom')), parts along dimension 0, may hold values from 16 to 64, as said below
- edge_nbr: int32 [1048576], P(('rep', 'dom')), parts along dimension 0, may hold values from 0 to 1791, as said below
- ghost_index: int32 [6, 4096], P(None, ('rep', 'dom')), parts along dimension 1, may hold values from 0 to 1023, as said below
- zeta_table: float32 [8], replicated, may hold values from 0.5 to 2
- energy_scale: float32 [8], replicated, may hold values from 0.5 to 2
- center_embed: float32 [64, 8], replicated, may hold values from -6 to 6
- nbr_embed: float32 [64], replicated, may hold values from -6 to 6
- radial_weight: float32 [64, 8], replicated, may hold values from -2 to 2
- latent_weight: float32 [64, 64], replicated, may hold values from -0.75 to 0.75
- env_weight: float32 [64, 64], replicated, may hold values from -0.75 to 0.75
- mix_weight: float32 [64, 128], replicated, may hold values from -0.5 to 0.5
- out_weight: float32 [64], replicated, may hold values from -0.75 to 0.75
Outputs:
- forces: float32 [3, 32768], P(None, ('rep', 'dom')), parts along dimension 1
The draws below stay inside these ranges and needn't reach their ends.
There are 2 independent parts, one for each index of `rep`. The reference program is written for one: setup_inputs(seed, part) draws one part's arguments, and reference() takes and returns one part's arrays. A program takes and returns all parts, laid end to end along the dimension named above; an argument that names none is the same for every part. Nothing has to cross between parts.
Inputs may be any that keep to these rules, and one draw needn't show every extreme that they name: Bins below live_bins[d] of domain d are occupied and the others are empty; some domain has all 64 occupied. `edge_nbr`: values below 1024 name an atom of an occupied bin of the same domain; a value v of 1024 or more names ghost slot v - 1024, 128 slots a face in face order. Edges of even-numbered bins name the domain's own atoms only. `ghost_index`: every entry names an atom of an occupied bin of the sending domain.
All inputs are finite; a program needn't handle non-finite values.
Results may differ from the reference program's by a relative error of at most 0.0003.
Values sent between devices are 32-bit elements; how exact they have to be, the bound alone decides.
No kernel may reach another device: no remote copies, remote signals or barrier semaphores. Data moves between devices by JAX's collectives and lax.ppermute only.
A program may use at most 128 MiB of HBM per device.

```python
import math
import jax
import jax.numpy as jnp
from jax import lax

LAT = 64
NBASIS = 8
NSPEC = 8
NBR = 32
BIN_ATOMS = 16
BINS = 64
GHOST = 128
ATOM_DEV = 1024
BIN_EDGES = 512
ATOMS = 16384
N_DOM = 16


def occupancy(key):
    key = jax.random.fold_in(key, 5)
    key_low, key_high, key_pick, key_order = jax.random.split(key, 4)
    low_fill = jax.random.randint(key_low, (N_DOM,), BINS // 4, BINS // 2 + 1)
    high_fill = jax.random.randint(key_high, (N_DOM,), BINS // 2, BINS + 1)
    picker = jax.random.randint(key_pick, (N_DOM,), 0, 8)
    occupied = jnp.where(picker == 0, high_fill, low_fill)
    shuffled = jax.random.permutation(key_order, N_DOM)
    occupied = occupied.at[shuffled[0]].set(BINS).at[shuffled[1]].set(BINS // 4)
    return (occupied.astype(jnp.int32), shuffled[0])


def draw_live_bins(key, part):
    occupied, fullest = occupancy(key)
    return occupied


def draw_edge_nbr(key, part):
    occupied, fullest = occupancy(key)
    key = jax.random.fold_in(key, 7)
    key_own, key_ghost, key_coin = jax.random.split(key, 3)
    shape = (N_DOM, BINS, BIN_EDGES)
    limit = (occupied * BIN_ATOMS)[:, None, None]
    own_pick = jax.random.randint(key_own, shape, 0, limit)
    ghost_pick = ATOM_DEV + jax.random.randint(key_ghost, shape, 0, 6 * GHOST)
    coin_flip = jax.random.randint(key_coin, shape, 0, 2)
    odd_bins = (jnp.arange(BINS) % 2 == 1)[None, :, None]
    chosen = jnp.where(odd_bins & (coin_flip == 1), ghost_pick, own_pick)
    chosen = chosen.at[fullest, 1, 0].set(ATOM_DEV + 6 * GHOST - 1).at[fullest, 0, 0].set(0)
    return chosen.reshape(N_DOM * BINS * BIN_EDGES).astype(jnp.int32)


def draw_ghost_index(key, part):
    occupied, fullest = occupancy(key)
    key = jax.random.fold_in(key, 9)
    limit = (occupied * BIN_ATOMS)[None, :, None]
    chosen = jax.random.randint(key, (6, N_DOM, GHOST), 0, limit)
    chosen = chosen.at[0, fullest, 0].set(ATOM_DEV - 1).at[0, fullest, 1].set(0)
    return chosen.reshape(6, N_DOM * GHOST).astype(jnp.int32)


def draw_radial_weight(key, part):
    key = jax.random.fold_in(key, 11)
    key_low, key_high, key_sign = jax.random.split(key, 3)
    row_ids = jnp.arange(LAT)[:, None]
    col_ids = jnp.arange(NBASIS)[None, :]
    low_part = jnp.clip(jax.random.normal(key_low, (LAT, NBASIS), jnp.float32) * NBASIS ** (-0.5), -2.0, 2.0)
    high_part = jax.random.uniform(key_high, (LAT, NBASIS), jnp.float32, -2.0, 2.0)
    planted = jnp.where(jax.random.randint(key_sign, (LAT, NBASIS), 0, 2) == 1, 2.0, -2.0)
    high_part = jnp.where(row_ids % 4 == 0, planted, high_part)
    return jnp.where(col_ids >= NBASIS - 3, high_part, low_part).astype(jnp.float32)


def set_ends(array, rng, smallest, largest):
    extent = array.shape
    index_at = [jax.random.randint(jax.random.fold_in(rng, axis), (), 0, extent[axis]) for axis in range(len(extent))]
    array = array.at[tuple(index_at)].set(smallest)
    longest = extent.index(max(extent))
    index_at[longest] = (index_at[longest] + 1) % extent[longest]
    return array.at[tuple(index_at)].set(largest)


def levels(stream_key, extent, cuts, smallest, largest):
    def one(position, parts):
        draws = jax.random.uniform(jax.random.fold_in(jax.random.fold_in(stream_key, 6), position), (parts,), jnp.float32, smallest / len(cuts), largest / len(cuts))
        return jnp.repeat(jnp.exp(draws), extent[position] // parts).reshape((-1,) + (1,) * (len(extent) - position - 1))

    gain = one(*cuts[0])
    for cut in cuts[1:]:
        gain = gain * one(*cut)
    return gain


def noise(rng, shape, deviation, most, cuts=(), held_as=jnp.bfloat16):
    values = jax.random.normal(rng, shape, jnp.float32) * deviation
    if len(cuts) > 0:
        values = levels(rng, shape, cuts, -0.22, 0.18) * values
    return jnp.clip(values, min=-most, max=most).astype(held_as)


def setup_inputs(seed: int = 0, part: int = 0) -> dict:
    keys = jax.random.split(jax.random.key(seed), 15)
    part_splits = jax.random.split(jax.random.fold_in(keys[14], part), 15)
    positions = noise(part_splits[0], (3, ATOMS), 1.5, 6.0, ((1, 16),), jnp.float32)
    species = set_ends(jax.random.randint(part_splits[1], (ATOMS,), 0, NSPEC), jax.random.fold_in(part_splits[1], 1), 0, NSPEC - 1).astype(jnp.int32)
    live_bins = draw_live_bins(jax.random.fold_in(jax.random.fold_in(keys[14], part), 71), part)
    edge_nbr = draw_edge_nbr(jax.random.fold_in(jax.random.fold_in(keys[14], part), 71), part)
    ghost_index = draw_ghost_index(jax.random.fold_in(jax.random.fold_in(keys[14], part), 71), part)
    zeta_table = jnp.clip(jnp.exp(jax.random.uniform(keys[5], (NSPEC,), jnp.float32, math.log(0.5), math.log(2.0))), 0.5, 2.0)
    energy_scale = jnp.clip(jnp.exp(jax.random.uniform(keys[6], (NSPEC,), jnp.float32, math.log(0.5), math.log(2.0))), 0.5, 2.0)
    center_embed = noise(keys[7], (LAT, NSPEC), 1.0, 6.0, (), jnp.float32)
    nbr_embed = noise(keys[8], (LAT,), 1.0, 6.0, (), jnp.float32)
    radial_weight = draw_radial_weight(jax.random.fold_in(keys[14], 71), part)
    latent_weight = noise(keys[10], (LAT, LAT), LAT ** -0.5, 0.75, (), jnp.float32)
    env_weight = noise(keys[11], (LAT, LAT), LAT ** -0.5, 0.75, (), jnp.float32)
    mix_weight = noise(keys[12], (LAT, 2 * LAT), (2 * LAT) ** -0.5, 0.5, (), jnp.float32)
    out_weight = noise(keys[13], (LAT,), LAT ** -0.5, 0.75, (), jnp.float32)
    return dict(positions=positions, species=species, live_bins=live_bins, edge_nbr=edge_nbr, ghost_index=ghost_index, zeta_table=zeta_table, energy_scale=energy_scale, center_embed=center_embed, nbr_embed=nbr_embed, radial_weight=radial_weight, latent_weight=latent_weight, env_weight=env_weight, mix_weight=mix_weight, out_weight=out_weight)


FACES = ((1, 0, -1.0), (-1, 0, 1.0), (2, 1, -1.0), (-2, 1, 1.0), (8, 2, -1.0), (-8, 2, 1.0))
CUTOFF = 6.0
SOFTEN = 0.5
BOX_SHIFT = 3.0
PRECISE = lax.Precision.HIGHEST

def product(left, right):
    return jnp.dot(left, right, precision=PRECISE, preferred_element_type=jnp.float32)

def bin_energy(geometry, center_kinds, params):
    energy_scale, center_embed, nbr_embed, radial_weight, latent_weight, env_weight, mix_weight, out_weight = params
    channels = latent_weight.shape[0]
    kind_count = energy_scale.shape[0]
    atom_total = center_kinds.shape[0]
    per_atom = geometry.shape[1] // atom_total
    displace = geometry[:3]
    zeta_edge = geometry[3]
    distance = jnp.sqrt(lax.optimization_barrier(jnp.sum(displace * displace, axis=0)) + SOFTEN * SOFTEN)
    unit_vec = displace / distance
    scaled = jnp.minimum(distance / CUTOFF, 1.0)
    envelope = jnp.square(1.0 - scaled * scaled)
    orders = jnp.arange(1, radial_weight.shape[1] + 1).astype(jnp.float32)[:, None]
    radial_basis = jnp.sin(math.pi * orders * scaled) / scaled * envelope
    kind_table = (center_kinds[None, :] == jnp.arange(kind_count, dtype=jnp.int32)[:, None]).astype(jnp.float32)
    center_term = jnp.repeat(product(center_embed, kind_table), per_atom, axis=1)
    preact = product(radial_weight, radial_basis) + center_term + nbr_embed[:, None] * zeta_edge
    first_latent = jax.nn.silu(preact)
    second = jax.nn.silu(product(latent_weight, first_latent))
    weights = product(env_weight, second) * envelope
    weight_grid = weights.reshape(channels, atom_total, per_atom)
    unit_grid = unit_vec.reshape(3, atom_total, per_atom)
    env_vector = jnp.einsum('lcn,mcn->mlc', weight_grid, unit_grid, precision=PRECISE) * per_atom ** (-0.5)
    invariant = jnp.einsum('mlc,mcn->lcn', env_vector, unit_grid, precision=PRECISE).reshape(channels, atom_total * per_atom)
    third_latent = jax.nn.silu(product(mix_weight[:, :channels], second) + product(mix_weight[:, channels:], invariant)) + second
    edge_energy = product(out_weight[None, :], third_latent)[0] * envelope
    center_scale = product(energy_scale[None, :], kind_table)[0]
    return jnp.sum(edge_energy.reshape(atom_total, per_atom) * center_scale[:, None])

def bin_force(geometry, center_kinds, params):
    return jax.grad(bin_energy)(geometry, center_kinds, params)[:3]

def add_at(target, columns, values):
    return target.at[:, columns].add(values)

def reference(positions, species, live_bins, edge_nbr, ghost_index, zeta_table, energy_scale, center_embed, nbr_embed, radial_weight, latent_weight, env_weight, mix_weight, out_weight):
    params = (energy_scale, center_embed, nbr_embed, radial_weight, latent_weight, env_weight, mix_weight, out_weight)
    kind_count = zeta_table.shape[0]
    kind_table = (species[None, :] == jnp.arange(kind_count, dtype=jnp.int32)[:, None]).astype(jnp.float32)
    atom_zeta = product(zeta_table[None, :], kind_table)
    atom_data = jnp.concatenate([positions, atom_zeta], axis=0).reshape(4, N_DOM, ATOM_DEV).transpose(1, 0, 2)
    ghost_lists = ghost_index.reshape(6, N_DOM, GHOST)
    pieces = [atom_data]
    for face_num, (offset, direction, polarity) in enumerate(FACES):
        outgoing = jnp.take_along_axis(atom_data, ghost_lists[face_num][:, None, :], axis=2)
        arrived = jnp.roll(outgoing, offset, axis=0)
        pieces.append(arrived.at[:, direction, :].add(polarity * BOX_SHIFT))
    slot_data = jnp.concatenate(pieces, axis=2)
    neighbours = edge_nbr.reshape(N_DOM, BINS * BIN_EDGES)
    kinds_dev = species.reshape(N_DOM, ATOM_DEV)

    def domain(inputs):
        slot_dev, nbr_dev, kind_dev, occupied = inputs
        remote = jnp.take(slot_dev, nbr_dev, axis=1)
        centers = jnp.repeat(slot_dev[:3, :ATOM_DEV], NBR, axis=1)
        geometry = jnp.concatenate([remote[:3] - centers, remote[3:]], axis=0)

        def one_bin(bin_num):
            geo_bin = lax.dynamic_slice_in_dim(geometry, bin_num * BIN_EDGES, BIN_EDGES, 1)
            kind_bin = lax.dynamic_slice_in_dim(kind_dev, bin_num * BIN_ATOMS, BIN_ATOMS, 0)
            return jnp.where(bin_num < occupied, bin_force(geo_bin, kind_bin, params), 0.0)
        gradients = lax.map(one_bin, jnp.arange(BINS, dtype=jnp.int32))
        gradients = gradients.transpose(1, 0, 2).reshape(3, BINS * BIN_EDGES)
        own_part = gradients.reshape(3, ATOM_DEV, NBR).sum(axis=2)
        slot_force = jnp.zeros((3, slot_dev.shape[1]), jnp.float32).at[:, nbr_dev].add(-gradients)
        return (own_part + slot_force[:, :ATOM_DEV], slot_force[:, ATOM_DEV:])
    forces, ghost_force = lax.map(domain, (slot_data, neighbours, kinds_dev, live_bins))
    for face_num, (offset, direction, polarity) in enumerate(FACES):
        ghost_part = ghost_force[:, :, face_num * GHOST:(face_num + 1) * GHOST]
        returned = jnp.roll(ghost_part, -offset, axis=0)
        forces = jax.vmap(add_at)(forces, ghost_lists[face_num], returned)
    return forces.transpose(1, 0, 2).reshape(3, ATOMS)
```

```python
import functools
import math

import jax
import jax.numpy as jnp
from jax import lax
from jax.experimental import pallas as pl
from jax.experimental.pallas import tpu as pltpu
from jax.sharding import PartitionSpec as P

NBR = 32
BIN_ATOMS = 16
LANES = 128

FACES = ((1, 0, -1.0), (-1, 0, 1.0), (2, 1, -1.0), (-2, 1, 1.0), (8, 2, -1.0), (-8, 2, 1.0))
CUTOFF = 6.0
SOFTEN = 0.5
BOX_SHIFT = 3.0
F32 = jnp.float32
BF16 = jnp.bfloat16

SIN_TERMS = [(-1.0) ** i / math.factorial(2 * i + 1) for i in range(8)]
COS_TERMS = [(-1.0) ** i / math.factorial(2 * i) for i in range(8)]


def from_behind(block, axis, distance):
    devices = range(lax.axis_size(axis))
    route = [((i - distance) % len(devices), i) for i in devices]
    return lax.ppermute(block, axis, route)


def poly(terms, square):
    total = jnp.full_like(square, terms[-1])
    for term in terms[-2::-1]:
        total = total * square + term
    return total


def halves(x):
    top = x.astype(BF16)
    return top, (x - top.astype(F32)).astype(BF16)


def wide(x):
    top, rest = halves(x)
    return jnp.concatenate([top, top, rest], axis=1)


def stacked(parts):
    cols = []
    for x in parts:
        top, rest = halves(x)
        cols.append(jnp.concatenate([top, rest, top], axis=0))
    return jnp.concatenate(cols, axis=1)


def mm(left, right):
    return jnp.dot(left, right, preferred_element_type=F32)


def mm_nt(left, right):
    return lax.dot_general(left, right, (((1,), (1,)), ((), ())), preferred_element_type=F32)


def split_cols(x):
    return [x[:, i * LANES : (i + 1) * LANES] for i in range(x.shape[1] // LANES)]


def lookup(row, index):
    return jnp.take_along_axis(
        jnp.broadcast_to(row, index.shape), index, axis=1, mode="promise_in_bounds"
    )


def prep_kernel(zeta_table, pos, species, ghost_index, zeta_out, *faces):
    kinds = species[...]
    zeta = jnp.zeros(kinds.shape, F32)
    for k in range(zeta_table.shape[0]):
        zeta = jnp.where(kinds == k, zeta_table[k], zeta)
    zeta_out[...] = zeta
    tiles = pos.shape[1] // LANES
    index = ghost_index[...]
    index = jnp.concatenate([index, index[:2]], axis=0)
    low, high = index & (LANES - 1), index >> 7
    for d in range(4):
        got = jnp.zeros(index.shape, F32)
        for t in range(tiles):
            lane = slice(t * LANES, (t + 1) * LANES)
            row = pos[d : d + 1, lane] if d < 3 else zeta[:, lane]
            got = jnp.where(high == t, lookup(row, low), got)
        for f, (_, direction, polarity) in enumerate(FACES):
            part = got[f : f + 1]
            if direction == d:
                part = part + polarity * BOX_SHIFT
            faces[f][d : d + 1, :] = part


def weights_kernel(
    center_embed, nbr_embed, radial, latent, env, mix, out, w1_o, w2_o, w3_o, w4_o, w5_o, w6_o, w7_o, w8_o
):
    chan = latent.shape[0]
    nb = radial.shape[1]
    first = jnp.concatenate(
        [0.5 * radial[...], 0.5 * nbr_embed[...], jnp.zeros((chan, 15 - nb), F32)], axis=1
    )
    top, rest = halves(0.5 * center_embed[...])
    w1_o[...] = jnp.concatenate([wide(first), top, rest], axis=1)
    w2_o[...] = wide(0.5 * latent[...])
    mix_a = mix[:, :chan]
    mix_b = mix[:, chan:]
    row = out[...]
    w3_o[...] = wide(
        jnp.concatenate([env[...], 0.5 * mix_a, row, jnp.zeros((15, chan), F32)], axis=0)
    )
    w4_o[...] = wide(0.5 * mix_b)
    w5_o[...] = wide(jnp.concatenate([mix_b.T * row, mix_a.T * row], axis=0))
    w6_o[...] = wide(env[...].T)
    w7_o[...] = wide(latent[...].T)
    pad = jnp.concatenate([radial[...], jnp.zeros((chan, 16 - nb), F32)], axis=1)
    w8_o[...] = wide(pad.T)


def edge_kernel(
    live,
    escale,
    pos,
    zeta,
    species,
    nbr,
    *refs,
    per,
    nfaces,
):
    ghosts = refs[:nfaces]
    w1, w2, w3, w4, w5, w6, w7, w8, out_col = refs[nfaces : nfaces + 9]
    own_out = refs[nfaces + 9]
    ghost_out = refs[nfaces + 10 : 2 * nfaces + 10]
    (
        basis_s,
        geo_s,
        red_s,
        db_s,
        df1_s,
        df2_s,
        y_s,
        pa_s,
        fa_s,
        env_s,
        denv_s,
        acc_s,
        own_s,
    ) = refs[2 * nfaces + 10 :]
    chan = out_col.shape[0]
    atoms = pos.shape[1]
    own_tiles = atoms // LANES
    tiles = own_tiles + nfaces
    rows16 = acc_s.shape[0] // 6
    steps = NBR // per
    norm = NBR ** (-0.5)
    acc_s[...] = jnp.zeros(acc_s.shape, F32)
    own_s[...] = jnp.zeros(own_s.shape, F32)
    occupied = live[0] * BIN_ATOMS

    def block(b, carry):
        base = pl.multiple_of(b * LANES, LANES)
        cols = pl.ds(base, LANES)
        index = nbr[:, cols]
        low, high = index & (LANES - 1), index >> 7
        kinds = species[:, cols]

        got = []
        for d in range(4):
            value = jnp.zeros((NBR, LANES), F32)
            for t in range(tiles):
                if t < own_tiles:
                    lane = slice(t * LANES, (t + 1) * LANES)
                    row = pos[d : d + 1, lane] if d < 3 else zeta[:, lane]
                else:
                    row = ghosts[t - own_tiles][d : d + 1, :]
                value = jnp.where(high == t, lookup(row, low), value)
            got.append(value)
        disp = [got[d] - pos[d : d + 1, cols] for d in range(3)]
        square = disp[0] * disp[0] + disp[1] * disp[1] + disp[2] * disp[2]
        dist = jnp.sqrt(square + SOFTEN * SOFTEN)
        inv_dist = 1.0 / dist
        unit = [disp[d] * inv_dist for d in range(3)]
        x = jnp.minimum(dist * (1.0 / CUTOFF), 1.0)
        inv_x = 1.0 / x
        gap = 1.0 - x * x
        envelope = gap * gap
        t = math.pi * (x - 0.5)
        tt = t * t
        s1 = poly(COS_TERMS, tt)
        c1 = -(t * poly(SIN_TERMS, tt))
        sins, coss = [s1], [c1]
        for k in range(2, 9):
            i, j = k // 2 - 1, k - k // 2 - 1
            sins.append(sins[i] * coss[j] + coss[i] * sins[j])
            coss.append(coss[i] * coss[j] - sins[i] * sins[j])
        scale = envelope * inv_x
        for k in range(8):
            basis_s[pl.ds(k, NBR, stride=16), :] = sins[k] * scale
        basis_s[pl.ds(8, NBR, stride=16), :] = got[3]
        for k in range(9, 16):
            basis_s[pl.ds(k, NBR, stride=16), :] = jnp.zeros((NBR, LANES), F32)
        for d in range(3):
            geo_s[d] = unit[d]
            geo_s[3 + d] = unit[d] * envelope

        kind8 = lax.broadcasted_iota(jnp.int32, (8, LANES), 0) == kinds
        onehot = kind8.astype(F32)
        onehot = jnp.concatenate([onehot, onehot], axis=0).astype(BF16)

        env_s[...] = jnp.zeros(env_s.shape, F32)
        denv_s[...] = jnp.zeros(denv_s.shape, F32)

        def slope(z, u, f):
            half = 0.5 * u
            return half + f * (1.0 - half)

        def ahead(g, c):
            ns = [g * per + i for i in range(per)]
            cols = []
            for n in ns:
                r = basis_s[pl.ds(pl.multiple_of(n * 16, 16), 16), :]
                top, rest = halves(r)
                cols.append(jnp.concatenate([top, rest, top, onehot], axis=0))
            z1 = split_cols(mm(w1[...], jnp.concatenate(cols, axis=1)))
            f1 = []
            for n, z in zip(ns, z1):
                u = 1.0 + jnp.tanh(z)
                f = z * u
                df1_s[n] = slope(z, u, f)
                f1.append(f)
            z2 = split_cols(mm(w2[...], stacked(f1)))
            f2 = []
            for n, z in zip(ns, z2):
                u = 1.0 + jnp.tanh(z)
                f = z * u
                df2_s[n] = slope(z, u, f)
                f2.append(f)
            third = split_cols(mm(w3[...], stacked(f2)))
            sums = [None] * 3
            for n, v in zip(ns, third):
                y = v[:chan]
                y_s[n] = y
                pa_s[n] = v[chan : 2 * chan]
                red_s[6, pl.ds(n, 1), :] = v[2 * chan : 2 * chan + 1]
                for d in range(3):
                    term = y * geo_s[3 + d, pl.ds(n, 1), :]
                    sums[d] = term if sums[d] is None else sums[d] + term
            for d in range(3):
                env_s[d] += sums[d]
            return c

        lax.fori_loop(0, steps, ahead, 0)
        for d in range(3):
            env_s[d] *= norm

        def middle(g, c):
            ns = [g * per + i for i in range(per)]
            inv = []
            for n in ns:
                v = env_s[0] * geo_s[0, pl.ds(n, 1), :]
                for d in range(1, 3):
                    v = v + env_s[d] * geo_s[d, pl.ds(n, 1), :]
                inv.append(v)
            z3 = split_cols(mm(w4[...], stacked(inv)))
            slopes = []
            for n, z in zip(ns, z3):
                z = z + pa_s[n]
                u = 1.0 + jnp.tanh(z)
                f = z * u
                red_s[6, pl.ds(n, 1), :] += jnp.sum(f * out_col[...], axis=0, keepdims=True)
                slopes.append(slope(z, u, f))
            back = split_cols(mm(w5[...], stacked(slopes)))
            sums = [None] * 3
            for n, v in zip(ns, back):
                dinv = v[:chan]
                fa_s[n] = v[chan:]
                for d in range(3):
                    term = dinv * geo_s[3 + d, pl.ds(n, 1), :]
                    sums[d] = term if sums[d] is None else sums[d] + term
                    red_s[d, pl.ds(n, 1), :] = jnp.sum(env_s[d] * dinv, axis=0, keepdims=True)
            for d in range(3):
                denv_s[d] += sums[d]
            return c

        lax.fori_loop(0, steps, middle, 0)
        for d in range(3):
            denv_s[d] *= norm

        def behind(g, c):
            ns = [g * per + i for i in range(per)]
            dy = []
            for n in ns:
                y = y_s[n]
                v = None
                for d in range(3):
                    term = denv_s[d] * geo_s[d, pl.ds(n, 1), :]
                    v = term if v is None else v + term
                    red_s[3 + d, pl.ds(n, 1), :] = jnp.sum(denv_s[d] * y, axis=0, keepdims=True)
                dy.append(v)
            d2 = split_cols(mm(w6[...], stacked(dy)))
            da2 = []
            for n, v in zip(ns, d2):
                da2.append((v + fa_s[n] + out_col[...]) * df2_s[n])
            d1 = split_cols(mm(w7[...], stacked(da2)))
            da1 = [v * df1_s[n] for n, v in zip(ns, d1)]
            db = split_cols(mm(w8[...], stacked(da1)))
            for n, v in zip(ns, db):
                db_s[pl.ds(pl.multiple_of(n * 8, 8), 8), :] = v[:8]
            return c

        lax.fori_loop(0, steps, behind, 0)

        d_unit = [envelope * (red_s[d] + red_s[3 + d]) for d in range(3)]
        d_env = red_s[6]
        for d in range(3):
            d_env = d_env + unit[d] * red_s[3 + d]
        along = jnp.zeros((NBR, LANES), F32)
        level = jnp.zeros((NBR, LANES), F32)
        for k in range(8):
            g = db_s[pl.ds(k, NBR, stride=8), :]
            ratio = sins[k] * inv_x
            level = level + g * ratio
            along = along + g * ((k + 1) * math.pi * coss[k] - ratio)
        d_env = d_env + envelope * level
        d_x = envelope * envelope * inv_x * along - 4.0 * x * gap * d_env
        d_dist = d_x * (1.0 / CUTOFF)
        radial = d_dist
        for d in range(3):
            radial = radial - d_unit[d] * unit[d] * inv_dist
        factor = jnp.zeros((1, LANES), F32)
        for k in range(8):
            factor = jnp.where(kinds == k, escale[k], factor)
        atom = base + lax.broadcasted_iota(jnp.int32, (1, LANES), 1)
        factor = jnp.where(atom < occupied, factor, 0.0)
        keep = jnp.broadcast_to(atom < occupied, (NBR, LANES))
        for d in range(3):
            g = jnp.where(keep, (d_unit[d] * inv_dist + radial * unit[d]) * factor, 0.0)
            geo_s[d] = g
            own_s[d, pl.ds(b, 1), :] = jnp.sum(g, axis=0, keepdims=True)
        low_s, high_s = db_s.at[pl.ds(0, NBR)], db_s.at[pl.ds(NBR, NBR)]
        low_s[...] = low.astype(F32)
        high_s[...] = high.astype(F32)

        def spread(g, c):
            lefts, rights = [], []
            for i in range(2):
                n = g * 2 + i
                lane_of = lax.broadcasted_iota(jnp.int32, (LANES, LANES), 0).astype(F32)
                hit = lane_of == low_s[pl.ds(n, 1), :]
                rights.append(jnp.where(hit, 1.0, 0.0).astype(BF16))
                tile_of = lax.broadcasted_iota(jnp.int32, (rows16, LANES), 0).astype(F32)
                tile_hit = tile_of == high_s[pl.ds(n, 1), :]
                rows = []
                for d in range(3):
                    a = jnp.where(tile_hit, geo_s[d, pl.ds(n, 1), :], 0.0)
                    rows.extend(halves(a))
                lefts.append(jnp.concatenate(rows, axis=0))
            return c + mm_nt(jnp.concatenate(lefts, axis=1), jnp.concatenate(rights, axis=1))

        acc_s[...] = lax.fori_loop(0, NBR // 2, spread, acc_s[...])
        return carry

    blocks = (occupied + LANES - 1) // LANES
    lax.fori_loop(0, blocks, block, 0)
    for d in range(3):
        a = acc_s[2 * d * rows16 : (2 * d + 1) * rows16, :]
        a = a + acc_s[(2 * d + 1) * rows16 : (2 * d + 2) * rows16, :]
        for t in range(own_tiles):
            own_out[d : d + 1, t * LANES : (t + 1) * LANES] = own_s[d, t : t + 1, :] - a[t : t + 1]
        for f in range(nfaces):
            ghost_out[f][d : d + 1, :] = -a[own_tiles + f : own_tiles + f + 1]


def fold_kernel(own, ghost_index, *refs):
    returned, out = refs[:-1], refs[-1]
    tiles = own.shape[1] // LANES
    index = ghost_index[...]
    low, high = index & (LANES - 1), index >> 7
    total = None
    for f, back in enumerate(returned):
        hit = lax.broadcasted_iota(jnp.int32, (LANES, LANES), 0) == low[f : f + 1]
        right = jnp.where(hit, 1.0, 0.0).astype(BF16)
        tile_hit = lax.broadcasted_iota(jnp.int32, (16, LANES), 0) == high[f : f + 1]
        rows = []
        for d in range(3):
            a = jnp.where(tile_hit, back[d : d + 1, :], 0.0)
            rows.extend(halves(a))
        part = mm_nt(jnp.concatenate(rows, axis=0), right)
        total = part if total is None else total + part
    for d in range(3):
        a = total[32 * d : 32 * d + 16] + total[32 * d + 16 : 32 * d + 32]
        for t in range(tiles):
            lane = slice(t * LANES, (t + 1) * LANES)
            out[d : d + 1, lane] = own[d : d + 1, lane] + a[t : t + 1]


VM = functools.partial(pl.BlockSpec, memory_space=pltpu.VMEM)
SM = functools.partial(pl.BlockSpec, memory_space=pltpu.SMEM)


def shards(
    positions,
    species,
    live_bins,
    edge_nbr,
    ghost_index,
    zeta_table,
    energy_scale,
    center_embed,
    nbr_embed,
    radial_weight,
    latent_weight,
    env_weight,
    mix_weight,
    out_weight,
):
    atoms = species.shape[0]
    chan = latent_weight.shape[0]
    ghosts = ghost_index.shape[1]
    nfaces = len(FACES)
    kinds = species.reshape(1, atoms)
    shape = jax.ShapeDtypeStruct

    prep = pl.pallas_call(
        prep_kernel,
        out_shape=[shape((1, atoms), F32)] + [shape((4, ghosts), F32)] * nfaces,
        in_specs=[SM(), VM(), VM(), VM()],
        out_specs=[VM()] * (1 + nfaces),
        name="prep",
    )(zeta_table, positions, kinds, ghost_index)
    zeta, faces = prep[0], prep[1:]
    arrived = [from_behind(face, "dom", o) for face, (o, _, _) in zip(faces, FACES)]

    heights = [(chan, 64), (chan, 3 * chan), (2 * chan + 16, 3 * chan), (chan, 3 * chan)]
    heights += [(2 * chan, 3 * chan), (chan, 3 * chan), (chan, 3 * chan), (16, 3 * chan)]
    weights = pl.pallas_call(
        weights_kernel,
        out_shape=[shape(h, BF16) for h in heights],
        in_specs=[VM()] * 7,
        out_specs=[VM()] * len(heights),
        name="weights",
    )(
        center_embed,
        nbr_embed.reshape(chan, 1),
        radial_weight,
        latent_weight,
        env_weight,
        mix_weight,
        out_weight.reshape(1, chan),
    )
    out_col = jnp.broadcast_to(out_weight.reshape(chan, 1), (chan, LANES))
    nbr_rows = edge_nbr.reshape(atoms, NBR).T

    rows16 = 16
    big = pltpu.VMEM((NBR, chan, LANES), F32)
    result = pl.pallas_call(
        functools.partial(edge_kernel, per=4, nfaces=nfaces),
        out_shape=[shape((3, atoms), F32)] + [shape((3, ghosts), F32)] * nfaces,
        in_specs=[SM(), SM()] + [VM()] * (4 + nfaces + len(weights) + 1),
        out_specs=[VM()] * (1 + nfaces),
        scratch_shapes=[
            pltpu.VMEM((NBR * 16, LANES), F32),
            pltpu.VMEM((6, NBR, LANES), F32),
            pltpu.VMEM((7, NBR, LANES), F32),
            pltpu.VMEM((NBR * 8, LANES), F32),
            big,
            big,
            big,
            big,
            big,
            pltpu.VMEM((3, chan, LANES), F32),
            pltpu.VMEM((3, chan, LANES), F32),
            pltpu.VMEM((6 * rows16, LANES), F32),
            pltpu.VMEM((3, max(8, atoms // LANES), LANES), F32),
        ],
        compiler_params=pltpu.CompilerParams(vmem_limit_bytes=48 * 1024 * 1024),
        name="edges",
    )(live_bins, energy_scale, positions, zeta, kinds, nbr_rows, *arrived, *weights, out_col)
    own, parts = result[0], result[1:]
    returned = [from_behind(part, "dom", -o) for part, (o, _, _) in zip(parts, FACES)]
    return pl.pallas_call(
        fold_kernel,
        out_shape=shape((3, atoms), F32),
        in_specs=[VM()] * (2 + nfaces),
        out_specs=VM(),
        name="fold",
    )(own, ghost_index, *returned)


def solution(mesh):
    in_specs = (
        P(None, ("rep", "dom")),
        P(("rep", "dom")),
        P(("rep", "dom")),
        P(("rep", "dom")),
        P(None, ("rep", "dom")),
        P(),
        P(),
        P(),
        P(),
        P(),
        P(),
        P(),
        P(),
        P(),
    )
    out_specs = P(None, ("rep", "dom"))
    return jax.shard_map(shards, mesh=mesh, in_specs=in_specs, out_specs=out_specs, check_vma=False)
```

```python
import functools
import math

import jax
import jax.numpy as jnp
from jax import lax
from jax.experimental import pallas as pl
from jax.experimental.pallas import tpu as pltpu
from jax.sharding import PartitionSpec as P

NBR = 32
BIN_ATOMS = 16
LANES = 128

FACES = ((1, 0, -1.0), (-1, 0, 1.0), (2, 1, -1.0), (-2, 1, 1.0), (8, 2, -1.0), (-8, 2, 1.0))
CUTOFF = 6.0
SOFTEN = 0.5
BOX_SHIFT = 3.0
F32 = jnp.float32
BF16 = jnp.bfloat16

SIN_TERMS = [(-1.0) ** i / math.factorial(2 * i + 1) for i in range(8)]
COS_TERMS = [(-1.0) ** i / math.factorial(2 * i) for i in range(8)]


def swap(block, size, step, flip):
    def partner(i):
        return (i + step if (i // step) % 2 == flip else i - step) % size

    return lax.ppermute(block, "dom", [(i, partner(i)) for i in range(size)])


def poly(terms, square):
    total = jnp.full_like(square, terms[-1])
    for term in terms[-2::-1]:
        total = total * square + term
    return total


def halves(x):
    top = x.astype(BF16)
    return top, (x - top.astype(F32)).astype(BF16)


def wide(x):
    top, rest = halves(x)
    return jnp.concatenate([top, top, rest], axis=1)


def stacked(parts):
    cols = []
    for x in parts:
        top, rest = halves(x)
        cols.append(jnp.concatenate([top, rest, top], axis=0))
    return jnp.concatenate(cols, axis=1)


def mm(left, right):
    return jnp.dot(left, right, preferred_element_type=F32)


def mm_nt(left, right):
    return lax.dot_general(left, right, (((1,), (1,)), ((), ())), preferred_element_type=F32)


def split_cols(x):
    return [x[:, i * LANES : (i + 1) * LANES] for i in range(x.shape[1] // LANES)]


def lookup(row, index):
    return jnp.take_along_axis(
        jnp.broadcast_to(row, index.shape), index, axis=1, mode="promise_in_bounds"
    )


def parity(step):
    return (lax.axis_index("dom") // step) % 2


def prep_kernel(zeta_table, live, pos, species, ghost_index, own8, *sends, steps):
    kinds = species[...]
    zeta = jnp.zeros(kinds.shape, F32)
    for k in range(zeta_table.shape[0]):
        zeta = jnp.where(kinds == k, zeta_table[k], zeta)
    width = kinds.shape[1]
    tiles = width // LANES
    own8[0:3, :] = pos[...]
    own8[3:4, :] = zeta
    own8[4:5, :] = kinds.astype(F32)
    own8[5:6, :] = jnp.full(kinds.shape, live[0].astype(F32))
    own8[6:8, :] = jnp.zeros((2, width), F32)
    index = ghost_index[...]
    index = jnp.concatenate([index, index[:2]], axis=0)
    low, high = index & (LANES - 1), index >> 7
    got = []
    for d in range(4):
        value = jnp.zeros(index.shape, F32)
        for t in range(tiles):
            row = own8[d : d + 1, t * LANES : (t + 1) * LANES]
            value = jnp.where(high == t, lookup(row, low), value)
        got.append(value)
    for a, step in enumerate(steps):
        par = parity(step)
        for flip in range(2):
            ahead = par == flip
            for d in range(4):
                first, second = got[d][2 * a : 2 * a + 1], got[d][2 * a + 1 : 2 * a + 2]
                if d == a:
                    first, second = first - BOX_SHIFT, second + BOX_SHIFT
                part = jnp.where(ahead, first, second)
                if a == 0 and flip == 0:
                    own8[6:7, d * LANES : (d + 1) * LANES] = part
                else:
                    sends[2 * a + flip - 1][d : d + 1, :] = part


def edge_kernel(
    live,
    escale,
    own8,
    mate8,
    nbr_even,
    nbr_odd,
    mate_nbr,
    *refs,
    steps,
):
    nfaces = 2 * len(steps)
    ghosts = refs[: nfaces - 1]
    center_t, nbr_row, radial_t, latent, env, mix, out_row = refs[nfaces - 1 : nfaces + 6]
    own_out, mate_out = refs[nfaces + 6 : nfaces + 8]
    ghost_out = refs[nfaces + 8 : 2 * nfaces + 7]
    (
        table,
        nbr,
        basis_s,
        geo_s,
        red_s,
        outf_s,
        db_s,
        acc_s,
        df1_s,
        df2_s,
        y_s,
        pa_s,
        fa_s,
    ) = refs[2 * nfaces + 7 :]
    chan = latent.shape[0]
    kinds_total = radial_t.shape[0]
    atoms = own8.shape[1]
    own_tiles = atoms // LANES
    tiles = own_tiles + nfaces
    norm = NBR ** (-0.5)
    group = LANES // BIN_ATOMS
    half_lanes = atoms // 2
    half_blocks = half_lanes // LANES

    for t in range(own_tiles):
        lane = slice(t * LANES, (t + 1) * LANES)
        table[0, t] = own8[:, lane]
        table[1, t] = mate8[:, lane]
    for a, step in enumerate(steps):
        par = parity(step)
        for flip in range(2):
            tile = own_tiles + 2 * a + jnp.where(par == flip, 1, 0)
            for d in range(4):
                if a == 0 and flip == 0:
                    row = mate8[6:7, d * LANES : (d + 1) * LANES]
                else:
                    row = ghosts[2 * a + flip - 1][d : d + 1, :]
                table[0, tile, d : d + 1, :] = row
    for k in range(half_blocks):
        lane = slice(k * LANES, (k + 1) * LANES)
        nbr[k] = nbr_even[:, lane]
        nbr[half_blocks + k] = nbr_odd[:, lane]
        nbr[2 * half_blocks + k] = mate_nbr[:, lane]
    acc_s[...] = jnp.zeros(acc_s.shape, F32)

    nb = radial_t.shape[0]
    first = jnp.concatenate(
        [radial_t[...], nbr_row[...], jnp.zeros((LANES - nb - 1, chan), F32)], axis=0
    ).T
    centers = jnp.concatenate([center_t[...], jnp.zeros((LANES - kinds_total, chan), F32)], axis=0).T
    top, rest = halves(0.5 * centers[:, :8])
    w1 = jnp.concatenate([wide(0.5 * first[:, :16]), top, rest], axis=1)
    w2 = wide(0.5 * latent[...])
    mix_a = mix[:, :chan]
    mix_b = mix[:, chan:]
    row = out_row[...]
    w3 = wide(jnp.concatenate([env[...], 0.5 * mix_a, row, jnp.zeros((15, chan), F32)], axis=0))
    w4 = wide(0.5 * mix_b)
    out_col = jnp.broadcast_to(row, (LANES, chan)).T
    otop, orest = halves(out_col)
    lane16 = lax.broadcasted_iota(jnp.int32, (chan, 16), 1)
    extra = jnp.where(lane16 == 0, out_col[:, :16], 0.0).astype(BF16)
    extra = extra + jnp.where(lane16 == 1, orest[:, :16].astype(F32), 0.0).astype(BF16)
    w5 = wide(jnp.concatenate([mix_b.T * (0.5 * row), mix_a.T * (0.5 * row)], axis=0))
    w5 = jnp.concatenate([w5, jnp.concatenate([jnp.zeros((chan, 16), BF16), extra], axis=0)], axis=1)
    w6 = wide(env[...].T)
    w7 = wide(0.5 * latent[...].T)
    w8 = wide(jnp.concatenate([0.5 * radial_t[...], jnp.zeros((16 - nb, chan), F32)], axis=0))
    sub16 = lax.broadcasted_iota(jnp.int32, (16, LANES), 0)
    ones = jnp.where(sub16 < 2, 1.0, 0.0).astype(BF16)

    mine = live[0]
    theirs = jnp.max(mate8[5:6, :]).astype(jnp.int32)

    def counts(bins):
        even = ((bins + 1) // 2 + group - 1) // group
        odd = (bins // 2 + group - 1) // group
        return even, odd

    my_even, my_odd = counts(mine)
    their_even, their_odd = counts(theirs)
    excess = my_even + my_odd - their_even - their_odd
    give = jnp.minimum(jnp.maximum(excess, 0) // 2, my_even)
    take = jnp.minimum(jnp.maximum(-excess, 0) // 2, their_even)
    keep_even = my_even - give

    def slope2(u, f):
        return u + f * (2.0 - u)

    def block(i, carry):
        is_mate = i >= keep_even + my_odd
        is_odd = jnp.logical_and(i >= keep_even, jnp.logical_not(is_mate))
        which = jnp.where(is_mate, 1, 0)
        odd = jnp.where(is_odd, 1, 0)
        kb = jnp.where(
            is_mate, their_even - take + i - keep_even - my_odd, jnp.where(is_odd, i - keep_even, i)
        )
        slot = kb + half_blocks * odd + 2 * half_blocks * which
        bins = jnp.where(is_mate, theirs, mine)
        index = nbr[slot]
        low, high = index & (LANES - 1), index >> 7

        lane = lax.broadcasted_iota(jnp.int32, (8, LANES), 1)
        local = 2 * (lane // BIN_ATOMS) + odd
        pick = (local % group) * BIN_ATOMS + lane % BIN_ATOMS
        here = jnp.where(
            lane < LANES // 2,
            jnp.take_along_axis(table[which, 2 * kb], pick, axis=1, mode="promise_in_bounds"),
            jnp.take_along_axis(table[which, 2 * kb + 1], pick, axis=1, mode="promise_in_bounds"),
        )
        kinds = here[4:5]
        bin_of = 2 * group * kb + local[0:1]
        occupied = bin_of < bins

        got = []
        for d in range(4):
            value = jnp.zeros((NBR, LANES), F32)
            for t in range(tiles):
                value = jnp.where(high == t, lookup(table[which, t, d : d + 1, :], low), value)
            got.append(value)
        disp = [got[d] - here[d : d + 1] for d in range(3)]
        square = disp[0] * disp[0] + disp[1] * disp[1] + disp[2] * disp[2]
        dist = jnp.sqrt(square + SOFTEN * SOFTEN)
        inv_dist = 1.0 / dist
        unit = [disp[d] * inv_dist for d in range(3)]
        x = jnp.minimum(dist * (1.0 / CUTOFF), 1.0)
        inv_x = 1.0 / x
        gap = 1.0 - x * x
        envelope = gap * gap
        t = math.pi * (x - 0.5)
        tt = t * t
        s1 = poly(COS_TERMS, tt)
        c1 = -(t * poly(SIN_TERMS, tt))
        sins, coss = [s1], [c1]
        for k in range(2, nb + 1):
            p, q = k // 2 - 1, k - k // 2 - 1
            sins.append(sins[p] * coss[q] + coss[p] * sins[q])
            coss.append(coss[p] * coss[q] - sins[p] * sins[q])
        scale = envelope * inv_x
        for k in range(nb):
            basis_s[pl.ds(k, NBR, stride=16), :] = sins[k] * scale
        basis_s[pl.ds(nb, NBR, stride=16), :] = got[3]
        for k in range(nb + 1, 16):
            basis_s[pl.ds(k, NBR, stride=16), :] = jnp.zeros((NBR, LANES), F32)
        for d in range(3):
            geo_s[d] = unit[d]
            geo_s[3 + d] = unit[d] * envelope

        kind8 = lax.broadcasted_iota(jnp.int32, (8, LANES), 0).astype(F32) == kinds
        onehot = jnp.where(kind8, 1.0, 0.0)
        onehot = jnp.concatenate([onehot, onehot], axis=0).astype(BF16)

        def fold8(v):
            return sum(v[8 * j : 8 * j + 8] for j in range(1, chan // 8)) + v[:8]

        cols = []
        for n in range(NBR):
            top, rest = halves(basis_s[n * 16 : n * 16 + 16, :])
            cols.append(jnp.concatenate([top, rest, top, onehot], axis=0))
        f1 = []
        for n, z in enumerate(split_cols(mm(w1, jnp.concatenate(cols, axis=1)))):
            u = 1.0 + jnp.tanh(z)
            f = z * u
            df1_s[n] = slope2(u, f)
            f1.append(f)
        f2 = []
        for n, z in enumerate(split_cols(mm(w2, stacked(f1)))):
            u = 1.0 + jnp.tanh(z)
            f = z * u
            df2_s[n] = slope2(u, f)
            f2.append(f)
        env_v = [None] * 3
        for n, v in enumerate(split_cols(mm(w3, stacked(f2)))):
            y = v[:chan]
            y_s[n] = y
            pa_s[n] = v[chan : 2 * chan]
            outf_s[n : n + 1, :] = v[2 * chan : 2 * chan + 1]
            for d in range(3):
                term = y * geo_s[3 + d, n : n + 1, :]
                env_v[d] = term if n == 0 else env_v[d] + term
        env_v = [v * norm for v in env_v]

        inv = []
        for n in range(NBR):
            v = env_v[0] * geo_s[0, n : n + 1, :]
            for d in range(1, 3):
                v = v + env_v[d] * geo_s[d, n : n + 1, :]
            inv.append(v)
        slopes = []
        for n, z in enumerate(split_cols(mm(w4, stacked(inv)))):
            z = z + pa_s[n]
            u = 1.0 + jnp.tanh(z)
            f = z * u
            red_s[6, 8 * n : 8 * n + 8, :] = fold8(f * out_col)
            slopes.append(slope2(u, f))
        cols = []
        for v in slopes:
            top, rest = halves(v)
            cols.append(jnp.concatenate([top, rest, top, ones], axis=0))
        denv = [None] * 3
        for n, v in enumerate(split_cols(mm(w5, jnp.concatenate(cols, axis=1)))):
            dinv = v[:chan]
            fa_s[n] = v[chan:]
            for d in range(3):
                term = dinv * geo_s[3 + d, n : n + 1, :]
                denv[d] = term if n == 0 else denv[d] + term
                red_s[d, 8 * n : 8 * n + 8, :] = fold8(env_v[d] * dinv)
        denv = [v * norm for v in denv]

        dy = []
        for n in range(NBR):
            y = y_s[n]
            v = None
            for d in range(3):
                term = denv[d] * geo_s[d, n : n + 1, :]
                v = term if v is None else v + term
                red_s[3 + d, 8 * n : 8 * n + 8, :] = fold8(denv[d] * y)
            dy.append(v)
        da2 = []
        for n, v in enumerate(split_cols(mm(w6, stacked(dy)))):
            da2.append((v + fa_s[n]) * df2_s[n])
        da1 = []
        for n, v in enumerate(split_cols(mm(w7, stacked(da2)))):
            da1.append(v * df1_s[n])
        for n, v in enumerate(split_cols(mm(w8, stacked(da1)))):
            db_s[8 * n : 8 * n + 8, :] = v[:8]

        def collect(ref, q):
            total = ref[q, pl.ds(0, NBR, stride=8), :]
            for k in range(1, 8):
                total = total + ref[q, pl.ds(k, NBR, stride=8), :]
            return total

        pulls = [collect(red_s, 3 + d) for d in range(3)]
        d_unit = [envelope * (collect(red_s, d) + pulls[d]) for d in range(3)]
        d_env = collect(red_s, 6) + outf_s[...]
        for d in range(3):
            d_env = d_env + unit[d] * pulls[d]
        along = jnp.zeros((NBR, LANES), F32)
        level = jnp.zeros((NBR, LANES), F32)
        for k in range(nb):
            g = db_s[pl.ds(k, NBR, stride=8), :]
            ratio = sins[k] * inv_x
            level = level + g * ratio
            along = along + g * ((k + 1) * math.pi * coss[k] - ratio)
        d_env = d_env + envelope * level
        d_x = envelope * envelope * inv_x * along - 4.0 * x * gap * d_env
        radial = d_x * (1.0 / CUTOFF)
        for d in range(3):
            radial = radial - d_unit[d] * unit[d] * inv_dist
        factor = jnp.zeros((1, LANES), F32)
        for k in range(kinds_total):
            factor = jnp.where(kinds == k, escale[k], factor)
        keep = jnp.broadcast_to(occupied, (NBR, LANES))
        force = []
        for d in range(3):
            g = jnp.where(keep, (d_unit[d] * inv_dist + radial * unit[d]) * factor, 0.0)
            geo_s[d] = g
            force.append(jnp.sum(g, axis=0, keepdims=True))

        atom = bin_of * BIN_ATOMS + lane[0:1] % BIN_ATOMS
        lane_of = lax.broadcasted_iota(jnp.int32, (LANES, LANES), 0)
        lefts, rights = [], []
        for n in range(NBR + 1):
            if n < NBR:
                lows, highs = low[n : n + 1], high[n : n + 1]
                values = [geo_s[d, n : n + 1, :] for d in range(3)]
            else:
                lows, highs = atom & (LANES - 1), atom >> 7
                values = [-v for v in force]
            rights.append(jnp.where(lane_of == lows, 1.0, 0.0).astype(BF16))
            hit = sub16 == highs
            rows = []
            for d in range(3):
                rows.extend(halves(jnp.where(hit, values[d], 0.0)))
            lefts.append(jnp.concatenate(rows, axis=0))
        acc_s[which] += mm_nt(jnp.concatenate(lefts, axis=1), jnp.concatenate(rights, axis=1))
        return carry

    lax.fori_loop(0, keep_even + my_odd + take, block, 0)

    mate_out[...] = jnp.zeros(mate_out.shape, F32)
    for d in range(3):
        for which in range(2):
            a = acc_s[which, 32 * d : 32 * d + 16, :] + acc_s[which, 32 * d + 16 : 32 * d + 32, :]
            a = -a
            dest = mate_out if which else own_out
            for t in range(own_tiles):
                dest[d : d + 1, t * LANES : (t + 1) * LANES] = a[t : t + 1]
            if which == 0:
                outf_s[16 * 0 : 16, :] = a
                for c, step in enumerate(steps):
                    par = parity(step)
                    for flip in range(2):
                        row = outf_s[pl.ds(own_tiles + 2 * c + jnp.where(par == flip, 1, 0), 1), :]
                        if c == 0 and flip == 0:
                            back0 = row
                        else:
                            ghost_out[2 * c + flip - 1][d : d + 1, :] = row
        mate_out[6:7, d * LANES : (d + 1) * LANES] = back0


def fold_kernel(own, back8, ghost_index, *refs, steps):
    returned, out = refs[:-1], refs[-1]
    tiles = own.shape[1] // LANES
    total = None
    for a, step in enumerate(steps):
        par = parity(step)
        for flip in range(2):
            index = ghost_index[pl.ds(2 * a + jnp.where(par == flip, 0, 1), 1), :]
            low, high = index & (LANES - 1), index >> 7
            hit = lax.broadcasted_iota(jnp.int32, (LANES, LANES), 0) == low
            right = jnp.where(hit, 1.0, 0.0).astype(BF16)
            tile_hit = lax.broadcasted_iota(jnp.int32, (16, LANES), 0) == high
            rows = []
            for d in range(3):
                if a == 0 and flip == 0:
                    value = back8[6:7, d * LANES : (d + 1) * LANES]
                else:
                    value = returned[2 * a + flip - 1][d : d + 1, :]
                rows.extend(halves(jnp.where(tile_hit, value, 0.0)))
            part = mm_nt(jnp.concatenate(rows, axis=0), right)
            total = part if total is None else total + part
    for d in range(3):
        a = total[32 * d : 32 * d + 16] + total[32 * d + 16 : 32 * d + 32]
        for t in range(tiles):
            lane = slice(t * LANES, (t + 1) * LANES)
            out[d : d + 1, lane] = own[d : d + 1, lane] + back8[d : d + 1, lane] + a[t : t + 1]


VM = functools.partial(pl.BlockSpec, memory_space=pltpu.VMEM)
SM = functools.partial(pl.BlockSpec, memory_space=pltpu.SMEM)


def shards(
    positions,
    species,
    live_bins,
    edge_nbr,
    ghost_index,
    zeta_table,
    energy_scale,
    center_embed,
    nbr_embed,
    radial_weight,
    latent_weight,
    env_weight,
    mix_weight,
    out_weight,
):
    size = lax.axis_size("dom")
    atoms = species.shape[0]
    bins = atoms // BIN_ATOMS
    chan = latent_weight.shape[0]
    ghosts = ghost_index.shape[1]
    steps = tuple(o for o, _, s in FACES if s < 0)
    nfaces = len(FACES)
    shape = jax.ShapeDtypeStruct

    rows = edge_nbr.reshape(bins // 2, 2, BIN_ATOMS, NBR)
    nbr_even, nbr_odd = [rows[:, p].transpose(2, 0, 1).reshape(NBR, atoms // 2) for p in range(2)]

    def exchange(parts, first):
        got = [swap(first, size, steps[0], 0)]
        for a, step in enumerate(steps):
            if 2 * step == size:
                both = jnp.concatenate(parts[2 * a - 1 : 2 * a + 1], axis=0)
                both = swap(both, size, step, 0)
                got.extend(jnp.split(both, 2, axis=0))
                continue
            for flip in range(2):
                if a or flip:
                    got.append(swap(parts[2 * a + flip - 1], size, step, flip))
        return got

    mate_nbr = swap(nbr_even, size, steps[0], 0)
    own8, *sends = pl.pallas_call(
        functools.partial(prep_kernel, steps=steps),
        out_shape=[shape((8, atoms), F32)] + [shape((4, ghosts), F32)] * (nfaces - 1),
        in_specs=[SM(), SM(), VM(), VM(), VM()],
        out_specs=[VM()] * nfaces,
        name="prep",
    )(zeta_table, live_bins, positions, species.reshape(1, atoms), ghost_index)
    mate8, *arrived = exchange(sends, own8)

    big = pltpu.VMEM((NBR, chan, LANES), F32)
    own, mate_part, *parts = pl.pallas_call(
        functools.partial(edge_kernel, steps=steps),
        out_shape=[shape((3, atoms), F32), shape((8, atoms), F32)]
        + [shape((3, ghosts), F32)] * (nfaces - 1),
        in_specs=[SM(), SM()] + [VM()] * (5 + nfaces - 1 + 7),
        out_specs=[VM()] * (1 + nfaces),
        scratch_shapes=[
            pltpu.VMEM((2, 16, 8, LANES), F32),
            pltpu.VMEM((3 * (atoms // 2 // LANES), NBR, LANES), jnp.int32),
            pltpu.VMEM((NBR * 16, LANES), F32),
            pltpu.VMEM((6, NBR, LANES), F32),
            pltpu.VMEM((7, NBR * 8, LANES), F32),
            pltpu.VMEM((NBR, LANES), F32),
            pltpu.VMEM((NBR * 8, LANES), F32),
            pltpu.VMEM((2, 96, LANES), F32),
            big,
            big,
            big,
            big,
            big,
        ],
        compiler_params=pltpu.CompilerParams(vmem_limit_bytes=48 * 1024 * 1024),
        name="edges",
    )(
        live_bins,
        energy_scale,
        own8,
        mate8,
        nbr_even,
        nbr_odd,
        mate_nbr,
        *arrived,
        center_embed.T,
        nbr_embed.reshape(1, chan),
        radial_weight.T,
        latent_weight,
        env_weight,
        mix_weight,
        out_weight.reshape(1, chan),
    )
    back8, *returned = exchange(parts, mate_part)
    return pl.pallas_call(
        functools.partial(fold_kernel, steps=steps),
        out_shape=shape((3, atoms), F32),
        in_specs=[VM()] * (3 + nfaces - 1),
        out_specs=VM(),
        name="fold",
    )(own, back8, ghost_index, *returned)


def solution(mesh):
    in_specs = (
        P(None, ("rep", "dom")),
        P(("rep", "dom")),
        P(("rep", "dom")),
        P(("rep", "dom")),
        P(None, ("rep", "dom")),
        P(),
        P(),
        P(),
        P(),
        P(),
        P(),
        P(),
        P(),
        P(),
    )
    out_specs = P(None, ("rep", "dom"))
    return jax.shard_map(shards, mesh=mesh, in_specs=in_specs, out_specs=out_specs, check_vma=False)
```

```python
import functools
import math

import jax
import jax.numpy as jnp
from jax import lax
from jax.experimental import pallas as pl
from jax.experimental.pallas import tpu as pltpu
from jax.sharding import PartitionSpec as P

NBR = 32
BIN_ATOMS = 16
LANES = 128

FACES = ((1, 0, -1.0), (-1, 0, 1.0), (2, 1, -1.0), (-2, 1, 1.0), (8, 2, -1.0), (-8, 2, 1.0))
CUTOFF = 6.0
SOFTEN = 0.5
BOX_SHIFT = 3.0
F32 = jnp.float32
BF16 = jnp.bfloat16

SIN_TERMS = [(-1.0) ** i / math.factorial(2 * i + 1) for i in range(8)]
COS_TERMS = [(-1.0) ** i / math.factorial(2 * i) for i in range(8)]


def swap(block, size, step, flip):
    def partner(i):
        return (i + step if (i // step) % 2 == flip else i - step) % size

    return lax.ppermute(block, "dom", [(i, partner(i)) for i in range(size)])


def poly(terms, square):
    total = jnp.full_like(square, terms[-1])
    for term in terms[-2::-1]:
        total = total * square + term
    return total


def halves(x):
    top = x.astype(BF16)
    return top, (x - top.astype(F32)).astype(BF16)


def wide(x):
    top, rest = halves(x)
    return jnp.concatenate([top, top, rest], axis=1)


def stack(x, *more):
    top, rest = halves(x)
    return jnp.concatenate([top, rest, top, *more], axis=0)


def stacked(parts, *more):
    return jnp.concatenate([stack(x, *more) for x in parts], axis=1)


def mm(left, right):
    return jnp.dot(left, right, preferred_element_type=F32)


def mm_nt(left, right):
    return lax.dot_general(left, right, (((1,), (1,)), ((), ())), preferred_element_type=F32)


def split_cols(x):
    return [x[:, i * LANES : (i + 1) * LANES] for i in range(x.shape[1] // LANES)]


def lookup(row, index):
    return jnp.take_along_axis(
        jnp.broadcast_to(row, index.shape), index, axis=1, mode="promise_in_bounds"
    )


def parity(step):
    return (lax.axis_index("dom") // step) % 2


def prep_kernel(zeta_table, live, pos, species, ghost_index, own8, *sends, steps):
    kinds = species[...]
    zeta = jnp.zeros(kinds.shape, F32)
    for k in range(zeta_table.shape[0]):
        zeta = jnp.where(kinds == k, zeta_table[k], zeta)
    width = kinds.shape[1]
    tiles = width // LANES
    own8[0:3, :] = pos[...]
    own8[3:4, :] = zeta
    own8[4:5, :] = kinds.astype(F32)
    own8[5:6, :] = jnp.full(kinds.shape, live[0].astype(F32))
    own8[6:8, :] = jnp.zeros((2, width), F32)
    index = ghost_index[...]
    index = jnp.concatenate([index, index[:2]], axis=0)
    low, high = index & (LANES - 1), index >> 7
    got = []
    for d in range(4):
        value = jnp.zeros(index.shape, F32)
        for t in range(tiles):
            row = own8[d : d + 1, t * LANES : (t + 1) * LANES]
            value = jnp.where(high == t, lookup(row, low), value)
        got.append(value)
    for a, step in enumerate(steps):
        par = parity(step)
        for flip in range(2):
            ahead = par == flip
            for d in range(4):
                first, second = got[d][2 * a : 2 * a + 1], got[d][2 * a + 1 : 2 * a + 2]
                if d == a:
                    first, second = first - BOX_SHIFT, second + BOX_SHIFT
                part = jnp.where(ahead, first, second)
                if a == 0 and flip == 0:
                    own8[6:7, d * LANES : (d + 1) * LANES] = part
                else:
                    sends[2 * a + flip - 1][d : d + 1, :] = part


def edge_kernel(
    live,
    escale,
    own8,
    mate8,
    nbr_even,
    nbr_odd,
    mate_nbr,
    *refs,
    steps,
):
    nfaces = 2 * len(steps)
    ghosts = refs[: nfaces - 1]
    center_t, nbr_row, radial_t, latent, env, mix, out_row = refs[nfaces - 1 : nfaces + 6]
    own_out, mate_out = refs[nfaces + 6 : nfaces + 8]
    ghost_out = refs[nfaces + 8 : 2 * nfaces + 7]
    (
        table,
        nbr,
        basis_s,
        geo_s,
        red_s,
        outf_s,
        db_s,
        acc_s,
        df1_s,
        df2_s,
        f2_s,
        pa_s,
        env_s,
        denv_s,
        out_s,
    ) = refs[2 * nfaces + 7 :]
    chan = latent.shape[0]
    kinds_total = radial_t.shape[0]
    atoms = own8.shape[1]
    own_tiles = atoms // LANES
    tiles = own_tiles + nfaces
    norm = NBR ** (-0.5)
    group = LANES // BIN_ATOMS
    half_lanes = atoms // 2
    half_blocks = half_lanes // LANES

    for t in range(own_tiles):
        lane = slice(t * LANES, (t + 1) * LANES)
        table[0, t] = own8[:, lane]
        table[1, t] = mate8[:, lane]
    for a, step in enumerate(steps):
        par = parity(step)
        for flip in range(2):
            tile = own_tiles + 2 * a + jnp.where(par == flip, 1, 0)
            for d in range(4):
                if a == 0 and flip == 0:
                    row = mate8[6:7, d * LANES : (d + 1) * LANES]
                else:
                    row = ghosts[2 * a + flip - 1][d : d + 1, :]
                table[0, tile, d : d + 1, :] = row
    for k in range(half_blocks):
        lane = slice(k * LANES, (k + 1) * LANES)
        nbr[k] = nbr_even[:, lane]
        nbr[half_blocks + k] = nbr_odd[:, lane]
        nbr[2 * half_blocks + k] = mate_nbr[:, lane]
    acc_s[...] = jnp.zeros(acc_s.shape, F32)

    nb = radial_t.shape[0]
    first = jnp.concatenate(
        [radial_t[...], nbr_row[...], jnp.zeros((LANES - nb - 1, chan), F32)], axis=0
    ).T
    centers = jnp.concatenate([center_t[...], jnp.zeros((LANES - kinds_total, chan), F32)], axis=0).T
    top, rest = halves(0.5 * centers[:, :8])
    w1 = jnp.concatenate([wide(0.5 * first[:, :16]), top, rest], axis=1)
    w2 = wide(0.5 * latent[...])
    mix_a = mix[:, :chan]
    mix_b = mix[:, chan:]
    row = out_row[...]
    w3 = wide(jnp.concatenate([0.5 * mix_a, row, jnp.zeros((15, chan), F32)], axis=0))
    both = (0.5 * norm) * mm(wide(mix_b), stack(env[...]))
    w4 = wide(both)
    out_col = jnp.broadcast_to(row, (LANES, chan)).T
    out_s[...] = out_col
    _, orest = halves(out_col)
    lane16 = lax.broadcasted_iota(jnp.int32, (chan, 16), 1)
    extra = jnp.where(lane16 == 0, out_col[:, :16], 0.0).astype(BF16)
    extra = extra + jnp.where(lane16 == 1, orest[:, :16].astype(F32), 0.0).astype(BF16)
    w5 = jnp.concatenate([wide(mix_a.T * (0.5 * row)), extra], axis=1)
    w6 = wide(both.T * row)
    w7 = wide(0.5 * latent[...].T)
    w8 = wide(jnp.concatenate([0.5 * radial_t[...], jnp.zeros((16 - nb, chan), F32)], axis=0))
    sub16 = lax.broadcasted_iota(jnp.int32, (16, LANES), 0)
    ones = jnp.where(sub16 < 2, 1.0, 0.0).astype(BF16)

    mine = live[0]
    theirs = jnp.max(mate8[5:6, :]).astype(jnp.int32)

    def counts(bins):
        even = ((bins + 1) // 2 + group - 1) // group
        odd = (bins // 2 + group - 1) // group
        return even, odd

    my_even, my_odd = counts(mine)
    their_even, their_odd = counts(theirs)
    excess = my_even + my_odd - their_even - their_odd
    give = jnp.minimum(jnp.maximum(excess, 0) // 2, my_even)
    take = jnp.minimum(jnp.maximum(-excess, 0) // 2, their_even)
    keep_even = my_even - give

    def slope2(u, f):
        return u + f * (2.0 - u)

    def block(i, carry):
        is_mate = i >= keep_even + my_odd
        is_odd = jnp.logical_and(i >= keep_even, jnp.logical_not(is_mate))
        which = jnp.where(is_mate, 1, 0)
        odd = jnp.where(is_odd, 1, 0)
        kb = jnp.where(
            is_mate, their_even - take + i - keep_even - my_odd, jnp.where(is_odd, i - keep_even, i)
        )
        slot = kb + half_blocks * odd + 2 * half_blocks * which
        bins = jnp.where(is_mate, theirs, mine)
        index = nbr[slot]
        low, high = index & (LANES - 1), index >> 7

        lane = lax.broadcasted_iota(jnp.int32, (8, LANES), 1)
        local = 2 * (lane // BIN_ATOMS) + odd
        pick = (local % group) * BIN_ATOMS + lane % BIN_ATOMS
        here = jnp.where(
            lane < LANES // 2,
            jnp.take_along_axis(table[which, 2 * kb], pick, axis=1, mode="promise_in_bounds"),
            jnp.take_along_axis(table[which, 2 * kb + 1], pick, axis=1, mode="promise_in_bounds"),
        )
        kinds = here[4:5]
        bin_of = 2 * group * kb + local[0:1]
        occupied = bin_of < bins

        got = []
        for d in range(4):
            value = jnp.zeros((NBR, LANES), F32)
            for t in range(tiles):
                value = jnp.where(high == t, lookup(table[which, t, d : d + 1, :], low), value)
            got.append(value)
        disp = [got[d] - here[d : d + 1] for d in range(3)]
        square = disp[0] * disp[0] + disp[1] * disp[1] + disp[2] * disp[2]
        dist = jnp.sqrt(square + SOFTEN * SOFTEN)
        inv_dist = 1.0 / dist
        unit = [disp[d] * inv_dist for d in range(3)]
        x = jnp.minimum(dist * (1.0 / CUTOFF), 1.0)
        inv_x = 1.0 / x
        gap = 1.0 - x * x
        envelope = gap * gap
        t = math.pi * (x - 0.5)
        tt = t * t
        s1 = poly(COS_TERMS, tt)
        c1 = -(t * poly(SIN_TERMS, tt))
        sins, coss = [s1], [c1]
        for k in range(2, nb + 1):
            p, q = k // 2 - 1, k - k // 2 - 1
            sins.append(sins[p] * coss[q] + coss[p] * sins[q])
            coss.append(coss[p] * coss[q] - sins[p] * sins[q])
        scale = envelope * inv_x
        for k in range(nb):
            basis_s[pl.ds(k, NBR, stride=16), :] = sins[k] * scale
        basis_s[pl.ds(nb, NBR, stride=16), :] = got[3]
        for k in range(nb + 1, 16):
            basis_s[pl.ds(k, NBR, stride=16), :] = jnp.zeros((NBR, LANES), F32)
        for d in range(3):
            geo_s[d] = unit[d]
            geo_s[3 + d] = unit[d] * envelope

        kind8 = lax.broadcasted_iota(jnp.int32, (8, LANES), 0).astype(F32) == kinds
        onehot = jnp.where(kind8, 1.0, 0.0)
        onehot = jnp.concatenate([onehot, onehot], axis=0).astype(BF16)

        def fold8(v):
            return sum(v[8 * j : 8 * j + 8] for j in range(1, chan // 8)) + v[:8]

        f1 = []
        parts = [basis_s[n * 16 : n * 16 + 16, :] for n in range(NBR)]
        for n, z in enumerate(split_cols(mm(w1, stacked(parts, onehot)))):
            u = 1.0 + jnp.tanh(z)
            f = z * u
            df1_s[n] = slope2(u, f)
            f1.append(f)
        f2 = []
        env_f = [None] * 3
        for n, z in enumerate(split_cols(mm(w2, stacked(f1)))):
            u = 1.0 + jnp.tanh(z)
            f = z * u
            df2_s[n] = slope2(u, f)
            f2_s[n] = f
            f2.append(f)
            for d in range(3):
                term = f * geo_s[3 + d, n : n + 1, :]
                env_f[d] = term if n == 0 else env_f[d] + term
        for n, v in enumerate(split_cols(mm(w3, stacked(f2)))):
            pa_s[n] = v[:chan]
            outf_s[n : n + 1, :] = v[chan : chan + 1]
        for d, v in enumerate(split_cols(mm(w4, stacked(env_f)))):
            env_s[d] = v
            env_s[3 + d] = v * out_col

        slopes = []
        denv = [None] * 3
        for n in range(NBR):
            z = pa_s[n]
            for d in range(3):
                z = z + env_s[d] * geo_s[d, n : n + 1, :]
            u = 1.0 + jnp.tanh(z)
            f = z * u
            red_s[6, 8 * n : 8 * n + 8, :] = fold8(f * out_s[...])
            v = slope2(u, f)
            slopes.append(v)
            for d in range(3):
                term = v * geo_s[3 + d, n : n + 1, :]
                denv[d] = term if n == 0 else denv[d] + term
                red_s[d, 8 * n : 8 * n + 8, :] = fold8(env_s[3 + d] * v)
        back = split_cols(mm(w5, stacked(slopes, ones)))
        for d, v in enumerate(split_cols(mm(w6, stacked(denv)))):
            denv_s[d] = v

        da2 = []
        for n, v in enumerate(back):
            f = f2_s[n]
            for d in range(3):
                v = v + denv_s[d] * geo_s[d, n : n + 1, :]
                red_s[3 + d, 8 * n : 8 * n + 8, :] = fold8(denv_s[d] * f)
            da2.append(v * df2_s[n])
        da1 = []
        for n, v in enumerate(split_cols(mm(w7, stacked(da2)))):
            da1.append(v * df1_s[n])
        for n, v in enumerate(split_cols(mm(w8, stacked(da1)))):
            db_s[8 * n : 8 * n + 8, :] = v[:8]

        def collect(ref, q):
            total = ref[q, pl.ds(0, NBR, stride=8), :]
            for k in range(1, 8):
                total = total + ref[q, pl.ds(k, NBR, stride=8), :]
            return total

        pulls = [collect(red_s, 3 + d) for d in range(3)]
        d_unit = [envelope * (collect(red_s, d) + pulls[d]) for d in range(3)]
        d_env = collect(red_s, 6) + outf_s[...]
        for d in range(3):
            d_env = d_env + unit[d] * pulls[d]
        along = jnp.zeros((NBR, LANES), F32)
        level = jnp.zeros((NBR, LANES), F32)
        for k in range(nb):
            g = db_s[pl.ds(k, NBR, stride=8), :]
            ratio = sins[k] * inv_x
            level = level + g * ratio
            along = along + g * ((k + 1) * math.pi * coss[k] - ratio)
        d_env = d_env + envelope * level
        d_x = envelope * envelope * inv_x * along - 4.0 * x * gap * d_env
        radial = d_x * (1.0 / CUTOFF)
        for d in range(3):
            radial = radial - d_unit[d] * unit[d] * inv_dist
        factor = jnp.zeros((1, LANES), F32)
        for k in range(kinds_total):
            factor = jnp.where(kinds == k, escale[k], factor)
        keep = jnp.broadcast_to(occupied, (NBR, LANES))
        force = []
        for d in range(3):
            g = jnp.where(keep, (d_unit[d] * inv_dist + radial * unit[d]) * factor, 0.0)
            geo_s[d] = g
            force.append(jnp.sum(g, axis=0, keepdims=True))

        atom = bin_of * BIN_ATOMS + lane[0:1] % BIN_ATOMS
        lane_of = lax.broadcasted_iota(jnp.int32, (LANES, LANES), 0)
        lefts, rights = [], []
        for n in range(NBR + 1):
            if n < NBR:
                lows, highs = low[n : n + 1], high[n : n + 1]
                values = [geo_s[d, n : n + 1, :] for d in range(3)]
            else:
                lows, highs = atom & (LANES - 1), atom >> 7
                values = [-v for v in force]
            rights.append(jnp.where(lane_of == lows, 1.0, 0.0).astype(BF16))
            hit = sub16 == highs
            rows = []
            for d in range(3):
                rows.extend(halves(jnp.where(hit, values[d], 0.0)))
            lefts.append(jnp.concatenate(rows, axis=0))
        acc_s[which] += mm_nt(jnp.concatenate(lefts, axis=1), jnp.concatenate(rights, axis=1))
        return carry

    lax.fori_loop(0, keep_even + my_odd + take, block, 0)

    mate_out[...] = jnp.zeros(mate_out.shape, F32)
    for d in range(3):
        for which in range(2):
            a = acc_s[which, 32 * d : 32 * d + 16, :] + acc_s[which, 32 * d + 16 : 32 * d + 32, :]
            a = -a
            dest = mate_out if which else own_out
            for t in range(own_tiles):
                dest[d : d + 1, t * LANES : (t + 1) * LANES] = a[t : t + 1]
            if which == 0:
                outf_s[16 * 0 : 16, :] = a
                for c, step in enumerate(steps):
                    par = parity(step)
                    for flip in range(2):
                        row = outf_s[pl.ds(own_tiles + 2 * c + jnp.where(par == flip, 1, 0), 1), :]
                        if c == 0 and flip == 0:
                            back0 = row
                        else:
                            ghost_out[2 * c + flip - 1][d : d + 1, :] = row
        mate_out[6:7, d * LANES : (d + 1) * LANES] = back0


def fold_kernel(own, back8, ghost_index, *refs, steps):
    returned, out = refs[:-1], refs[-1]
    tiles = own.shape[1] // LANES
    total = None
    for a, step in enumerate(steps):
        par = parity(step)
        for flip in range(2):
            index = ghost_index[pl.ds(2 * a + jnp.where(par == flip, 0, 1), 1), :]
            low, high = index & (LANES - 1), index >> 7
            hit = lax.broadcasted_iota(jnp.int32, (LANES, LANES), 0) == low
            right = jnp.where(hit, 1.0, 0.0).astype(BF16)
            tile_hit = lax.broadcasted_iota(jnp.int32, (16, LANES), 0) == high
            rows = []
            for d in range(3):
                if a == 0 and flip == 0:
                    value = back8[6:7, d * LANES : (d + 1) * LANES]
                else:
                    value = returned[2 * a + flip - 1][d : d + 1, :]
                rows.extend(halves(jnp.where(tile_hit, value, 0.0)))
            part = mm_nt(jnp.concatenate(rows, axis=0), right)
            total = part if total is None else total + part
    for d in range(3):
        a = total[32 * d : 32 * d + 16] + total[32 * d + 16 : 32 * d + 32]
        for t in range(tiles):
            lane = slice(t * LANES, (t + 1) * LANES)
            out[d : d + 1, lane] = own[d : d + 1, lane] + back8[d : d + 1, lane] + a[t : t + 1]


VM = functools.partial(pl.BlockSpec, memory_space=pltpu.VMEM)
SM = functools.partial(pl.BlockSpec, memory_space=pltpu.SMEM)


def shards(
    positions,
    species,
    live_bins,
    edge_nbr,
    ghost_index,
    zeta_table,
    energy_scale,
    center_embed,
    nbr_embed,
    radial_weight,
    latent_weight,
    env_weight,
    mix_weight,
    out_weight,
):
    size = lax.axis_size("dom")
    atoms = species.shape[0]
    bins = atoms // BIN_ATOMS
    chan = latent_weight.shape[0]
    ghosts = ghost_index.shape[1]
    steps = tuple(o for o, _, s in FACES if s < 0)
    nfaces = len(FACES)
    shape = jax.ShapeDtypeStruct

    rows = edge_nbr.reshape(bins // 2, 2, BIN_ATOMS, NBR)
    nbr_even, nbr_odd = [rows[:, p].transpose(2, 0, 1).reshape(NBR, atoms // 2) for p in range(2)]

    def exchange(parts, first):
        got = [swap(first, size, steps[0], 0)]
        for a, step in enumerate(steps):
            if 2 * step == size:
                both = jnp.concatenate(parts[2 * a - 1 : 2 * a + 1], axis=0)
                both = swap(both, size, step, 0)
                got.extend(jnp.split(both, 2, axis=0))
                continue
            for flip in range(2):
                if a or flip:
                    got.append(swap(parts[2 * a + flip - 1], size, step, flip))
        return got

    mate_nbr = swap(nbr_even, size, steps[0], 0)
    own8, *sends = pl.pallas_call(
        functools.partial(prep_kernel, steps=steps),
        out_shape=[shape((8, atoms), F32)] + [shape((4, ghosts), F32)] * (nfaces - 1),
        in_specs=[SM(), SM(), VM(), VM(), VM()],
        out_specs=[VM()] * nfaces,
        name="prep",
    )(zeta_table, live_bins, positions, species.reshape(1, atoms), ghost_index)
    mate8, *arrived = exchange(sends, own8)

    big = pltpu.VMEM((NBR, chan, LANES), F32)
    own, mate_part, *parts = pl.pallas_call(
        functools.partial(edge_kernel, steps=steps),
        out_shape=[shape((3, atoms), F32), shape((8, atoms), F32)]
        + [shape((3, ghosts), F32)] * (nfaces - 1),
        in_specs=[SM(), SM()] + [VM()] * (5 + nfaces - 1 + 7),
        out_specs=[VM()] * (1 + nfaces),
        scratch_shapes=[
            pltpu.VMEM((2, 16, 8, LANES), F32),
            pltpu.VMEM((3 * (atoms // 2 // LANES), NBR, LANES), jnp.int32),
            pltpu.VMEM((NBR * 16, LANES), F32),
            pltpu.VMEM((6, NBR, LANES), F32),
            pltpu.VMEM((7, NBR * 8, LANES), F32),
            pltpu.VMEM((NBR, LANES), F32),
            pltpu.VMEM((NBR * 8, LANES), F32),
            pltpu.VMEM((2, 96, LANES), F32),
            big,
            big,
            big,
            big,
            pltpu.VMEM((6, chan, LANES), F32),
            pltpu.VMEM((3, chan, LANES), F32),
            pltpu.VMEM((chan, LANES), F32),
        ],
        compiler_params=pltpu.CompilerParams(vmem_limit_bytes=48 * 1024 * 1024),
        name="edges",
    )(
        live_bins,
        energy_scale,
        own8,
        mate8,
        nbr_even,
        nbr_odd,
        mate_nbr,
        *arrived,
        center_embed.T,
        nbr_embed.reshape(1, chan),
        radial_weight.T,
        latent_weight,
        env_weight,
        mix_weight,
        out_weight.reshape(1, chan),
    )
    back8, *returned = exchange(parts, mate_part)
    return pl.pallas_call(
        functools.partial(fold_kernel, steps=steps),
        out_shape=shape((3, atoms), F32),
        in_specs=[VM()] * (3 + nfaces - 1),
        out_specs=VM(),
        name="fold",
    )(own, back8, ghost_index, *returned)


def solution(mesh):
    in_specs = (
        P(None, ("rep", "dom")),
        P(("rep", "dom")),
        P(("rep", "dom")),
        P(("rep", "dom")),
        P(None, ("rep", "dom")),
        P(),
        P(),
        P(),
        P(),
        P(),
        P(),
        P(),
        P(),
        P(),
    )
    out_specs = P(None, ("rep", "dom"))
    return jax.shard_map(shards, mesh=mesh, in_specs=in_specs, out_specs=out_specs, check_vma=False)
```

```python
import functools
import math

import jax
import jax.numpy as jnp
from jax import lax
from jax.experimental import pallas as pl
from jax.experimental.pallas import tpu as pltpu
from jax.sharding import PartitionSpec as P

NBR = 32
BIN_ATOMS = 16
LANES = 128

FACES = ((1, 0, -1.0), (-1, 0, 1.0), (2, 1, -1.0), (-2, 1, 1.0), (8, 2, -1.0), (-8, 2, 1.0))
CUTOFF = 6.0
SOFTEN = 0.5
BOX_SHIFT = 3.0
F32 = jnp.float32
BF16 = jnp.bfloat16

SIN_TERMS = [(-1.0) ** i / math.factorial(2 * i + 1) for i in range(8)]
COS_TERMS = [(-1.0) ** i / math.factorial(2 * i) for i in range(8)]


def swap(block, size, step, flip):
    def partner(i):
        return (i + step if (i // step) % 2 == flip else i - step) % size

    return lax.ppermute(block, "dom", [(i, partner(i)) for i in range(size)])


def poly(terms, square):
    total = jnp.full_like(square, terms[-1])
    for term in terms[-2::-1]:
        total = total * square + term
    return total


def halves(x):
    top = x.astype(BF16)
    return top, (x - top.astype(F32)).astype(BF16)


def wide(x):
    top, rest = halves(x)
    return jnp.concatenate([top, top, rest], axis=1)


def stack(x, *more):
    top, rest = halves(x)
    return jnp.concatenate([top, rest, top, *more], axis=0)


def mm(left, right):
    return jnp.dot(left, right, preferred_element_type=F32)


def mm_nt(left, right):
    return lax.dot_general(left, right, (((1,), (1,)), ((), ())), preferred_element_type=F32)


def lookup(row, index):
    return jnp.take_along_axis(
        jnp.broadcast_to(row, index.shape), index, axis=1, mode="promise_in_bounds"
    )


def parity(step):
    return (lax.axis_index("dom") // step) % 2


def merged(step):
    return 2 * step == lax.axis_size("dom")


def face_slot(refs, a, flip, steps):
    place = 0
    for i, step in enumerate(steps):
        for f in range(1 if merged(step) else 2):
            if i == a and (f == flip or merged(step)):
                return refs[place - 1], 4 * flip if merged(step) else 0
            place += 1
    raise ValueError(a)


def prep_kernel(zeta_table, escale, live, pos, species, ghost_index, nbr, pack, *sends, steps):
    kinds = species[...]
    zeta = scale = jnp.zeros(kinds.shape, F32)
    for k in range(zeta_table.shape[0]):
        zeta = jnp.where(kinds == k, zeta_table[k], zeta)
        scale = jnp.where(kinds == k, escale[k], scale)
    width = kinds.shape[1]
    tiles = width // LANES
    live_row = jnp.full((1, LANES), live[0].astype(F32))
    for t in range(tiles):
        lane = slice(t * LANES, (t + 1) * LANES)
        parts = [pos[:, lane], zeta[:, lane], kinds[:, lane].astype(F32), live_row]
        pack[8 * t : 8 * t + 6, :] = jnp.concatenate(parts, axis=0)
        pack[8 * t + 6 : 8 * t + 7, :] = jnp.zeros((1, LANES), F32)
        pack[8 * t + 7 : 8 * t + 8, :] = scale[:, lane]
    pack[8 * tiles :, :] = nbr[...].astype(F32)
    index = ghost_index[...]
    index = jnp.concatenate([index, index[:2]], axis=0)
    low, high = index & (LANES - 1), index >> 7
    got = []
    for d in range(4):
        value = jnp.zeros(index.shape, F32)
        for t in range(tiles):
            row = pack[8 * t + d : 8 * t + d + 1, :]
            value = jnp.where(high == t, lookup(row, low), value)
        got.append(value)
    for a, step in enumerate(steps):
        par = parity(step)
        for flip in range(2):
            ahead = par == flip
            for d in range(4):
                first, second = got[d][2 * a : 2 * a + 1], got[d][2 * a + 1 : 2 * a + 2]
                if d == a:
                    first, second = first - BOX_SHIFT, second + BOX_SHIFT
                part = jnp.where(ahead, first, second)
                if a == 0 and flip == 0:
                    pack[8 * d + 6 : 8 * d + 7, :] = part
                else:
                    ref, row = face_slot(sends, a, flip, steps)
                    ref[row + d : row + d + 1, :] = part


def weights_kernel(pack, center_t, nbr_row, radial_t, latent, env, mix, out_row, *outs):
    pack_o, out_wide_o, out_row2_o = outs[:3]
    pack_o[...] = pack[...]
    chan = latent.shape[0]
    kinds_total = center_t.shape[0]
    norm = NBR ** (-0.5)
    nb = radial_t.shape[0]
    first = jnp.concatenate(
        [radial_t[...], nbr_row[...], jnp.zeros((LANES - nb - 1, chan), F32)], axis=0
    ).T
    centers = jnp.concatenate([center_t[...], jnp.zeros((LANES - kinds_total, chan), F32)], axis=0).T
    top, rest = halves(0.5 * centers[:, :8])
    w1 = jnp.concatenate([wide(0.5 * first[:, :16]), top, rest], axis=1)
    w2 = wide(0.5 * latent[...])
    mix_a = mix[:, :chan]
    mix_b = mix[:, chan:]
    row = out_row[...]
    w3 = wide(jnp.concatenate([0.5 * mix_a, row, jnp.zeros((15, chan), F32)], axis=0))
    both = (0.5 * norm) * mm(wide(mix_b), stack(env[...]))
    out_col = jnp.broadcast_to(row, (LANES, chan)).T
    out_wide_o[...] = jnp.concatenate([out_col, out_col], axis=1)
    _, orest = halves(out_col)
    lane16 = lax.broadcasted_iota(jnp.int32, (chan, 16), 1)
    extra = jnp.where(lane16 == 0, out_col[:, :16], 0.0).astype(BF16)
    extra = extra + jnp.where(lane16 == 1, orest[:, :16].astype(F32), 0.0).astype(BF16)
    w5 = jnp.concatenate([wide(mix_a.T * (0.5 * row)), extra], axis=1)
    out_row2_o[...] = jnp.concatenate([row, row], axis=1)

    def doubled(x):
        top, rest = halves(jnp.concatenate([jnp.concatenate([x, x], axis=0)] * 2, axis=1))
        return jnp.concatenate([top, top, rest], axis=0)

    w4 = doubled(both.T)
    w6 = doubled(out_col[:, :chan] * both)
    w7 = wide(0.5 * latent[...].T)
    last = jnp.concatenate([0.5 * radial_t[...], jnp.zeros((16 - nb, chan), F32)], axis=0)
    top, rest = halves(jnp.concatenate([last, last], axis=1))
    w8 = jnp.concatenate([top, rest], axis=0)
    for ref, value in zip(outs[3:], (w1, w2, w3, w4, w5, w6, w7, w8)):
        ref[...] = value


def edge_kernel(
    live,
    pack,
    mate,
    out_s,
    row2,
    *refs,
    steps,
    batch,
    basis_count,
    lag,
):
    nfaces = 2 * len(steps)
    nsends = sum(1 if merged(step) else 2 for step in steps) - 1
    ghosts = refs[:nsends]
    weights = refs[nsends : nsends + 8]
    own_out, mate_out = refs[nsends + 8 : nsends + 10]
    ghost_out = refs[nsends + 10 : 2 * nsends + 10]
    (
        table,
        index_s,
        basis_s,
        kinds_s,
        geo_s,
        red_s,
        outf_s,
        db_s,
        acc_s,
        own_s,
        df1_s,
        df2_s,
        f2_s,
        ua_s,
        ub_s,
        sel_s,
    ) = refs[2 * nsends + 10 :]
    chan = out_s.shape[0]
    nb = basis_count
    own_tiles = pack.shape[0] // (8 + NBR)
    tiles = own_tiles + nfaces
    group = LANES // BIN_ATOMS
    wide_row = 2 * LANES

    for t in range(own_tiles):
        table[0, t] = pack[8 * t : 8 * t + 8, :]
        table[1, t] = mate[8 * t : 8 * t + 8, :]
    for a, step in enumerate(steps):
        par = parity(step)
        for flip in range(2):
            tile = own_tiles + 2 * a + jnp.where(par == flip, 1, 0)
            for d in range(4):
                if a == 0 and flip == 0:
                    row = mate[8 * d + 6 : 8 * d + 7, :]
                else:
                    ref, first = face_slot(ghosts, a, flip, steps)
                    row = ref[first + d : first + d + 1, :]
                table[0, tile, d : d + 1, :] = row
    acc_s[...] = jnp.zeros(acc_s.shape, F32)
    own_s[...] = jnp.zeros(own_s.shape, F32)

    w1, w2, w3, w4, w5, w6, w7, w8 = [ref[...] for ref in weights]
    out_row2 = row2[...]
    sub16 = lax.broadcasted_iota(jnp.int32, (16, LANES), 0)
    sub16w = lax.broadcasted_iota(jnp.int32, (16, wide_row), 0)
    ones = jnp.where(sub16w < 2, 1.0, 0.0).astype(BF16)
    from_lane = lax.broadcasted_iota(jnp.int32, (LANES, LANES), 0)
    to_lane = lax.broadcasted_iota(jnp.int32, (LANES, LANES), 1)
    per_row = LANES // NBR
    sel_s[...] = jnp.where(from_lane // NBR == to_lane % per_row, 1.0, 0.0).astype(BF16)
    sub8 = lax.broadcasted_iota(jnp.int32, (8, LANES), 0)
    lane8 = lax.broadcasted_iota(jnp.int32, (8, LANES), 1)
    masks = [jnp.where(sub8 == h * per_row + lane8 // NBR, 1.0, 0.0) for h in range(2)]
    zero8 = jnp.zeros((8, LANES), F32)
    lower = lax.broadcasted_iota(jnp.int32, (NBR, LANES), 1) < chan

    mine = live[0]
    theirs = jnp.max(mate[5:6, :]).astype(jnp.int32)

    def counts(bins):
        even = ((bins + 1) // 2 + group - 1) // group
        odd = (bins // 2 + group - 1) // group
        return even, odd

    my_even, my_odd = counts(mine)
    their_even, their_odd = counts(theirs)
    excess = my_even + my_odd - their_even - their_odd
    give = jnp.minimum(jnp.maximum(excess, 0) // 2, my_even)
    take = jnp.minimum(jnp.maximum(-excess, 0) // 2, their_even)
    keep_even = my_even - give

    def slope2(u, f):
        return u + f * (2.0 - u)

    def block(i, carry):
        is_mate = i >= keep_even + my_odd
        is_odd = jnp.logical_and(i >= keep_even, jnp.logical_not(is_mate))
        which = jnp.where(is_mate, 1, 0)
        odd = jnp.where(is_odd, 1, 0)
        kb = jnp.where(
            is_mate, their_even - take + i - keep_even - my_odd, jnp.where(is_odd, i - keep_even, i)
        )
        bins = jnp.where(is_mate, theirs, mine)
        row0 = pl.multiple_of(64 * kb, 64)

        @pl.when(is_mate)
        def _():
            for part in range(4):
                got = mate[pl.ds(8 * own_tiles + row0 + part, 8, stride=8), :]
                index_s[8 * part : 8 * part + 8, :] = got

        @pl.when(jnp.logical_not(is_mate))
        def _():
            for part in range(4):
                start = 8 * own_tiles + row0 + 4 * odd + part
                index_s[8 * part : 8 * part + 8, :] = pack[pl.ds(start, 8, stride=8), :]

        index = index_s[...].astype(jnp.int32)
        low, high = index & (LANES - 1), index >> 7

        local = 2 * sub8 + odd
        bin_of = 16 * kb + local
        upper = sub8 < 4
        here = []
        for d in (0, 1, 2, 4, 7):
            source = jnp.where(
                upper,
                jnp.broadcast_to(table[which, 2 * kb, d : d + 1, :], (8, LANES)),
                jnp.broadcast_to(table[which, 2 * kb + 1, d : d + 1, :], (8, LANES)),
            )
            found = []
            for part in range(4):
                pick = (local % group) * BIN_ATOMS + part * per_row + lane8 // NBR
                found.append(jnp.take_along_axis(source, pick, axis=1, mode="promise_in_bounds"))
            here.append(jnp.concatenate(found, axis=0))
        kinds = here[3]
        kinds_s[...] = kinds
        occupied = jnp.concatenate([jnp.where(bin_of < bins, 1.0, 0.0)] * 4, axis=0)

        got = []
        for d in range(4):
            value = jnp.zeros((NBR, LANES), F32)
            for t in range(tiles):
                value = jnp.where(high == t, lookup(table[which, t, d : d + 1, :], low), value)
            got.append(value)
        disp = [got[d] - here[d] for d in range(3)]
        square = disp[0] * disp[0] + disp[1] * disp[1] + disp[2] * disp[2]
        dist = jnp.sqrt(square + SOFTEN * SOFTEN)
        inv_dist = 1.0 / dist
        unit = [disp[d] * inv_dist for d in range(3)]
        x = jnp.minimum(dist * (1.0 / CUTOFF), 1.0)
        inv_x = 1.0 / x
        gap = 1.0 - x * x
        envelope = gap * gap
        t = math.pi * (x - 0.5)
        tt = t * t
        s1 = poly(COS_TERMS, tt)
        c1 = -(t * poly(SIN_TERMS, tt))
        sins, coss = [s1], [c1]
        for k in range(2, nb + 1):
            p, q = k // 2 - 1, k - k // 2 - 1
            sins.append(sins[p] * coss[q] + coss[p] * sins[q])
            coss.append(coss[p] * coss[q] - sins[p] * sins[q])
        scale = envelope * inv_x
        for k in range(nb):
            basis_s[pl.ds(k, NBR, stride=16), :] = sins[k] * scale
        basis_s[pl.ds(nb, NBR, stride=16), :] = got[3]
        for k in range(nb + 1, 16):
            basis_s[pl.ds(k, NBR, stride=16), :] = jnp.zeros((NBR, LANES), F32)
        for d in range(3):
            for q, value in ((d, unit[d]), (6 + d, unit[d] * envelope)):
                top = value.astype(BF16).astype(F32)
                geo_s[q] = top
                geo_s[q + 3] = value - top

        def fold8(v):
            return sum(v[8 * j : 8 * j + 8] for j in range(1, chan // 8)) + v[:8]

        def parted(x):
            top = x.astype(BF16).astype(F32)
            return top, x - top

        def terms(top, rest):
            rows = jnp.concatenate([top[:24], top[:24], rest[:24], zero8], axis=0)
            return rows.T[:chan].astype(BF16)

        def centre_sum(both_parts, t):
            found = mm_nt(ub_s[t], both_parts)
            return found[:NBR] + jnp.where(lower, found[NBR:], 0.0)

        def spread_rows(sums, weight):
            top, rest = halves(jnp.concatenate(sums, axis=0))
            out = mm(jnp.concatenate([top, rest, top], axis=1), weight)
            return [out[NBR * i : NBR * i + NBR] for i in range(len(sums))]

        def pieces(q, r):
            return [geo_s[q + d, r : r + 1, :] * masks[r % 2] for d in range(3)]

        def cells(t):
            return [(2 * t + h, h, slice(h * LANES, (h + 1) * LANES)) for h in range(2)]

        z1, z2, z3, direct, sums, lefts, got5, v3, d1 = ({} for _ in range(9))

        def stage_basis(ts):
            for t in ts:
                cols = []
                for r, h, cell in cells(t):
                    hit = sub8.astype(F32) == kinds_s[r : r + 1, :]
                    onehot = jnp.where(hit, 1.0, 0.0)
                    onehot = jnp.concatenate([onehot, onehot], axis=0).astype(BF16)
                    cols.append(stack(basis_s[r * 16 : r * 16 + 16, :], onehot))
                z1[t] = mm(w1, jnp.concatenate(cols, axis=1))

        def stage_units(ts):
            for t in ts:
                for r, h, cell in cells(t):
                    a, b = pieces(0, r), pieces(3, r)
                    ua = jnp.concatenate([*a, *b, *a, zero8], axis=0)
                    ua_s[t, :, cell] = ua.astype(BF16)
                    a, b = pieces(6, r), pieces(9, r)
                    ub = jnp.concatenate([*a, zero8, *b, zero8], axis=0)
                    ub_s[t, :, cell] = ub.astype(BF16)

        def stage_first(ts):
            for t in ts:
                u = 1.0 + jnp.tanh(z1[t])
                f = z1[t] * u
                df1_s[t] = slope2(u, f)
                z2[t] = mm(w2, stack(f))

        def stage_second(ts):
            for t in ts:
                u = 1.0 + jnp.tanh(z2[t])
                f = z2[t] * u
                df2_s[t] = slope2(u, f)
                top, rest = halves(f)
                both_parts = jnp.concatenate([top, rest], axis=0)
                f2_s[t] = both_parts
                sums[t] = centre_sum(both_parts, t)
                direct[t] = mm(w3, jnp.concatenate([top, rest, top], axis=0))

        def stage_env(ts):
            for t, g in zip(ts, spread_rows([sums[t] for t in ts], w4)):
                lefts[t] = terms(*parted(g))
                top, rest = halves(g * out_row2)
                rest = jnp.where(lower, rest, 0.0)[:, :80]
                lefts[t, 1] = jnp.concatenate([w5, jnp.concatenate([top, rest], axis=1)], axis=0)

        def stage_mix(ts):
            for t in ts:
                z3[t] = mm(lefts[t], ua_s[t])

        def stage_third(ts):
            for t in ts:
                for r, h, cell in cells(t):
                    outf_s[r : r + 1, :] = direct[t][chan : chan + 1, cell]
                z = direct[t][:chan] + z3[t]
                u = 1.0 + jnp.tanh(z)
                f = z * u
                v = slope2(u, f)
                folded = fold8(f * out_s[...])
                for r, h, cell in cells(t):
                    red_s[6, 8 * r : 8 * r + 8, :] = folded[:, cell]
                top, rest = halves(v)
                sums[t] = centre_sum(jnp.concatenate([top, rest], axis=0), t)
                got5[t] = mm(lefts[t, 1], jnp.concatenate([top, rest, top, ones], axis=0))

        def stage_denv(ts):
            for t, g in zip(ts, spread_rows([sums[t] for t in ts], w6)):
                top, rest = parted(g)
                lefts[t] = terms(top, rest)
                lefts[t, 1] = jnp.concatenate([top, rest], axis=0).astype(BF16)
                for r, h, cell in cells(t):
                    for d in range(3):
                        part = got5[t][chan + 8 * d : chan + 8 * d + 8, cell]
                        red_s[d, 8 * r : 8 * r + 8, :] = part * masks[h]

        def stage_back(ts):
            for t in ts:
                v3[t] = mm(lefts[t], ua_s[t])

        def stage_slope2(ts):
            for t in ts:
                v = got5[t][:chan] + v3[t]
                d1[t] = mm(w7, stack(v * df2_s[t]))

        def stage_pull(ts):
            for t in ts:
                pulled = mm(lefts[t, 1], f2_s[t])
                for r, h, cell in cells(t):
                    for d in range(3):
                        part = pulled[8 * d : 8 * d + 8, cell] + pulled[NBR + 8 * d : NBR + 8 * d + 8, cell]
                        red_s[3 + d, 8 * r : 8 * r + 8, :] = part * masks[h]

        def stage_slope1(ts):
            for t in ts:
                top, rest = halves(d1[t] * df1_s[t])
                v = mm(w8, jnp.concatenate([top, rest], axis=0))
                v = v[:8] + v[16:24]
                for r, h, cell in cells(t):
                    db_s[8 * r : 8 * r + 8, :] = v[:, cell]

        stages = [
            stage_basis,
            stage_units,
            stage_first,
            stage_second,
            stage_env,
            stage_mix,
            stage_third,
            stage_denv,
            stage_back,
            stage_slope2,
            stage_pull,
            stage_slope1,
        ]
        groups = [range(t0, t0 + batch) for t0 in range(0, NBR // 2, batch)]
        for turn in range(len(stages) + (len(groups) - 1) * lag):
            for i, ts in enumerate(groups):
                if 0 <= turn - i * lag < len(stages):
                    stages[turn - i * lag](ts)

        def collect(ref, q):
            total = ref[q, pl.ds(0, NBR, stride=8), :]
            for k in range(1, 8):
                total = total + ref[q, pl.ds(k, NBR, stride=8), :]
            return total

        pulls = [collect(red_s, 3 + d) for d in range(3)]
        d_unit = [envelope * (collect(red_s, d) + pulls[d]) for d in range(3)]
        d_env = collect(red_s, 6) + outf_s[...]
        for d in range(3):
            d_env = d_env + unit[d] * pulls[d]
        along = jnp.zeros((NBR, LANES), F32)
        level = jnp.zeros((NBR, LANES), F32)
        for k in range(nb):
            g = db_s[pl.ds(k, NBR, stride=8), :]
            ratio = sins[k] * inv_x
            level = level + g * ratio
            along = along + g * ((k + 1) * math.pi * coss[k] - ratio)
        d_env = d_env + envelope * level
        d_x = envelope * envelope * inv_x * along - 4.0 * x * gap * d_env
        radial = d_x * (1.0 / CUTOFF)
        for d in range(3):
            radial = radial - d_unit[d] * unit[d] * inv_dist
        lefts = []
        for d in range(3):
            g = jnp.where(occupied > 0.0, (d_unit[d] * inv_dist + radial * unit[d]) * here[4], 0.0)
            top = g.astype(BF16).astype(F32)
            geo_s[2 * d] = top
            geo_s[2 * d + 1] = g - top
            lefts += [top, g - top]
        sums = mm(jnp.concatenate(lefts, axis=0).astype(BF16), sel_s[...])
        own_rows = []
        for d in range(3):
            total = jnp.zeros((8, LANES), F32)
            for part in range(4):
                row = 64 * d + 8 * part
                value = sums[row : row + 8] + sums[row + NBR : row + NBR + 8]
                total = total + jnp.where((lane8 % BIN_ATOMS) // per_row == part, value, 0.0)
            total = jnp.where(lane8 // BIN_ATOMS == local % group, total, 0.0)
            for h in range(2):
                own_rows.append(jnp.sum(jnp.where(upper == (h == 0), total, 0.0), axis=0, keepdims=True))
        for d in range(3):
            for h in range(2):
                own_s[which, d, pl.ds(2 * kb + h, 1), :] += own_rows[2 * d + h]

        lefts, rights = [], []
        for n in range(NBR):
            lows, highs = low[n : n + 1], high[n : n + 1]
            rights.append(jnp.where(from_lane == lows, 1.0, 0.0).astype(BF16))
            hit = sub16 == highs
            rows = [jnp.where(hit, geo_s[q, n : n + 1, :], 0.0) for q in range(6)]
            lefts.append(jnp.concatenate(rows, axis=0).astype(BF16))
        acc_s[which] += mm_nt(jnp.concatenate(lefts, axis=1), jnp.concatenate(rights, axis=1))
        return carry

    lax.fori_loop(0, keep_even + my_odd + take, block, 0)

    for d in range(3):
        for which in range(2):
            a = acc_s[which, 32 * d : 32 * d + 16, :] + acc_s[which, 32 * d + 16 : 32 * d + 32, :]
            a = own_s[which, d] - a
            for t in range(own_tiles):
                if which:
                    mate_out[4 * t + d : 4 * t + d + 1, :] = a[t : t + 1]
                else:
                    own_out[d : d + 1, t * LANES : (t + 1) * LANES] = a[t : t + 1]
            if which == 0:
                outf_s[0:16, :] = a
                for c, step in enumerate(steps):
                    par = parity(step)
                    for flip in range(2):
                        row = outf_s[pl.ds(own_tiles + 2 * c + jnp.where(par == flip, 1, 0), 1), :]
                        if c == 0 and flip == 0:
                            mate_out[4 * d + 3 : 4 * d + 4, :] = row
                        else:
                            ref, first = face_slot(ghost_out, c, flip, steps)
                            ref[first + d : first + d + 1, :] = row


def fold_kernel(own, back, ghost_index, *refs, steps):
    returned, out = refs[:-1], refs[-1]
    tiles = own.shape[1] // LANES
    lefts, rights = [], []
    for a, step in enumerate(steps):
        par = parity(step)
        for flip in range(2):
            index = ghost_index[pl.ds(2 * a + jnp.where(par == flip, 0, 1), 1), :]
            low, high = index & (LANES - 1), index >> 7
            hit = lax.broadcasted_iota(jnp.int32, (LANES, LANES), 0) == low
            rights.append(jnp.where(hit, 1.0, 0.0).astype(BF16))
            tile_hit = lax.broadcasted_iota(jnp.int32, (16, LANES), 0) == high
            rows = []
            for d in range(3):
                if a == 0 and flip == 0:
                    value = back[4 * d + 3 : 4 * d + 4, :]
                else:
                    ref, first = face_slot(returned, a, flip, steps)
                    value = ref[first + d : first + d + 1, :]
                rows.extend(halves(jnp.where(tile_hit, value, 0.0)))
            lefts.append(jnp.concatenate(rows, axis=0))
    total = mm_nt(jnp.concatenate(lefts, axis=1), jnp.concatenate(rights, axis=1))
    for d in range(3):
        a = total[32 * d : 32 * d + 16] + total[32 * d + 16 : 32 * d + 32]
        for t in range(tiles):
            lane = slice(t * LANES, (t + 1) * LANES)
            out[d : d + 1, lane] = own[d : d + 1, lane] + back[4 * t + d : 4 * t + d + 1, :] + a[t : t + 1]


VM = functools.partial(pl.BlockSpec, memory_space=pltpu.VMEM)
SM = functools.partial(pl.BlockSpec, memory_space=pltpu.SMEM)
SMALL = pltpu.CompilerParams(vmem_limit_bytes=4 * 1024 * 1024)


def shards(
    positions,
    species,
    live_bins,
    edge_nbr,
    ghost_index,
    zeta_table,
    energy_scale,
    center_embed,
    nbr_embed,
    radial_weight,
    latent_weight,
    env_weight,
    mix_weight,
    out_weight,
):
    size = lax.axis_size("dom")
    atoms = species.shape[0]
    chan = latent_weight.shape[0]
    ghosts = ghost_index.shape[1]
    steps = tuple(o for o, _, s in FACES if s < 0)
    shape = jax.ShapeDtypeStruct

    nbr = edge_nbr.reshape(atoms * NBR // LANES, LANES)
    tiles = atoms // LANES
    swaps = [(step, flip) for step in steps for flip in range(1 if 2 * step == size else 2)]
    buffers = [shape((8 if 2 * step == size else 4, ghosts), F32) for step, _ in swaps[1:]]

    def exchange(parts):
        return [swap(part, size, step, flip) for part, (step, flip) in zip(parts, swaps)]

    pack, *sends = pl.pallas_call(
        functools.partial(prep_kernel, steps=steps),
        out_shape=[shape((8 * tiles + nbr.shape[0], LANES), F32)] + buffers,
        in_specs=[SM(), SM(), SM()] + [VM()] * 4,
        out_specs=[VM()] * (1 + len(buffers)),
        name="prep",
    )(zeta_table, energy_scale, live_bins, positions, species.reshape(1, atoms), ghost_index, nbr)
    mate, *arrived = exchange([pack, *sends])

    heights = [(chan, 64), (chan, 3 * chan), (chan + 16, 3 * chan), (6 * chan, LANES)]
    heights += [(chan, 3 * chan + 16), (6 * chan, LANES), (chan, 3 * chan), (32, LANES)]
    pack_here, out_wide, out_row2, *weights = pl.pallas_call(
        weights_kernel,
        out_shape=[shape(pack.shape, F32), shape((chan, 2 * LANES), F32), shape((1, 2 * chan), F32)]
        + [shape(h, BF16) for h in heights],
        in_specs=[VM()] * 8,
        out_specs=[VM()] * (3 + len(heights)),
        compiler_params=SMALL,
        name="weights",
    )(
        pack,
        center_embed.T,
        nbr_embed.reshape(1, chan),
        radial_weight.T,
        latent_weight,
        env_weight,
        mix_weight,
        out_weight.reshape(1, chan),
    )

    pairs = NBR // 2
    big = pltpu.VMEM((pairs, chan, 2 * LANES), F32)
    own, mate_part, *parts = pl.pallas_call(
        functools.partial(edge_kernel, steps=steps, batch=8, lag=1, basis_count=radial_weight.shape[1]),
        out_shape=[shape((3, atoms), F32), shape((4 * tiles, LANES), F32)] + buffers,
        in_specs=[SM()] + [VM()] * (4 + len(buffers) + len(weights)),
        out_specs=[VM()] * (2 + len(buffers)),
        scratch_shapes=[
            pltpu.VMEM((2, 16, 8, LANES), F32),
            pltpu.VMEM((NBR, LANES), F32),
            pltpu.VMEM((NBR * 16, LANES), F32),
            pltpu.VMEM((NBR, LANES), F32),
            pltpu.VMEM((12, NBR, LANES), F32),
            pltpu.VMEM((7, NBR * 8, LANES), F32),
            pltpu.VMEM((NBR, LANES), F32),
            pltpu.VMEM((NBR * 8, LANES), F32),
            pltpu.VMEM((2, 96, LANES), F32),
            pltpu.VMEM((2, 3, 16, LANES), F32),
            big,
            big,
            pltpu.VMEM((pairs, 2 * chan, 2 * LANES), BF16),
            pltpu.VMEM((pairs, 80, 2 * LANES), BF16),
            pltpu.VMEM((pairs, 2 * NBR, 2 * LANES), BF16),
            pltpu.VMEM((LANES, LANES), BF16),
        ],
        compiler_params=pltpu.CompilerParams(vmem_limit_bytes=24 * 1024 * 1024),
        name="edges",
    )(live_bins, pack_here, mate, out_wide, out_row2, *arrived, *weights)
    back, *returned = exchange([mate_part, *parts])
    return pl.pallas_call(
        functools.partial(fold_kernel, steps=steps),
        out_shape=shape((3, atoms), F32),
        in_specs=[VM()] * (3 + len(buffers)),
        out_specs=VM(),
        compiler_params=SMALL,
        name="fold",
    )(own, back, ghost_index, *returned)


def solution(mesh):
    in_specs = (
        P(None, ("rep", "dom")),
        P(("rep", "dom")),
        P(("rep", "dom")),
        P(("rep", "dom")),
        P(None, ("rep", "dom")),
        P(),
        P(),
        P(),
        P(),
        P(),
        P(),
        P(),
        P(),
        P(),
    )
    out_specs = P(None, ("rep", "dom"))
    return jax.shard_map(shards, mesh=mesh, in_specs=in_specs, out_specs=out_specs, check_vma=False)
```

```python
import functools
import math

import jax
import jax.numpy as jnp
from jax import lax
from jax.experimental import pallas as pl
from jax.experimental.pallas import tpu as pltpu
from jax.sharding import PartitionSpec as P

NBR = 32
BIN_ATOMS = 16
LANES = 128

FACES = ((1, 0, -1.0), (-1, 0, 1.0), (2, 1, -1.0), (-2, 1, 1.0), (8, 2, -1.0), (-8, 2, 1.0))
CUTOFF = 6.0
SOFTEN = 0.5
BOX_SHIFT = 3.0
F32 = jnp.float32
BF16 = jnp.bfloat16

SIN_TERMS = [(-1.0) ** i / math.factorial(2 * i + 1) for i in range(8)]
COS_TERMS = [(-1.0) ** i / math.factorial(2 * i) for i in range(8)]


def swap(block, size, step, flip):
    def partner(i):
        return (i + step if (i // step) % 2 == flip else i - step) % size

    return lax.ppermute(block, "dom", [(i, partner(i)) for i in range(size)])


def poly(terms, square):
    total = jnp.full_like(square, terms[-1])
    for term in terms[-2::-1]:
        total = total * square + term
    return total


def halves(x):
    top = x.astype(BF16)
    return top, (x - top.astype(F32)).astype(BF16)


def wide(x):
    top, rest = halves(x)
    return jnp.concatenate([top, top, rest], axis=1)


def stack(x, *more):
    top, rest = halves(x)
    return jnp.concatenate([top, rest, top, *more], axis=0)


def mm(left, right):
    return jnp.dot(left, right, preferred_element_type=F32)


def mm_nt(left, right):
    return lax.dot_general(left, right, (((1,), (1,)), ((), ())), preferred_element_type=F32)


def lookup(row, index):
    return jnp.take_along_axis(
        jnp.broadcast_to(row, index.shape), index, axis=1, mode="promise_in_bounds"
    )


def parity(step):
    return (lax.axis_index("dom") // step) % 2


def merged(step):
    return 2 * step == lax.axis_size("dom")


def face_slot(refs, a, flip, steps):
    place = 0
    for i, step in enumerate(steps):
        for f in range(1 if merged(step) else 2):
            if i == a and (f == flip or merged(step)):
                return refs[place - 1], 4 * flip if merged(step) else 0
            place += 1
    raise ValueError(a)


def prep_kernel(zeta_table, escale, live, pos, species, ghost_index, nbr, pack, *sends, steps):
    kinds = species[...]
    zeta = scale = jnp.zeros(kinds.shape, F32)
    for k in range(zeta_table.shape[0]):
        zeta = jnp.where(kinds == k, zeta_table[k], zeta)
        scale = jnp.where(kinds == k, escale[k], scale)
    width = kinds.shape[1]
    tiles = width // LANES
    live_row = jnp.full((1, LANES), live[0].astype(F32))
    for t in range(tiles):
        lane = slice(t * LANES, (t + 1) * LANES)
        parts = [pos[:, lane], zeta[:, lane], kinds[:, lane].astype(F32), live_row]
        pack[8 * t : 8 * t + 6, :] = jnp.concatenate(parts, axis=0)
        pack[8 * t + 6 : 8 * t + 7, :] = jnp.zeros((1, LANES), F32)
        pack[8 * t + 7 : 8 * t + 8, :] = scale[:, lane]
    pack[8 * tiles :, :] = nbr[...].astype(F32)
    index = ghost_index[...]
    index = jnp.concatenate([index, index[:2]], axis=0)
    low, high = index & (LANES - 1), index >> 7
    got = []
    for d in range(4):
        value = jnp.zeros(index.shape, F32)
        for t in range(tiles):
            row = pack[8 * t + d : 8 * t + d + 1, :]
            value = jnp.where(high == t, lookup(row, low), value)
        got.append(value)
    for a, step in enumerate(steps):
        par = parity(step)
        for flip in range(2):
            ahead = par == flip
            for d in range(4):
                first, second = got[d][2 * a : 2 * a + 1], got[d][2 * a + 1 : 2 * a + 2]
                if d == a:
                    first, second = first - BOX_SHIFT, second + BOX_SHIFT
                part = jnp.where(ahead, first, second)
                if a == 0 and flip == 0:
                    pack[8 * d + 6 : 8 * d + 7, :] = part
                else:
                    ref, row = face_slot(sends, a, flip, steps)
                    ref[row + d : row + d + 1, :] = part


def weights_kernel(pack, center_t, nbr_row, radial_t, latent, env, mix, out_row, *outs):
    pack_o, out_wide_o, out_row2_o = outs[:3]
    pack_o[...] = pack[...]
    chan = latent.shape[0]
    kinds_total = center_t.shape[0]
    norm = NBR ** (-0.5)
    nb = radial_t.shape[0]
    first = jnp.concatenate(
        [radial_t[...], nbr_row[...], jnp.zeros((LANES - nb - 1, chan), F32)], axis=0
    ).T
    centers = jnp.concatenate([center_t[...], jnp.zeros((LANES - kinds_total, chan), F32)], axis=0).T
    top, rest = halves(0.5 * centers[:, :8])
    w1 = jnp.concatenate([wide(0.5 * first[:, :16]), top, rest], axis=1)
    w2 = wide(0.5 * latent[...])
    mix_a = mix[:, :chan]
    mix_b = mix[:, chan:]
    row = out_row[...]
    w3 = wide(jnp.concatenate([0.5 * mix_a, row, jnp.zeros((15, chan), F32)], axis=0))
    both = (0.5 * norm) * mm(wide(mix_b), stack(env[...]))
    out_col = jnp.broadcast_to(row, (LANES, chan)).T
    out_wide_o[...] = jnp.concatenate([out_col, out_col], axis=1)
    _, orest = halves(out_col)
    lane16 = lax.broadcasted_iota(jnp.int32, (chan, 16), 1)
    extra = jnp.where(lane16 == 0, out_col[:, :16], 0.0).astype(BF16)
    extra = extra + jnp.where(lane16 == 1, orest[:, :16].astype(F32), 0.0).astype(BF16)
    w5 = jnp.concatenate([wide(mix_a.T * (0.5 * row)), extra], axis=1)
    out_row2_o[...] = jnp.concatenate([row, row], axis=1)

    def doubled(x):
        top, rest = halves(jnp.concatenate([jnp.concatenate([x, x], axis=0)] * 2, axis=1))
        return jnp.concatenate([top, top, rest], axis=0)

    w4 = doubled(both.T)
    w6 = doubled(out_col[:, :chan] * both)
    w7 = wide(0.5 * latent[...].T)
    last = jnp.concatenate([0.5 * radial_t[...], jnp.zeros((16 - nb, chan), F32)], axis=0)
    top, rest = halves(jnp.concatenate([last, last], axis=1))
    w8 = jnp.concatenate([top, rest], axis=0)
    for ref, value in zip(outs[3:], (w1, w2, w3, w4, w5, w6, w7, w8)):
        ref[...] = value


def edge_kernel(
    live,
    pack,
    mate,
    out_s,
    row2,
    *refs,
    steps,
    batch,
    basis_count,
    lag,
):
    nfaces = 2 * len(steps)
    nsends = sum(1 if merged(step) else 2 for step in steps) - 1
    ghosts = refs[:nsends]
    weights = refs[nsends : nsends + 8]
    own_out, mate_out = refs[nsends + 8 : nsends + 10]
    ghost_out = refs[nsends + 10 : 2 * nsends + 10]
    (
        table,
        lists,
        index_s,
        keep_s,
        basis_s,
        kinds_s,
        geo_s,
        force_s,
        red_s,
        outf_s,
        db_s,
        acc_s,
        own_s,
        df1_s,
        df2_s,
        f2_s,
        ua_s,
        ub_s,
        sel_s,
    ) = refs[2 * nsends + 10 :]
    chan = out_s.shape[0]
    nb = basis_count
    own_tiles = pack.shape[0] // (8 + NBR)
    tiles = own_tiles + nfaces
    group = LANES // BIN_ATOMS
    wide_row = 2 * LANES

    for t in range(own_tiles):
        table[0, t] = pack[8 * t : 8 * t + 8, :]
        table[1, t] = mate[8 * t : 8 * t + 8, :]
    edge_rows = pack.shape[0] - 8 * own_tiles
    lists[:edge_rows, :] = pack[8 * own_tiles :, :]
    lists[edge_rows:, :] = mate[8 * own_tiles :, :]
    for a, step in enumerate(steps):
        par = parity(step)
        for flip in range(2):
            tile = own_tiles + 2 * a + jnp.where(par == flip, 1, 0)
            for d in range(4):
                if a == 0 and flip == 0:
                    row = mate[8 * d + 6 : 8 * d + 7, :]
                else:
                    ref, first = face_slot(ghosts, a, flip, steps)
                    row = ref[first + d : first + d + 1, :]
                table[0, tile, d : d + 1, :] = row
    acc_s[...] = jnp.zeros(acc_s.shape, F32)
    own_s[...] = jnp.zeros(own_s.shape, F32)
    for ref in (keep_s, index_s, red_s, outf_s, db_s):
        ref[...] = jnp.zeros(ref.shape, F32)

    w1, w2, w3, w4, w5, w6, w7, w8 = [ref[...] for ref in weights]
    out_row2 = row2[...]
    sub16 = lax.broadcasted_iota(jnp.int32, (16, LANES), 0)
    sub16w = lax.broadcasted_iota(jnp.int32, (16, wide_row), 0)
    ones = jnp.where(sub16w < 2, 1.0, 0.0).astype(BF16)
    from_lane = lax.broadcasted_iota(jnp.int32, (LANES, LANES), 0)
    to_lane = lax.broadcasted_iota(jnp.int32, (LANES, LANES), 1)
    per_row = LANES // NBR
    lane_bf = from_lane.astype(F32).astype(BF16)
    one_bf, zero_bf = jnp.ones((), BF16), jnp.zeros((), BF16)
    sel_s[...] = jnp.where(from_lane // NBR == to_lane % per_row, 1.0, 0.0).astype(BF16)
    sub8 = lax.broadcasted_iota(jnp.int32, (8, LANES), 0)
    lane8 = lax.broadcasted_iota(jnp.int32, (8, LANES), 1)
    masks = [jnp.where(sub8 == h * per_row + lane8 // NBR, 1.0, 0.0) for h in range(2)]
    zero8 = jnp.zeros((8, LANES), F32)
    lower = lax.broadcasted_iota(jnp.int32, (NBR, LANES), 1) < chan

    mine = live[0]
    theirs = jnp.max(mate[5:6, :]).astype(jnp.int32)

    def counts(bins):
        even = ((bins + 1) // 2 + group - 1) // group
        odd = (bins // 2 + group - 1) // group
        return even, odd

    my_even, my_odd = counts(mine)
    their_even, their_odd = counts(theirs)
    excess = my_even + my_odd - their_even - their_odd
    give = jnp.minimum(jnp.maximum(excess, 0) // 2, my_even)
    take = jnp.minimum(jnp.maximum(-excess, 0) // 2, their_even)
    keep_even = my_even - give

    def slope2(u, f):
        return u + f * (2.0 - u)

    def finish(which, kb, odd):
        index = index_s[...].astype(jnp.int32)
        low, high = index & (LANES - 1), index >> 7
        local = 2 * sub8 + odd
        upper = sub8 < 4
        kept = [keep_s[q] for q in range(keep_s.shape[0])]
        sins, coss, unit = kept[:nb], kept[nb : 2 * nb], kept[2 * nb : 2 * nb + 3]
        envelope, x, inv_x, gap, inv_dist, scale_of, occupied = kept[2 * nb + 3 :]

        def collect(ref, q):
            total = ref[q, pl.ds(0, NBR, stride=8), :]
            for k in range(1, 8):
                total = total + ref[q, pl.ds(k, NBR, stride=8), :]
            return total

        pulls = [collect(red_s, 3 + d) for d in range(3)]
        d_unit = [envelope * (collect(red_s, d) + pulls[d]) for d in range(3)]
        d_env = collect(red_s, 6) + outf_s[...]
        for d in range(3):
            d_env = d_env + unit[d] * pulls[d]
        along = jnp.zeros((NBR, LANES), F32)
        level = jnp.zeros((NBR, LANES), F32)
        for k in range(nb):
            g = db_s[pl.ds(k, NBR, stride=8), :]
            ratio = sins[k] * inv_x
            level = level + g * ratio
            along = along + g * ((k + 1) * math.pi * coss[k] - ratio)
        d_env = d_env + envelope * level
        d_x = envelope * envelope * inv_x * along - 4.0 * x * gap * d_env
        radial = d_x * (1.0 / CUTOFF)
        for d in range(3):
            radial = radial - d_unit[d] * unit[d] * inv_dist
        lefts = []
        for d in range(3):
            g = jnp.where(occupied > 0.0, (d_unit[d] * inv_dist + radial * unit[d]) * scale_of, 0.0)
            top = g.astype(BF16).astype(F32)
            force_s[2 * d] = top
            force_s[2 * d + 1] = g - top
            lefts += [top, g - top]
        sums = mm(jnp.concatenate(lefts, axis=0).astype(BF16), sel_s[...])
        own_rows = []
        for d in range(3):
            total = jnp.zeros((8, LANES), F32)
            for part in range(4):
                row = 64 * d + 8 * part
                value = sums[row : row + 8] + sums[row + NBR : row + NBR + 8]
                total = total + jnp.where((lane8 % BIN_ATOMS) // per_row == part, value, 0.0)
            total = jnp.where(lane8 // BIN_ATOMS == local % group, total, 0.0)
            for h in range(2):
                own_rows.append(jnp.sum(jnp.where(upper == (h == 0), total, 0.0), axis=0, keepdims=True))
        for d in range(3):
            for h in range(2):
                own_s[which, d, pl.ds(2 * kb + h, 1), :] += own_rows[2 * d + h]

        lefts, rights = [], []
        index_s[...] = low.astype(F32)
        for n in range(NBR):
            highs = high[n : n + 1]
            lows = jnp.broadcast_to(index_s[n : n + 1, :], (16, LANES)).astype(BF16)
            lows = jnp.concatenate([lows] * (LANES // 16), axis=0)
            rights.append(jnp.where(lane_bf == lows, one_bf, zero_bf))
            hit = sub16 == highs
            rows = [jnp.where(hit, force_s[q, n : n + 1, :], 0.0) for q in range(6)]
            lefts.append(jnp.concatenate(rows, axis=0).astype(BF16))
        acc_s[which] += mm_nt(jnp.concatenate(lefts, axis=1), jnp.concatenate(rights, axis=1))

    def block(i, carry):
        finish(*carry)
        is_mate = i >= keep_even + my_odd
        is_odd = jnp.logical_and(i >= keep_even, jnp.logical_not(is_mate))
        which = jnp.where(is_mate, 1, 0)
        odd = jnp.where(is_odd, 1, 0)
        kb = jnp.where(
            is_mate, their_even - take + i - keep_even - my_odd, jnp.where(is_odd, i - keep_even, i)
        )
        bins = jnp.where(is_mate, theirs, mine)
        start = edge_rows * which + 64 * kb + 4 * odd
        rows = [lists[pl.ds(start + part, 8, stride=8), :] for part in range(4)]
        index = jnp.concatenate(rows, axis=0)
        index_s[...] = index
        index = index.astype(jnp.int32)
        low, high = index & (LANES - 1), index >> 7

        local = 2 * sub8 + odd
        bin_of = 16 * kb + local
        upper = sub8 < 4
        here = []
        for d in (0, 1, 2, 4, 7):
            source = jnp.where(
                upper,
                jnp.broadcast_to(table[which, 2 * kb, d : d + 1, :], (8, LANES)),
                jnp.broadcast_to(table[which, 2 * kb + 1, d : d + 1, :], (8, LANES)),
            )
            found = []
            for part in range(4):
                pick = (local % group) * BIN_ATOMS + part * per_row + lane8 // NBR
                found.append(jnp.take_along_axis(source, pick, axis=1, mode="promise_in_bounds"))
            here.append(jnp.concatenate(found, axis=0))
        kinds = here[3]
        kinds_s[...] = kinds
        occupied = jnp.concatenate([jnp.where(bin_of < bins, 1.0, 0.0)] * 4, axis=0)

        got = []
        for d in range(4):
            value = jnp.zeros((NBR, LANES), F32)
            for t in range(tiles):
                value = jnp.where(high == t, lookup(table[which, t, d : d + 1, :], low), value)
            got.append(value)
        disp = [got[d] - here[d] for d in range(3)]
        square = disp[0] * disp[0] + disp[1] * disp[1] + disp[2] * disp[2]
        dist = jnp.sqrt(square + SOFTEN * SOFTEN)
        inv_dist = 1.0 / dist
        unit = [disp[d] * inv_dist for d in range(3)]
        x = jnp.minimum(dist * (1.0 / CUTOFF), 1.0)
        inv_x = 1.0 / x
        gap = 1.0 - x * x
        envelope = gap * gap
        t = math.pi * (x - 0.5)
        tt = t * t
        s1 = poly(COS_TERMS, tt)
        c1 = -(t * poly(SIN_TERMS, tt))
        sins, coss = [s1], [c1]
        for k in range(2, nb + 1):
            p, q = k // 2 - 1, k - k // 2 - 1
            sins.append(sins[p] * coss[q] + coss[p] * sins[q])
            coss.append(coss[p] * coss[q] - sins[p] * sins[q])
        scale = envelope * inv_x
        for k in range(nb):
            basis_s[pl.ds(k, NBR, stride=16), :] = sins[k] * scale
        basis_s[pl.ds(nb, NBR, stride=16), :] = got[3]
        for k in range(nb + 1, 16):
            basis_s[pl.ds(k, NBR, stride=16), :] = jnp.zeros((NBR, LANES), F32)
        for d in range(3):
            for q, value in ((d, unit[d]), (6 + d, unit[d] * envelope)):
                top = value.astype(BF16).astype(F32)
                geo_s[q] = top
                geo_s[q + 3] = value - top

        def fold8(v):
            return sum(v[8 * j : 8 * j + 8] for j in range(1, chan // 8)) + v[:8]

        def parted(x):
            top = x.astype(BF16).astype(F32)
            return top, x - top

        def terms(top, rest):
            rows = jnp.concatenate([top[:24], top[:24], rest[:24], zero8], axis=0)
            return rows.T[:chan].astype(BF16)

        def centre_sum(both_parts, t):
            found = mm_nt(ub_s[t], both_parts)
            return found[:NBR] + jnp.where(lower, found[NBR:], 0.0)

        def spread_rows(sums, weight):
            top, rest = halves(jnp.concatenate(sums, axis=0))
            out = mm(jnp.concatenate([top, rest, top], axis=1), weight)
            return [out[NBR * i : NBR * i + NBR] for i in range(len(sums))]

        def pieces(q, r):
            return [geo_s[q + d, r : r + 1, :] * masks[r % 2] for d in range(3)]

        def cells(t):
            return [(2 * t + h, h, slice(h * LANES, (h + 1) * LANES)) for h in range(2)]

        z1, z2, z3, direct, sums, lefts, got5, v3, d1 = ({} for _ in range(9))

        def stage_basis(ts):
            for t in ts:
                cols = []
                for r, h, cell in cells(t):
                    hit = sub8.astype(F32) == kinds_s[r : r + 1, :]
                    onehot = jnp.where(hit, 1.0, 0.0)
                    onehot = jnp.concatenate([onehot, onehot], axis=0).astype(BF16)
                    cols.append(stack(basis_s[r * 16 : r * 16 + 16, :], onehot))
                z1[t] = mm(w1, jnp.concatenate(cols, axis=1))

        def stage_units(ts):
            for t in ts:
                for r, h, cell in cells(t):
                    a, b = pieces(0, r), pieces(3, r)
                    ua = jnp.concatenate([*a, *b, *a, zero8], axis=0)
                    ua_s[t, :, cell] = ua.astype(BF16)
                    a, b = pieces(6, r), pieces(9, r)
                    ub = jnp.concatenate([*a, zero8, *b, zero8], axis=0)
                    ub_s[t, :, cell] = ub.astype(BF16)

        def stage_first(ts):
            for t in ts:
                u = 1.0 + jnp.tanh(z1[t])
                f = z1[t] * u
                df1_s[t] = slope2(u, f)
                z2[t] = mm(w2, stack(f))

        def stage_second(ts):
            for t in ts:
                u = 1.0 + jnp.tanh(z2[t])
                f = z2[t] * u
                df2_s[t] = slope2(u, f)
                top, rest = halves(f)
                both_parts = jnp.concatenate([top, rest], axis=0)
                f2_s[t] = both_parts
                sums[t] = centre_sum(both_parts, t)
                direct[t] = mm(w3, jnp.concatenate([top, rest, top], axis=0))

        def stage_env(ts):
            for t, g in zip(ts, spread_rows([sums[t] for t in ts], w4)):
                lefts[t] = terms(*parted(g))
                top, rest = halves(g * out_row2)
                rest = jnp.where(lower, rest, 0.0)[:, :80]
                lefts[t, 1] = jnp.concatenate([w5, jnp.concatenate([top, rest], axis=1)], axis=0)

        def stage_mix(ts):
            for t in ts:
                z3[t] = mm(lefts[t], ua_s[t])

        def stage_third(ts):
            for t in ts:
                for r, h, cell in cells(t):
                    outf_s[r : r + 1, :] = direct[t][chan : chan + 1, cell]
                z = direct[t][:chan] + z3[t]
                u = 1.0 + jnp.tanh(z)
                f = z * u
                v = slope2(u, f)
                folded = fold8(f * out_s[...])
                for r, h, cell in cells(t):
                    red_s[6, 8 * r : 8 * r + 8, :] = folded[:, cell]
                top, rest = halves(v)
                sums[t] = centre_sum(jnp.concatenate([top, rest], axis=0), t)
                got5[t] = mm(lefts[t, 1], jnp.concatenate([top, rest, top, ones], axis=0))

        def stage_denv(ts):
            for t, g in zip(ts, spread_rows([sums[t] for t in ts], w6)):
                top, rest = parted(g)
                lefts[t] = terms(top, rest)
                lefts[t, 1] = jnp.concatenate([top, rest], axis=0).astype(BF16)
                for r, h, cell in cells(t):
                    for d in range(3):
                        part = got5[t][chan + 8 * d : chan + 8 * d + 8, cell]
                        red_s[d, 8 * r : 8 * r + 8, :] = part * masks[h]

        def stage_back(ts):
            for t in ts:
                v3[t] = mm(lefts[t], ua_s[t])

        def stage_slope2(ts):
            for t in ts:
                v = got5[t][:chan] + v3[t]
                d1[t] = mm(w7, stack(v * df2_s[t]))

        def stage_pull(ts):
            for t in ts:
                pulled = mm(lefts[t, 1], f2_s[t])
                for r, h, cell in cells(t):
                    for d in range(3):
                        part = pulled[8 * d : 8 * d + 8, cell] + pulled[NBR + 8 * d : NBR + 8 * d + 8, cell]
                        red_s[3 + d, 8 * r : 8 * r + 8, :] = part * masks[h]

        def stage_slope1(ts):
            for t in ts:
                top, rest = halves(d1[t] * df1_s[t])
                v = mm(w8, jnp.concatenate([top, rest], axis=0))
                v = v[:8] + v[16:24]
                for r, h, cell in cells(t):
                    db_s[8 * r : 8 * r + 8, :] = v[:, cell]

        stages = [
            stage_basis,
            stage_units,
            stage_first,
            stage_second,
            stage_env,
            stage_mix,
            stage_third,
            stage_denv,
            stage_pull,
            stage_back,
            stage_slope2,
            stage_slope1,
        ]
        groups = [range(t0, t0 + batch) for t0 in range(0, NBR // 2, batch)]
        for turn in range(len(stages) + (len(groups) - 1) * lag):
            for i, ts in enumerate(groups):
                if 0 <= turn - i * lag < len(stages):
                    stages[turn - i * lag](ts)

        for q, value in enumerate([*sins, *coss, *unit, envelope, x, inv_x, gap, inv_dist, here[4], occupied]):
            keep_s[q] = value
        return which, kb, odd

    zero = jnp.int32(0)
    last = lax.fori_loop(0, keep_even + my_odd + take, block, (zero, zero, zero))
    finish(*last)

    for d in range(3):
        for which in range(2):
            a = acc_s[which, 32 * d : 32 * d + 16, :] + acc_s[which, 32 * d + 16 : 32 * d + 32, :]
            a = own_s[which, d] - a
            for t in range(own_tiles):
                if which:
                    mate_out[4 * t + d : 4 * t + d + 1, :] = a[t : t + 1]
                else:
                    own_out[d : d + 1, t * LANES : (t + 1) * LANES] = a[t : t + 1]
            if which == 0:
                outf_s[0:16, :] = a
                for c, step in enumerate(steps):
                    par = parity(step)
                    for flip in range(2):
                        row = outf_s[pl.ds(own_tiles + 2 * c + jnp.where(par == flip, 1, 0), 1), :]
                        if c == 0 and flip == 0:
                            mate_out[4 * d + 3 : 4 * d + 4, :] = row
                        else:
                            ref, first = face_slot(ghost_out, c, flip, steps)
                            ref[first + d : first + d + 1, :] = row


def fold_kernel(own, back, ghost_index, *refs, steps):
    returned, out = refs[:-1], refs[-1]
    tiles = own.shape[1] // LANES
    lefts, rights = [], []
    for a, step in enumerate(steps):
        par = parity(step)
        for flip in range(2):
            index = ghost_index[pl.ds(2 * a + jnp.where(par == flip, 0, 1), 1), :]
            low, high = index & (LANES - 1), index >> 7
            hit = lax.broadcasted_iota(jnp.int32, (LANES, LANES), 0) == low
            rights.append(jnp.where(hit, 1.0, 0.0).astype(BF16))
            tile_hit = lax.broadcasted_iota(jnp.int32, (16, LANES), 0) == high
            rows = []
            for d in range(3):
                if a == 0 and flip == 0:
                    value = back[4 * d + 3 : 4 * d + 4, :]
                else:
                    ref, first = face_slot(returned, a, flip, steps)
                    value = ref[first + d : first + d + 1, :]
                rows.extend(halves(jnp.where(tile_hit, value, 0.0)))
            lefts.append(jnp.concatenate(rows, axis=0))
    total = mm_nt(jnp.concatenate(lefts, axis=1), jnp.concatenate(rights, axis=1))
    for d in range(3):
        a = total[32 * d : 32 * d + 16] + total[32 * d + 16 : 32 * d + 32]
        for t in range(tiles):
            lane = slice(t * LANES, (t + 1) * LANES)
            out[d : d + 1, lane] = own[d : d + 1, lane] + back[4 * t + d : 4 * t + d + 1, :] + a[t : t + 1]


VM = functools.partial(pl.BlockSpec, memory_space=pltpu.VMEM)
SM = functools.partial(pl.BlockSpec, memory_space=pltpu.SMEM)
SMALL = pltpu.CompilerParams(vmem_limit_bytes=4 * 1024 * 1024)


def shards(
    positions,
    species,
    live_bins,
    edge_nbr,
    ghost_index,
    zeta_table,
    energy_scale,
    center_embed,
    nbr_embed,
    radial_weight,
    latent_weight,
    env_weight,
    mix_weight,
    out_weight,
):
    size = lax.axis_size("dom")
    atoms = species.shape[0]
    chan = latent_weight.shape[0]
    ghosts = ghost_index.shape[1]
    steps = tuple(o for o, _, s in FACES if s < 0)
    shape = jax.ShapeDtypeStruct

    nbr = edge_nbr.reshape(atoms * NBR // LANES, LANES)
    tiles = atoms // LANES
    swaps = [(step, flip) for step in steps for flip in range(1 if 2 * step == size else 2)]
    buffers = [shape((8 if 2 * step == size else 4, ghosts), F32) for step, _ in swaps[1:]]

    def exchange(parts):
        return [swap(part, size, step, flip) for part, (step, flip) in zip(parts, swaps)]

    pack, *sends = pl.pallas_call(
        functools.partial(prep_kernel, steps=steps),
        out_shape=[shape((8 * tiles + nbr.shape[0], LANES), F32)] + buffers,
        in_specs=[SM(), SM(), SM()] + [VM()] * 4,
        out_specs=[VM()] * (1 + len(buffers)),
        name="prep",
    )(zeta_table, energy_scale, live_bins, positions, species.reshape(1, atoms), ghost_index, nbr)
    mate, *arrived = exchange([pack, *sends])

    heights = [(chan, 64), (chan, 3 * chan), (chan + 16, 3 * chan), (6 * chan, LANES)]
    heights += [(chan, 3 * chan + 16), (6 * chan, LANES), (chan, 3 * chan), (32, LANES)]
    pack_here, out_wide, out_row2, *weights = pl.pallas_call(
        weights_kernel,
        out_shape=[shape(pack.shape, F32), shape((chan, 2 * LANES), F32), shape((1, 2 * chan), F32)]
        + [shape(h, BF16) for h in heights],
        in_specs=[VM()] * 8,
        out_specs=[VM()] * (3 + len(heights)),
        compiler_params=SMALL,
        name="weights",
    )(
        pack,
        center_embed.T,
        nbr_embed.reshape(1, chan),
        radial_weight.T,
        latent_weight,
        env_weight,
        mix_weight,
        out_weight.reshape(1, chan),
    )

    pairs = NBR // 2
    big = pltpu.VMEM((pairs, chan, 2 * LANES), F32)
    own, mate_part, *parts = pl.pallas_call(
        functools.partial(edge_kernel, steps=steps, batch=8, lag=1, basis_count=radial_weight.shape[1]),
        out_shape=[shape((3, atoms), F32), shape((4 * tiles, LANES), F32)] + buffers,
        in_specs=[SM()] + [VM()] * (4 + len(buffers) + len(weights)),
        out_specs=[VM()] * (2 + len(buffers)),
        scratch_shapes=[
            pltpu.VMEM((2, 16, 8, LANES), F32),
            pltpu.VMEM((2 * nbr.shape[0], LANES), F32),
            pltpu.VMEM((NBR, LANES), F32),
            pltpu.VMEM((2 * radial_weight.shape[1] + 10, NBR, LANES), F32),
            pltpu.VMEM((NBR * 16, LANES), F32),
            pltpu.VMEM((NBR, LANES), F32),
            pltpu.VMEM((12, NBR, LANES), F32),
            pltpu.VMEM((6, NBR, LANES), F32),
            pltpu.VMEM((7, NBR * 8, LANES), F32),
            pltpu.VMEM((NBR, LANES), F32),
            pltpu.VMEM((NBR * 8, LANES), F32),
            pltpu.VMEM((2, 96, LANES), F32),
            pltpu.VMEM((2, 3, 16, LANES), F32),
            big,
            big,
            pltpu.VMEM((pairs, 2 * chan, 2 * LANES), BF16),
            pltpu.VMEM((pairs, 80, 2 * LANES), BF16),
            pltpu.VMEM((pairs, 2 * NBR, 2 * LANES), BF16),
            pltpu.VMEM((LANES, LANES), BF16),
        ],
        compiler_params=pltpu.CompilerParams(vmem_limit_bytes=24 * 1024 * 1024),
        name="edges",
    )(live_bins, pack_here, mate, out_wide, out_row2, *arrived, *weights)
    back, *returned = exchange([mate_part, *parts])
    return pl.pallas_call(
        functools.partial(fold_kernel, steps=steps),
        out_shape=shape((3, atoms), F32),
        in_specs=[VM()] * (3 + len(buffers)),
        out_specs=VM(),
        compiler_params=SMALL,
        name="fold",
    )(own, back, ghost_index, *returned)


def solution(mesh):
    in_specs = (
        P(None, ("rep", "dom")),
        P(("rep", "dom")),
        P(("rep", "dom")),
        P(("rep", "dom")),
        P(None, ("rep", "dom")),
        P(),
        P(),
        P(),
        P(),
        P(),
        P(),
        P(),
        P(),
        P(),
    )
    out_specs = P(None, ("rep", "dom"))
    return jax.shard_map(shards, mesh=mesh, in_specs=in_specs, out_specs=out_specs, check_vma=False)
```

```python
import functools
import math

import jax
import jax.numpy as jnp
from jax import lax
from jax.experimental import pallas as pl
from jax.experimental.pallas import tpu as pltpu
from jax.sharding import PartitionSpec as P

NBR = 32
BIN_ATOMS = 16
LANES = 128

FACES = ((1, 0, -1.0), (-1, 0, 1.0), (2, 1, -1.0), (-2, 1, 1.0), (8, 2, -1.0), (-8, 2, 1.0))
CUTOFF = 6.0
SOFTEN = 0.5
BOX_SHIFT = 3.0
F32 = jnp.float32
BF16 = jnp.bfloat16

SIN_TERMS = [(-1.0) ** i / math.factorial(2 * i + 1) for i in range(8)]
COS_TERMS = [(-1.0) ** i / math.factorial(2 * i) for i in range(8)]


def swap(block, size, step, flip):
    def partner(i):
        return (i + step if (i // step) % 2 == flip else i - step) % size

    return lax.ppermute(block, "dom", [(i, partner(i)) for i in range(size)])


def poly(terms, square):
    total = jnp.full_like(square, terms[-1])
    for term in terms[-2::-1]:
        total = total * square + term
    return total


def halves(x):
    top = x.astype(BF16)
    return top, (x - top.astype(F32)).astype(BF16)


def wide(x):
    top, rest = halves(x)
    return jnp.concatenate([top, top, rest], axis=1)


def stack(x, *more):
    top, rest = halves(x)
    return jnp.concatenate([top, rest, top, *more], axis=0)


def mm(left, right):
    return jnp.dot(left, right, preferred_element_type=F32)


def mm_nt(left, right):
    return lax.dot_general(left, right, (((1,), (1,)), ((), ())), preferred_element_type=F32)


def lookup(row, index):
    return jnp.take_along_axis(
        jnp.broadcast_to(row, index.shape), index, axis=1, mode="promise_in_bounds"
    )


def parity(step):
    return (lax.axis_index("dom") // step) % 2


def merged(step):
    return 2 * step == lax.axis_size("dom")


def face_slot(refs, a, flip, steps):
    place = 0
    for i, step in enumerate(steps):
        for f in range(1 if merged(step) else 2):
            if i == a and (f == flip or merged(step)):
                return refs[place - 1], 4 * flip if merged(step) else 0
            place += 1
    raise ValueError(a)


def prep_kernel(
    zeta_table, escale, live, pos, species, ghost_index, nbr, nbr_row, out_row, pack, *sends, steps
):
    kinds = species[...]
    zeta = scale = jnp.zeros(kinds.shape, F32)
    for k in range(zeta_table.shape[0]):
        zeta = jnp.where(kinds == k, zeta_table[k], zeta)
        scale = jnp.where(kinds == k, escale[k], scale)
    width = kinds.shape[1]
    tiles = width // LANES
    live_row = jnp.full((1, LANES), live[0].astype(F32))
    for t in range(tiles):
        lane = slice(t * LANES, (t + 1) * LANES)
        parts = [pos[:, lane], zeta[:, lane], kinds[:, lane].astype(F32), live_row]
        pack[8 * t : 8 * t + 6, :] = jnp.concatenate(parts, axis=0)
        pack[8 * t + 6 : 8 * t + 7, :] = jnp.zeros((1, LANES), F32)
        pack[8 * t + 7 : 8 * t + 8, :] = scale[:, lane]
    chan = nbr_row.shape[1]
    pack[38:39, :chan] = nbr_row[...]
    pack[38:39, chan : 2 * chan] = out_row[...]
    pack[8 * tiles :, :] = nbr[...].astype(F32)
    index = ghost_index[...]
    index = jnp.concatenate([index, index[:2]], axis=0)
    low, high = index & (LANES - 1), index >> 7
    got = []
    for d in range(4):
        value = jnp.zeros(index.shape, F32)
        for t in range(tiles):
            row = pack[8 * t + d : 8 * t + d + 1, :]
            value = jnp.where(high == t, lookup(row, low), value)
        got.append(value)
    for a, step in enumerate(steps):
        par = parity(step)
        for flip in range(2):
            ahead = par == flip
            for d in range(4):
                first, second = got[d][2 * a : 2 * a + 1], got[d][2 * a + 1 : 2 * a + 2]
                if d == a:
                    first, second = first - BOX_SHIFT, second + BOX_SHIFT
                part = jnp.where(ahead, first, second)
                if a == 0 and flip == 0:
                    pack[8 * d + 6 : 8 * d + 7, :] = part
                else:
                    ref, row = face_slot(sends, a, flip, steps)
                    ref[row + d : row + d + 1, :] = part


def weights_kernel(pack, center_t, radial_t, latent, env, mix, *outs):
    pack_o, out_wide_o, out_row2_o = outs[:3]
    pack_o[...] = pack[...]
    chan = latent.shape[0]
    kinds_total = center_t.shape[0]
    nbr_row, row = pack[38:39, :chan], pack[38:39, chan : 2 * chan]
    norm = NBR ** (-0.5)
    nb = radial_t.shape[0]
    first = jnp.concatenate(
        [radial_t[...], nbr_row, jnp.zeros((LANES - nb - 1, chan), F32)], axis=0
    ).T
    centers = jnp.concatenate([center_t[...], jnp.zeros((LANES - kinds_total, chan), F32)], axis=0).T
    top, rest = halves(0.5 * centers[:, :8])
    w1 = jnp.concatenate([wide(0.5 * first[:, :16]), top, rest], axis=1)
    w2 = wide(0.5 * latent[...])
    mix_a = mix[:, :chan]
    mix_b = mix[:, chan:]
    w3 = wide(jnp.concatenate([0.5 * mix_a, row, jnp.zeros((15, chan), F32)], axis=0))
    both = (0.5 * norm) * mm(wide(mix_b), stack(env[...]))
    out_col = jnp.broadcast_to(row, (LANES, chan)).T
    out_wide_o[...] = jnp.concatenate([out_col, out_col], axis=1)
    _, orest = halves(out_col)
    lane16 = lax.broadcasted_iota(jnp.int32, (chan, 16), 1)
    extra = jnp.where(lane16 == 0, out_col[:, :16], 0.0).astype(BF16)
    extra = extra + jnp.where(lane16 == 1, orest[:, :16].astype(F32), 0.0).astype(BF16)
    w5 = jnp.concatenate([wide(mix_a.T * (0.5 * row)), extra], axis=1)
    out_row2_o[...] = jnp.concatenate([row, row], axis=1)

    def doubled(x):
        top, rest = halves(jnp.concatenate([jnp.concatenate([x, x], axis=0)] * 2, axis=1))
        return jnp.concatenate([top, top, rest], axis=0)

    w4 = doubled(both.T)
    w6 = doubled(out_col[:, :chan] * both)
    w7 = wide(0.5 * latent[...].T)
    last = jnp.concatenate([0.5 * radial_t[...], jnp.zeros((16 - nb, chan), F32)], axis=0)
    top, rest = halves(jnp.concatenate([last, last], axis=1))
    w8 = jnp.concatenate([top, rest], axis=0)
    for ref, value in zip(outs[3:], (w1, w2, w3, w4, w5, w6, w7, w8)):
        ref[...] = value


def edge_kernel(
    live,
    pack,
    mate,
    out_s,
    row2,
    *refs,
    steps,
    batch,
    basis_count,
    lag,
):
    nfaces = 2 * len(steps)
    nsends = sum(1 if merged(step) else 2 for step in steps) - 1
    ghosts = refs[:nsends]
    weights = refs[nsends : nsends + 8]
    own_out, mate_out = refs[nsends + 8 : nsends + 10]
    ghost_out = refs[nsends + 10 : 2 * nsends + 10]
    (
        table,
        lists,
        index_s,
        keep_s,
        basis_s,
        kinds_s,
        geo_s,
        force_s,
        red_s,
        outf_s,
        db_s,
        acc_s,
        own_s,
        df1_s,
        df2_s,
        f2_s,
        ua_s,
        ub_s,
        sel_s,
    ) = refs[2 * nsends + 10 :]
    chan = out_s.shape[0]
    nb = basis_count
    own_tiles = pack.shape[0] // (8 + NBR)
    tiles = own_tiles + nfaces
    group = LANES // BIN_ATOMS
    wide_row = 2 * LANES

    for t in range(own_tiles):
        table[0, t] = pack[8 * t : 8 * t + 8, :]
        table[1, t] = mate[8 * t : 8 * t + 8, :]
    edge_rows = pack.shape[0] - 8 * own_tiles
    lists[:edge_rows, :] = pack[8 * own_tiles :, :]
    lists[edge_rows:, :] = mate[8 * own_tiles :, :]
    for a, step in enumerate(steps):
        par = parity(step)
        for flip in range(2):
            tile = own_tiles + 2 * a + jnp.where(par == flip, 1, 0)
            for d in range(4):
                if a == 0 and flip == 0:
                    row = mate[8 * d + 6 : 8 * d + 7, :]
                else:
                    ref, first = face_slot(ghosts, a, flip, steps)
                    row = ref[first + d : first + d + 1, :]
                table[0, tile, d : d + 1, :] = row
    acc_s[...] = jnp.zeros(acc_s.shape, F32)
    own_s[...] = jnp.zeros(own_s.shape, F32)
    keep_s[...] = jnp.zeros(keep_s.shape, F32)

    w1, w2, w3, w4, w5, w6, w7, w8 = [ref[...] for ref in weights]
    out_row2 = row2[...]
    sub16 = lax.broadcasted_iota(jnp.int32, (16, LANES), 0)
    sub16w = lax.broadcasted_iota(jnp.int32, (16, wide_row), 0)
    ones = jnp.where(sub16w < 2, 1.0, 0.0).astype(BF16)
    from_lane = lax.broadcasted_iota(jnp.int32, (LANES, LANES), 0)
    to_lane = lax.broadcasted_iota(jnp.int32, (LANES, LANES), 1)
    per_row = LANES // NBR
    lane_bf = from_lane.astype(F32).astype(BF16)
    one_bf, zero_bf = jnp.ones((), BF16), jnp.zeros((), BF16)
    sel_s[...] = jnp.where(from_lane // NBR == to_lane % per_row, 1.0, 0.0).astype(BF16)
    sub8 = lax.broadcasted_iota(jnp.int32, (8, LANES), 0)
    lane8 = lax.broadcasted_iota(jnp.int32, (8, LANES), 1)
    masks = [jnp.where(sub8 == h * per_row + lane8 // NBR, 1.0, 0.0) for h in range(2)]
    zero8 = jnp.zeros((8, LANES), F32)
    lower = lax.broadcasted_iota(jnp.int32, (NBR, LANES), 1) < chan

    mine = live[0]
    theirs = jnp.max(mate[5:6, :]).astype(jnp.int32)

    def counts(bins):
        even = ((bins + 1) // 2 + group - 1) // group
        odd = (bins // 2 + group - 1) // group
        return even, odd

    my_even, my_odd = counts(mine)
    their_even, their_odd = counts(theirs)
    excess = my_even + my_odd - their_even - their_odd
    give = jnp.minimum(jnp.maximum(excess, 0) // 2, my_even)
    take = jnp.minimum(jnp.maximum(-excess, 0) // 2, their_even)
    keep_even = my_even - give

    def slope2(u, f):
        return u + f * (2.0 - u)

    def finish(which, kb, odd):
        index = index_s[...].astype(jnp.int32)
        low, high = index & (LANES - 1), index >> 7
        local = 2 * sub8 + odd
        upper = sub8 < 4
        kept = [keep_s[q] for q in range(keep_s.shape[0])]
        sins, coss, unit = kept[:nb], kept[nb : 2 * nb], kept[2 * nb : 2 * nb + 3]
        envelope, x, inv_x, gap, inv_dist, scale_of, occupied = kept[2 * nb + 3 :]

        def collect(ref, q):
            total = ref[q, pl.ds(0, NBR, stride=8), :]
            for k in range(1, 8):
                total = total + ref[q, pl.ds(k, NBR, stride=8), :]
            return total

        pulls = [collect(red_s, 3 + d) for d in range(3)]
        d_unit = [envelope * (collect(red_s, d) + pulls[d]) for d in range(3)]
        d_env = collect(red_s, 6) + outf_s[...]
        for d in range(3):
            d_env = d_env + unit[d] * pulls[d]
        along = jnp.zeros((NBR, LANES), F32)
        level = jnp.zeros((NBR, LANES), F32)
        for k in range(nb):
            g = db_s[pl.ds(k, NBR, stride=8), :]
            ratio = sins[k] * inv_x
            level = level + g * ratio
            along = along + g * ((k + 1) * math.pi * coss[k] - ratio)
        d_env = d_env + envelope * level
        d_x = envelope * envelope * inv_x * along - 4.0 * x * gap * d_env
        radial = d_x * (1.0 / CUTOFF)
        for d in range(3):
            radial = radial - d_unit[d] * unit[d] * inv_dist
        lefts = []
        for d in range(3):
            g = jnp.where(occupied > 0.0, (d_unit[d] * inv_dist + radial * unit[d]) * scale_of, 0.0)
            top = g.astype(BF16).astype(F32)
            force_s[2 * d] = top
            force_s[2 * d + 1] = g - top
            lefts += [top, g - top]
        sums = mm(jnp.concatenate(lefts, axis=0).astype(BF16), sel_s[...])
        own_rows = []
        for d in range(3):
            total = jnp.zeros((8, LANES), F32)
            for part in range(4):
                row = 64 * d + 8 * part
                value = sums[row : row + 8] + sums[row + NBR : row + NBR + 8]
                total = total + jnp.where((lane8 % BIN_ATOMS) // per_row == part, value, 0.0)
            total = jnp.where(lane8 // BIN_ATOMS == local % group, total, 0.0)
            for h in range(2):
                own_rows.append(jnp.sum(jnp.where(upper == (h == 0), total, 0.0), axis=0, keepdims=True))
        for d in range(3):
            for h in range(2):
                own_s[which, d, pl.ds(2 * kb + h, 1), :] += own_rows[2 * d + h]

        lefts, rights = [], []
        index_s[...] = low.astype(F32)
        for n in range(NBR):
            highs = high[n : n + 1]
            lows = jnp.broadcast_to(index_s[n : n + 1, :], (16, LANES)).astype(BF16)
            lows = jnp.concatenate([lows] * (LANES // 16), axis=0)
            rights.append(jnp.where(lane_bf == lows, one_bf, zero_bf))
            hit = sub16 == highs
            rows = [jnp.where(hit, force_s[q, n : n + 1, :], 0.0) for q in range(6)]
            lefts.append(jnp.concatenate(rows, axis=0).astype(BF16))
        for c in range(0, NBR, 8):
            acc_s[which] += mm_nt(jnp.concatenate(lefts[c : c + 8], axis=1), jnp.concatenate(rights[c : c + 8], axis=1))

    def block(i, carry):
        finish(*carry)
        is_mate = i >= keep_even + my_odd
        is_odd = jnp.logical_and(i >= keep_even, jnp.logical_not(is_mate))
        which = jnp.where(is_mate, 1, 0)
        odd = jnp.where(is_odd, 1, 0)
        kb = jnp.where(
            is_mate, their_even - take + i - keep_even - my_odd, jnp.where(is_odd, i - keep_even, i)
        )
        bins = jnp.where(is_mate, theirs, mine)
        start = edge_rows * which + 64 * kb + 4 * odd
        rows = [lists[pl.ds(start + part, 8, stride=8), :] for part in range(4)]
        index = jnp.concatenate(rows, axis=0)
        index_s[...] = index
        index = index.astype(jnp.int32)
        low, high = index & (LANES - 1), index >> 7

        local = 2 * sub8 + odd
        bin_of = 16 * kb + local
        upper = sub8 < 4
        here = []
        for d in (0, 1, 2, 4, 7):
            source = jnp.where(
                upper,
                jnp.broadcast_to(table[which, 2 * kb, d : d + 1, :], (8, LANES)),
                jnp.broadcast_to(table[which, 2 * kb + 1, d : d + 1, :], (8, LANES)),
            )
            found = []
            for part in range(4):
                pick = (local % group) * BIN_ATOMS + part * per_row + lane8 // NBR
                found.append(jnp.take_along_axis(source, pick, axis=1, mode="promise_in_bounds"))
            here.append(jnp.concatenate(found, axis=0))
        kinds = here[3]
        kinds_s[...] = kinds
        occupied = jnp.concatenate([jnp.where(bin_of < bins, 1.0, 0.0)] * 4, axis=0)

        got = []
        for d in range(4):
            value = jnp.zeros((NBR, LANES), F32)
            for t in range(tiles):
                value = jnp.where(high == t, lookup(table[which, t, d : d + 1, :], low), value)
            got.append(value)
        disp = [got[d] - here[d] for d in range(3)]
        square = disp[0] * disp[0] + disp[1] * disp[1] + disp[2] * disp[2]
        dist = jnp.sqrt(square + SOFTEN * SOFTEN)
        inv_dist = 1.0 / dist
        unit = [disp[d] * inv_dist for d in range(3)]
        x = jnp.minimum(dist * (1.0 / CUTOFF), 1.0)
        inv_x = 1.0 / x
        gap = 1.0 - x * x
        envelope = gap * gap
        t = math.pi * (x - 0.5)
        tt = t * t
        s1 = poly(COS_TERMS, tt)
        c1 = -(t * poly(SIN_TERMS, tt))
        sins, coss = [s1], [c1]
        for k in range(2, nb + 1):
            p, q = k // 2 - 1, k - k // 2 - 1
            sins.append(sins[p] * coss[q] + coss[p] * sins[q])
            coss.append(coss[p] * coss[q] - sins[p] * sins[q])
        scale = envelope * inv_x
        for k in range(nb):
            basis_s[pl.ds(k, NBR, stride=16), :] = sins[k] * scale
        basis_s[pl.ds(nb, NBR, stride=16), :] = got[3]
        for k in range(nb + 1, 16):
            basis_s[pl.ds(k, NBR, stride=16), :] = jnp.zeros((NBR, LANES), F32)
        for d in range(3):
            for q, value in ((d, unit[d]), (6 + d, unit[d] * envelope)):
                top = value.astype(BF16).astype(F32)
                geo_s[q] = top
                geo_s[q + 3] = value - top

        def fold8(v):
            return sum(v[8 * j : 8 * j + 8] for j in range(1, chan // 8)) + v[:8]

        def parted(x):
            top = x.astype(BF16).astype(F32)
            return top, x - top

        def terms(top, rest):
            rows = jnp.concatenate([top[:24], top[:24], rest[:24], zero8], axis=0)
            return rows.T[:chan].astype(BF16)

        def centre_sum(both_parts, t):
            found = mm_nt(ub_s[t], both_parts)
            return found[:24] + jnp.where(lower[:24], found[24:], 0.0)

        def spread_rows(sums, weight):
            top, rest = halves(jnp.concatenate(sums, axis=0))
            out = mm(jnp.concatenate([top, rest, top], axis=1), weight)
            return [out[24 * i : 24 * i + 24] for i in range(len(sums))]

        def pieces(q, r):
            return [geo_s[q + d, r : r + 1, :] * masks[r % 2] for d in range(3)]

        def cells(t):
            return [(2 * t + h, h, slice(h * LANES, (h + 1) * LANES)) for h in range(2)]

        z1, z2, z3, direct, sums, lefts, got5, v3, d1 = ({} for _ in range(9))

        def stage_basis(ts):
            for t in ts:
                cols = []
                for r, h, cell in cells(t):
                    hit = sub8.astype(F32) == kinds_s[r : r + 1, :]
                    onehot = jnp.where(hit, 1.0, 0.0)
                    onehot = jnp.concatenate([onehot, onehot], axis=0).astype(BF16)
                    cols.append(stack(basis_s[r * 16 : r * 16 + 16, :], onehot))
                z1[t] = mm(w1, jnp.concatenate(cols, axis=1))

        def stage_units(ts):
            for t in ts:
                for r, h, cell in cells(t):
                    a, b = pieces(0, r), pieces(3, r)
                    ua = jnp.concatenate([*a, *b, *a, zero8], axis=0)
                    ua_s[t, :, cell] = ua.astype(BF16)
                    a, b = pieces(6, r), pieces(9, r)
                    ub = jnp.concatenate([*a, *b], axis=0)
                    ub_s[t, :, cell] = ub.astype(BF16)

        def stage_first(ts):
            for t in ts:
                u = 1.0 + jnp.tanh(z1[t])
                f = z1[t] * u
                df1_s[t] = slope2(u, f)
                z2[t] = mm(w2, stack(f))

        def stage_second(ts):
            for t in ts:
                u = 1.0 + jnp.tanh(z2[t])
                f = z2[t] * u
                df2_s[t] = slope2(u, f)
                top, rest = halves(f)
                both_parts = jnp.concatenate([top, rest], axis=0)
                f2_s[t] = both_parts
                sums[t] = centre_sum(both_parts, t)
                direct[t] = mm(w3, jnp.concatenate([top, rest, top], axis=0))

        def stage_env(ts):
            for t, g in zip(ts, spread_rows([sums[t] for t in ts], w4)):
                lefts[t] = terms(*parted(g))
                top, rest = halves(jnp.concatenate([g * out_row2, zero8], axis=0))
                rest = jnp.where(lower, rest, 0.0)[:, :80]
                lefts[t, 1] = jnp.concatenate([w5, jnp.concatenate([top, rest], axis=1)], axis=0)

        def stage_mix(ts):
            for t in ts:
                z3[t] = mm(lefts[t], ua_s[t])

        def stage_third(ts):
            for t in ts:
                for r, h, cell in cells(t):
                    outf_s[r : r + 1, :] = direct[t][chan : chan + 1, cell]
                z = direct[t][:chan] + z3[t]
                u = 1.0 + jnp.tanh(z)
                f = z * u
                v = slope2(u, f)
                folded = fold8(f * out_s[...])
                for r, h, cell in cells(t):
                    red_s[6, 8 * r : 8 * r + 8, :] = folded[:, cell]
                top, rest = halves(v)
                sums[t] = centre_sum(jnp.concatenate([top, rest], axis=0), t)
                got5[t] = mm(lefts[t, 1], jnp.concatenate([top, rest, top, ones], axis=0))

        def stage_denv(ts):
            for t, g in zip(ts, spread_rows([sums[t] for t in ts], w6)):
                top, rest = parted(g)
                lefts[t] = terms(top, rest)
                lefts[t, 1] = jnp.concatenate([top, rest], axis=0).astype(BF16)
                for r, h, cell in cells(t):
                    for d in range(3):
                        part = got5[t][chan + 8 * d : chan + 8 * d + 8, cell]
                        red_s[d, 8 * r : 8 * r + 8, :] = part * masks[h]

        def stage_back(ts):
            for t in ts:
                v3[t] = mm(lefts[t], ua_s[t])

        def stage_slope2(ts):
            for t in ts:
                v = got5[t][:chan] + v3[t]
                d1[t] = mm(w7, stack(v * df2_s[t]))

        def stage_pull(ts):
            for t in ts:
                pulled = mm(lefts[t, 1], f2_s[t])
                for r, h, cell in cells(t):
                    for d in range(3):
                        part = pulled[8 * d : 8 * d + 8, cell] + pulled[24 + 8 * d : 32 + 8 * d, cell]
                        red_s[3 + d, 8 * r : 8 * r + 8, :] = part * masks[h]

        def stage_slope1(ts):
            for t in ts:
                top, rest = halves(d1[t] * df1_s[t])
                v = mm(w8, jnp.concatenate([top, rest], axis=0))
                v = v[:8] + v[16:24]
                for r, h, cell in cells(t):
                    db_s[8 * r : 8 * r + 8, :] = v[:, cell]

        stages = [
            stage_basis,
            stage_units,
            stage_first,
            stage_second,
            stage_env,
            stage_mix,
            stage_third,
            stage_denv,
            stage_pull,
            stage_back,
            stage_slope2,
            stage_slope1,
        ]
        groups = [range(t0, t0 + batch) for t0 in range(0, NBR // 2, batch)]
        for turn in range(len(stages) + (len(groups) - 1) * lag):
            for i, ts in enumerate(groups):
                if 0 <= turn - i * lag < len(stages):
                    stages[turn - i * lag](ts)

        for q, value in enumerate([*sins, *coss, *unit, envelope, x, inv_x, gap, inv_dist, here[4], occupied]):
            keep_s[q] = value
        return which, kb, odd

    zero = jnp.int32(0)
    last = lax.fori_loop(0, keep_even + my_odd + take, block, (zero, zero, zero))
    finish(*last)

    for d in range(3):
        for which in range(2):
            a = acc_s[which, 32 * d : 32 * d + 16, :] + acc_s[which, 32 * d + 16 : 32 * d + 32, :]
            a = own_s[which, d] - a
            for t in range(own_tiles):
                if which:
                    mate_out[4 * t + d : 4 * t + d + 1, :] = a[t : t + 1]
                else:
                    own_out[d : d + 1, t * LANES : (t + 1) * LANES] = a[t : t + 1]
            if which == 0:
                outf_s[0:16, :] = a
                for c, step in enumerate(steps):
                    par = parity(step)
                    for flip in range(2):
                        row = outf_s[pl.ds(own_tiles + 2 * c + jnp.where(par == flip, 1, 0), 1), :]
                        if c == 0 and flip == 0:
                            mate_out[4 * d + 3 : 4 * d + 4, :] = row
                        else:
                            ref, first = face_slot(ghost_out, c, flip, steps)
                            ref[first + d : first + d + 1, :] = row


def fold_kernel(own, back, ghost_index, *refs, steps):
    returned, out = refs[:-1], refs[-1]
    tiles = own.shape[1] // LANES
    lefts, rights = [], []
    for a, step in enumerate(steps):
        par = parity(step)
        for flip in range(2):
            index = ghost_index[pl.ds(2 * a + jnp.where(par == flip, 0, 1), 1), :]
            low, high = index & (LANES - 1), index >> 7
            hit = lax.broadcasted_iota(jnp.int32, (LANES, LANES), 0) == low
            rights.append(jnp.where(hit, 1.0, 0.0).astype(BF16))
            tile_hit = lax.broadcasted_iota(jnp.int32, (16, LANES), 0) == high
            rows = []
            for d in range(3):
                if a == 0 and flip == 0:
                    value = back[4 * d + 3 : 4 * d + 4, :]
                else:
                    ref, first = face_slot(returned, a, flip, steps)
                    value = ref[first + d : first + d + 1, :]
                rows.extend(halves(jnp.where(tile_hit, value, 0.0)))
            lefts.append(jnp.concatenate(rows, axis=0))
    total = mm_nt(jnp.concatenate(lefts, axis=1), jnp.concatenate(rights, axis=1))
    for d in range(3):
        a = total[32 * d : 32 * d + 16] + total[32 * d + 16 : 32 * d + 32]
        for t in range(tiles):
            lane = slice(t * LANES, (t + 1) * LANES)
            out[d : d + 1, lane] = own[d : d + 1, lane] + back[4 * t + d : 4 * t + d + 1, :] + a[t : t + 1]


VM = functools.partial(pl.BlockSpec, memory_space=pltpu.VMEM)
SM = functools.partial(pl.BlockSpec, memory_space=pltpu.SMEM)
SMALL = pltpu.CompilerParams(vmem_limit_bytes=4 * 1024 * 1024)


def shards(
    positions,
    species,
    live_bins,
    edge_nbr,
    ghost_index,
    zeta_table,
    energy_scale,
    center_embed,
    nbr_embed,
    radial_weight,
    latent_weight,
    env_weight,
    mix_weight,
    out_weight,
):
    size = lax.axis_size("dom")
    atoms = species.shape[0]
    chan = latent_weight.shape[0]
    ghosts = ghost_index.shape[1]
    steps = tuple(o for o, _, s in FACES if s < 0)
    shape = jax.ShapeDtypeStruct

    nbr = edge_nbr.reshape(atoms * NBR // LANES, LANES)
    tiles = atoms // LANES
    swaps = [(step, flip) for step in steps for flip in range(1 if 2 * step == size else 2)]
    buffers = [shape((8 if 2 * step == size else 4, ghosts), F32) for step, _ in swaps[1:]]

    def exchange(parts):
        return [swap(part, size, step, flip) for part, (step, flip) in zip(parts, swaps)]

    pack, *sends = pl.pallas_call(
        functools.partial(prep_kernel, steps=steps),
        out_shape=[shape((8 * tiles + nbr.shape[0], LANES), F32)] + buffers,
        in_specs=[SM(), SM(), SM()] + [VM()] * 6,
        out_specs=[VM()] * (1 + len(buffers)),
        name="prep",
    )(
        zeta_table,
        energy_scale,
        live_bins,
        positions,
        species.reshape(1, atoms),
        ghost_index,
        nbr,
        nbr_embed.reshape(1, chan),
        out_weight.reshape(1, chan),
    )
    mate, *arrived = exchange([pack, *sends])

    heights = [(chan, 64), (chan, 3 * chan), (chan + 16, 3 * chan), (6 * chan, LANES)]
    heights += [(chan, 3 * chan + 16), (6 * chan, LANES), (chan, 3 * chan), (32, LANES)]
    pack_here, out_wide, out_row2, *weights = pl.pallas_call(
        weights_kernel,
        out_shape=[shape(pack.shape, F32), shape((chan, 2 * LANES), F32), shape((1, 2 * chan), F32)]
        + [shape(h, BF16) for h in heights],
        in_specs=[VM()] * 6,
        out_specs=[VM()] * (3 + len(heights)),
        compiler_params=SMALL,
        name="weights",
    )(
        pack,
        center_embed.T,
        radial_weight.T,
        latent_weight,
        env_weight,
        mix_weight,
    )

    pairs = NBR // 2
    big = pltpu.VMEM((pairs, chan, 2 * LANES), F32)
    own, mate_part, *parts = pl.pallas_call(
        functools.partial(edge_kernel, steps=steps, batch=8, lag=1, basis_count=radial_weight.shape[1]),
        out_shape=[shape((3, atoms), F32), shape((4 * tiles, LANES), F32)] + buffers,
        in_specs=[SM()] + [VM()] * (4 + len(buffers) + len(weights)),
        out_specs=[VM()] * (2 + len(buffers)),
        scratch_shapes=[
            pltpu.VMEM((2, 16, 8, LANES), F32),
            pltpu.VMEM((2 * nbr.shape[0], LANES), F32),
            pltpu.VMEM((NBR, LANES), F32),
            pltpu.VMEM((2 * radial_weight.shape[1] + 10, NBR, LANES), F32),
            pltpu.VMEM((NBR * 16, LANES), F32),
            pltpu.VMEM((NBR, LANES), F32),
            pltpu.VMEM((12, NBR, LANES), F32),
            pltpu.VMEM((6, NBR, LANES), F32),
            pltpu.VMEM((7, NBR * 8, LANES), F32),
            pltpu.VMEM((NBR, LANES), F32),
            pltpu.VMEM((NBR * 8, LANES), F32),
            pltpu.VMEM((2, 96, LANES), F32),
            pltpu.VMEM((2, 3, 16, LANES), F32),
            big,
            big,
            pltpu.VMEM((pairs, 2 * chan, 2 * LANES), BF16),
            pltpu.VMEM((pairs, 80, 2 * LANES), BF16),
            pltpu.VMEM((pairs, 48, 2 * LANES), BF16),
            pltpu.VMEM((LANES, LANES), BF16),
        ],
        compiler_params=pltpu.CompilerParams(vmem_limit_bytes=24 * 1024 * 1024),
        name="edges",
    )(live_bins, pack_here, mate, out_wide, out_row2, *arrived, *weights)
    back, *returned = exchange([mate_part, *parts])
    return pl.pallas_call(
        functools.partial(fold_kernel, steps=steps),
        out_shape=shape((3, atoms), F32),
        in_specs=[VM()] * (3 + len(buffers)),
        out_specs=VM(),
        compiler_params=SMALL,
        name="fold",
    )(own, back, ghost_index, *returned)


def solution(mesh):
    in_specs = (
        P(None, ("rep", "dom")),
        P(("rep", "dom")),
        P(("rep", "dom")),
        P(("rep", "dom")),
        P(None, ("rep", "dom")),
        P(),
        P(),
        P(),
        P(),
        P(),
        P(),
        P(),
        P(),
        P(),
    )
    out_specs = P(None, ("rep", "dom"))
    return jax.shard_map(shards, mesh=mesh, in_specs=in_specs, out_specs=out_specs, check_vma=False)
```

```python
import functools
import math

import jax
import jax.numpy as jnp
from jax import lax
from jax.experimental import pallas as pl
from jax.experimental.pallas import tpu as pltpu
from jax.sharding import PartitionSpec as P

NBR = 32
BIN_ATOMS = 16
LANES = 128

FACES = ((1, 0, -1.0), (-1, 0, 1.0), (2, 1, -1.0), (-2, 1, 1.0), (8, 2, -1.0), (-8, 2, 1.0))
CUTOFF = 6.0
SOFTEN = 0.5
BOX_SHIFT = 3.0
F32 = jnp.float32
BF16 = jnp.bfloat16

SIN_TERMS = [(-1.0) ** i / math.factorial(2 * i + 1) for i in range(8)]
COS_TERMS = [(-1.0) ** i / math.factorial(2 * i) for i in range(8)]


def swap(block, size, step, flip):
    def partner(i):
        return (i + step if (i // step) % 2 == flip else i - step) % size

    return lax.ppermute(block, "dom", [(i, partner(i)) for i in range(size)])


def poly(terms, square):
    total = jnp.full_like(square, terms[-1])
    for term in terms[-2::-1]:
        total = total * square + term
    return total


def halves(x):
    top = x.astype(BF16)
    return top, (x - top.astype(F32)).astype(BF16)


def wide(x):
    top, rest = halves(x)
    return jnp.concatenate([top, top, rest], axis=1)


def stack(x, *more):
    top, rest = halves(x)
    return jnp.concatenate([top, rest, top, *more], axis=0)


def mm(left, right):
    return jnp.dot(left, right, preferred_element_type=F32)


def mm_nt(left, right):
    return lax.dot_general(left, right, (((1,), (1,)), ((), ())), preferred_element_type=F32)


def lookup(row, index):
    return jnp.take_along_axis(
        jnp.broadcast_to(row, index.shape), index, axis=1, mode="promise_in_bounds"
    )


def parity(step):
    return (lax.axis_index("dom") // step) % 2


def merged(step):
    return 2 * step == lax.axis_size("dom")


def swap_order(steps):
    pairs = [(a, f) for a, step in enumerate(steps) for f in range(1 if merged(step) else 2)]
    return sorted(pairs, key=lambda p: (p != (0, 0), merged(steps[p[0]]), -p[1], -p[0]))


def face_slot(refs, a, flip, steps):
    both = merged(steps[a])
    place = swap_order(steps).index((a, 0 if both else flip))
    return refs[place - 1], 4 * flip if both else 0


def prep_kernel(
    zeta_table, escale, live, pos, species, ghost_index, nbr, nbr_row, out_row, pack, *sends, steps
):
    kinds = species[...]
    zeta = scale = jnp.zeros(kinds.shape, F32)
    for k in range(zeta_table.shape[0]):
        zeta = jnp.where(kinds == k, zeta_table[k], zeta)
        scale = jnp.where(kinds == k, escale[k], scale)
    width = kinds.shape[1]
    tiles = width // LANES
    live_row = jnp.full((1, LANES), live[0].astype(F32))
    for t in range(tiles):
        lane = slice(t * LANES, (t + 1) * LANES)
        parts = [pos[:, lane], zeta[:, lane], kinds[:, lane].astype(F32), live_row]
        pack[8 * t : 8 * t + 6, :] = jnp.concatenate(parts, axis=0)
        pack[8 * t + 6 : 8 * t + 7, :] = jnp.zeros((1, LANES), F32)
        pack[8 * t + 7 : 8 * t + 8, :] = scale[:, lane]
    chan = nbr_row.shape[1]
    pack[38:39, :chan] = nbr_row[...]
    pack[38:39, chan : 2 * chan] = out_row[...]
    pack[8 * tiles :, :] = nbr[...].astype(F32)
    index = ghost_index[...]
    index = jnp.concatenate([index, index[:2]], axis=0)
    low, high = index & (LANES - 1), index >> 7
    got = []
    for d in range(4):
        value = jnp.zeros(index.shape, F32)
        for t in range(tiles):
            row = pack[8 * t + d : 8 * t + d + 1, :]
            value = jnp.where(high == t, lookup(row, low), value)
        got.append(value)
    for a, step in enumerate(steps):
        par = parity(step)
        for flip in range(2):
            ahead = par == flip
            for d in range(4):
                first, second = got[d][2 * a : 2 * a + 1], got[d][2 * a + 1 : 2 * a + 2]
                if d == a:
                    first, second = first - BOX_SHIFT, second + BOX_SHIFT
                part = jnp.where(ahead, first, second)
                if a == 0 and flip == 0:
                    pack[8 * d + 6 : 8 * d + 7, :] = part
                else:
                    ref, row = face_slot(sends, a, flip, steps)
                    ref[row + d : row + d + 1, :] = part


def weights_kernel(pack, center_t, radial_t, latent, env, mix, *outs):
    pack_o, out_wide_o, out_row2_o = outs[:3]
    pack_o[...] = pack[...]
    chan = latent.shape[0]
    kinds_total = center_t.shape[0]
    nbr_row, row = pack[38:39, :chan], pack[38:39, chan : 2 * chan]
    norm = NBR ** (-0.5)
    nb = radial_t.shape[0]
    first = jnp.concatenate(
        [radial_t[...], nbr_row, jnp.zeros((LANES - nb - 1, chan), F32)], axis=0
    ).T
    centers = jnp.concatenate([center_t[...], jnp.zeros((LANES - kinds_total, chan), F32)], axis=0).T
    top, rest = halves(0.5 * centers[:, :8])
    w1 = jnp.concatenate([wide(0.5 * first[:, :16]), top, rest], axis=1)
    w2 = wide(0.5 * latent[...])
    mix_a = mix[:, :chan]
    mix_b = mix[:, chan:]
    w3 = wide(jnp.concatenate([0.5 * mix_a, row, jnp.zeros((15, chan), F32)], axis=0))
    both = (0.5 * norm) * mm(wide(mix_b), stack(env[...]))
    out_col = jnp.broadcast_to(row, (LANES, chan)).T
    out_wide_o[...] = jnp.concatenate([out_col, out_col], axis=1)
    _, orest = halves(out_col)
    lane16 = lax.broadcasted_iota(jnp.int32, (chan, 16), 1)
    extra = jnp.where(lane16 == 0, out_col[:, :16], 0.0).astype(BF16)
    extra = extra + jnp.where(lane16 == 1, orest[:, :16].astype(F32), 0.0).astype(BF16)
    w5 = jnp.concatenate([wide(mix_a.T * (0.5 * row)), extra], axis=1)
    out_row2_o[...] = jnp.concatenate([row, row], axis=1)

    def doubled(x):
        top, rest = halves(jnp.concatenate([jnp.concatenate([x, x], axis=0)] * 2, axis=1))
        return jnp.concatenate([top, top, rest], axis=0)

    w4 = doubled(both.T)
    w6 = doubled(out_col[:, :chan] * both)
    w7 = wide(0.5 * latent[...].T)
    last = jnp.concatenate([0.5 * radial_t[...], jnp.zeros((16 - nb, chan), F32)], axis=0)
    top, rest = halves(jnp.concatenate([last, last], axis=1))
    w8 = jnp.concatenate([top, rest], axis=0)
    for ref, value in zip(outs[3:], (w1, w2, w3, w4, w5, w6, w7, w8)):
        ref[...] = value


def edge_kernel(
    live,
    pack,
    mate,
    out_s,
    row2,
    *refs,
    steps,
    batch,
    basis_count,
    lag,
):
    nfaces = 2 * len(steps)
    nsends = sum(1 if merged(step) else 2 for step in steps) - 1
    ghosts = refs[:nsends]
    weights = refs[nsends : nsends + 8]
    own_out, mate_out = refs[nsends + 8 : nsends + 10]
    ghost_out = refs[nsends + 10 : 2 * nsends + 10]
    (
        table,
        lists,
        index_s,
        keep_s,
        basis_s,
        kinds_s,
        geo_s,
        force_s,
        red_s,
        outf_s,
        db_s,
        acc_s,
        own_s,
        df1_s,
        df2_s,
        f2_s,
        ua_s,
        ub_s,
        sel_s,
    ) = refs[2 * nsends + 10 :]
    chan = out_s.shape[0]
    nb = basis_count
    own_tiles = pack.shape[0] // (8 + NBR)
    tiles = own_tiles + nfaces
    group = LANES // BIN_ATOMS
    wide_row = 2 * LANES

    for t in range(own_tiles):
        table[0, t] = pack[8 * t : 8 * t + 8, :]
        table[1, t] = mate[8 * t : 8 * t + 8, :]
    edge_rows = pack.shape[0] - 8 * own_tiles
    lists[:edge_rows, :] = pack[8 * own_tiles :, :]
    lists[edge_rows:, :] = mate[8 * own_tiles :, :]
    for a, step in enumerate(steps):
        par = parity(step)
        for flip in range(2):
            tile = own_tiles + 2 * a + jnp.where(par == flip, 1, 0)
            for d in range(4):
                if a == 0 and flip == 0:
                    row = mate[8 * d + 6 : 8 * d + 7, :]
                else:
                    ref, first = face_slot(ghosts, a, flip, steps)
                    row = ref[first + d : first + d + 1, :]
                table[0, tile, d : d + 1, :] = row
    acc_s[...] = jnp.zeros(acc_s.shape, F32)
    own_s[...] = jnp.zeros(own_s.shape, F32)
    keep_s[...] = jnp.zeros(keep_s.shape, F32)

    w1, w2, w3, w4, w5, w6, w7, w8 = [ref[...] for ref in weights]
    out_row2 = row2[...]
    sub16 = lax.broadcasted_iota(jnp.int32, (16, LANES), 0)
    sub16w = lax.broadcasted_iota(jnp.int32, (16, wide_row), 0)
    ones = jnp.where(sub16w < 2, 1.0, 0.0).astype(BF16)
    from_lane = lax.broadcasted_iota(jnp.int32, (LANES, LANES), 0)
    to_lane = lax.broadcasted_iota(jnp.int32, (LANES, LANES), 1)
    per_row = LANES // NBR
    lane_bf = from_lane.astype(F32).astype(BF16)
    one_bf, zero_bf = jnp.ones((), BF16), jnp.zeros((), BF16)
    sel_s[...] = jnp.where(from_lane // NBR == to_lane % per_row, 1.0, 0.0).astype(BF16)
    sub8 = lax.broadcasted_iota(jnp.int32, (8, LANES), 0)
    lane8 = lax.broadcasted_iota(jnp.int32, (8, LANES), 1)
    masks = [jnp.where(sub8 == h * per_row + lane8 // NBR, 1.0, 0.0) for h in range(2)]
    zero8 = jnp.zeros((8, LANES), F32)
    lower = lax.broadcasted_iota(jnp.int32, (NBR, LANES), 1) < chan

    mine = live[0]
    theirs = jnp.max(mate[5:6, :]).astype(jnp.int32)

    def counts(bins):
        even = ((bins + 1) // 2 + group - 1) // group
        odd = (bins // 2 + group - 1) // group
        return even, odd

    my_even, my_odd = counts(mine)
    their_even, their_odd = counts(theirs)
    excess = my_even + my_odd - their_even - their_odd
    give = jnp.minimum(jnp.maximum(excess, 0) // 2, my_even)
    take = jnp.minimum(jnp.maximum(-excess, 0) // 2, their_even)
    keep_even = my_even - give

    def slope2(u, f):
        return u + f * (2.0 - u)

    def finish(which, kb, odd):
        index = index_s[...].astype(jnp.int32)
        low, high = index & (LANES - 1), index >> 7
        local = 2 * sub8 + odd
        upper = sub8 < 4
        kept = [keep_s[q] for q in range(keep_s.shape[0])]
        sins, coss, unit = kept[:nb], kept[nb : 2 * nb], kept[2 * nb : 2 * nb + 3]
        envelope, x, inv_x, gap, inv_dist, scale_of, occupied = kept[2 * nb + 3 :]

        def collect(ref, q):
            total = ref[q, pl.ds(0, NBR, stride=8), :]
            for k in range(1, 8):
                total = total + ref[q, pl.ds(k, NBR, stride=8), :]
            return total

        pulls = [collect(red_s, 3 + d) for d in range(3)]
        d_unit = [envelope * (collect(red_s, d) + pulls[d]) for d in range(3)]
        d_env = collect(red_s, 6) + outf_s[...]
        for d in range(3):
            d_env = d_env + unit[d] * pulls[d]
        along = jnp.zeros((NBR, LANES), F32)
        level = jnp.zeros((NBR, LANES), F32)
        for k in range(nb):
            g = db_s[pl.ds(k, NBR, stride=8), :]
            ratio = sins[k] * inv_x
            level = level + g * ratio
            along = along + g * ((k + 1) * math.pi * coss[k] - ratio)
        d_env = d_env + envelope * level
        d_x = envelope * envelope * inv_x * along - 4.0 * x * gap * d_env
        radial = d_x * (1.0 / CUTOFF)
        for d in range(3):
            radial = radial - d_unit[d] * unit[d] * inv_dist
        lefts = []
        for d in range(3):
            g = jnp.where(occupied > 0.0, (d_unit[d] * inv_dist + radial * unit[d]) * scale_of, 0.0)
            top = g.astype(BF16).astype(F32)
            force_s[2 * d] = top
            force_s[2 * d + 1] = g - top
            lefts += [top, g - top]
        sums = mm(jnp.concatenate(lefts, axis=0).astype(BF16), sel_s[...])
        own_rows = []
        for d in range(3):
            total = jnp.zeros((8, LANES), F32)
            for part in range(4):
                row = 64 * d + 8 * part
                value = sums[row : row + 8] + sums[row + NBR : row + NBR + 8]
                total = total + jnp.where((lane8 % BIN_ATOMS) // per_row == part, value, 0.0)
            total = jnp.where(lane8 // BIN_ATOMS == local % group, total, 0.0)
            for h in range(2):
                own_rows.append(jnp.sum(jnp.where(upper == (h == 0), total, 0.0), axis=0, keepdims=True))
        for d in range(3):
            for h in range(2):
                own_s[which, d, pl.ds(2 * kb + h, 1), :] += own_rows[2 * d + h]

        lefts, rights = [], []
        index_s[...] = low.astype(F32)
        for n in range(NBR):
            highs = high[n : n + 1]
            lows = jnp.broadcast_to(index_s[n : n + 1, :], (16, LANES)).astype(BF16)
            lows = jnp.concatenate([lows] * (LANES // 16), axis=0)
            rights.append(jnp.where(lane_bf == lows, one_bf, zero_bf))
            hit = sub16 == highs
            rows = [jnp.where(hit, force_s[q, n : n + 1, :], 0.0) for q in range(6)]
            lefts.append(jnp.concatenate(rows, axis=0).astype(BF16))
        for c in range(0, NBR, 8):
            acc_s[which] += mm_nt(jnp.concatenate(lefts[c : c + 8], axis=1), jnp.concatenate(rights[c : c + 8], axis=1))

    def block(i, carry):
        finish(*carry)
        is_mate = i >= keep_even + my_odd
        is_odd = jnp.logical_and(i >= keep_even, jnp.logical_not(is_mate))
        which = jnp.where(is_mate, 1, 0)
        odd = jnp.where(is_odd, 1, 0)
        kb = jnp.where(
            is_mate, their_even - take + i - keep_even - my_odd, jnp.where(is_odd, i - keep_even, i)
        )
        bins = jnp.where(is_mate, theirs, mine)
        start = edge_rows * which + 64 * kb + 4 * odd
        rows = [lists[pl.ds(start + part, 8, stride=8), :] for part in range(4)]
        index = jnp.concatenate(rows, axis=0)
        index_s[...] = index
        index = index.astype(jnp.int32)
        low, high = index & (LANES - 1), index >> 7

        local = 2 * sub8 + odd
        bin_of = 16 * kb + local
        upper = sub8 < 4
        here = []
        for d in (0, 1, 2, 4, 7):
            source = jnp.where(
                upper,
                jnp.broadcast_to(table[which, 2 * kb, d : d + 1, :], (8, LANES)),
                jnp.broadcast_to(table[which, 2 * kb + 1, d : d + 1, :], (8, LANES)),
            )
            found = []
            for part in range(4):
                pick = (local % group) * BIN_ATOMS + part * per_row + lane8 // NBR
                found.append(jnp.take_along_axis(source, pick, axis=1, mode="promise_in_bounds"))
            here.append(jnp.concatenate(found, axis=0))
        kinds = here[3]
        kinds_s[...] = kinds
        occupied = jnp.concatenate([jnp.where(bin_of < bins, 1.0, 0.0)] * 4, axis=0)

        got = []
        for d in range(4):
            value = jnp.zeros((NBR, LANES), F32)
            for t in range(tiles):
                value = jnp.where(high == t, lookup(table[which, t, d : d + 1, :], low), value)
            got.append(value)
        disp = [got[d] - here[d] for d in range(3)]
        square = disp[0] * disp[0] + disp[1] * disp[1] + disp[2] * disp[2]
        dist = jnp.sqrt(square + SOFTEN * SOFTEN)
        inv_dist = 1.0 / dist
        unit = [disp[d] * inv_dist for d in range(3)]
        x = jnp.minimum(dist * (1.0 / CUTOFF), 1.0)
        inv_x = 1.0 / x
        gap = 1.0 - x * x
        envelope = gap * gap
        t = math.pi * (x - 0.5)
        tt = t * t
        s1 = poly(COS_TERMS, tt)
        c1 = -(t * poly(SIN_TERMS, tt))
        sins, coss = [s1], [c1]
        for k in range(2, nb + 1):
            p, q = k // 2 - 1, k - k // 2 - 1
            sins.append(sins[p] * coss[q] + coss[p] * sins[q])
            coss.append(coss[p] * coss[q] - sins[p] * sins[q])
        scale = envelope * inv_x
        for k in range(nb):
            basis_s[pl.ds(k, NBR, stride=16), :] = sins[k] * scale
        basis_s[pl.ds(nb, NBR, stride=16), :] = got[3]
        for k in range(nb + 1, 16):
            basis_s[pl.ds(k, NBR, stride=16), :] = jnp.zeros((NBR, LANES), F32)
        for d in range(3):
            for q, value in ((d, unit[d]), (6 + d, unit[d] * envelope)):
                top = value.astype(BF16).astype(F32)
                geo_s[q] = top
                geo_s[q + 3] = value - top

        def fold8(v):
            return sum(v[8 * j : 8 * j + 8] for j in range(1, chan // 8)) + v[:8]

        def parted(x):
            top = x.astype(BF16).astype(F32)
            return top, x - top

        def terms(top, rest):
            rows = jnp.concatenate([top[:24], top[:24], rest[:24], zero8], axis=0)
            return rows.T[:chan].astype(BF16)

        def centre_sum(both_parts, t):
            found = mm_nt(ub_s[t], both_parts)
            return found[:24] + jnp.where(lower[:24], found[24:], 0.0)

        def spread_rows(sums, weight):
            top, rest = halves(jnp.concatenate(sums, axis=0))
            out = mm(jnp.concatenate([top, rest, top], axis=1), weight)
            return [out[24 * i : 24 * i + 24] for i in range(len(sums))]

        def pieces(q, r):
            return [geo_s[q + d, r : r + 1, :] * masks[r % 2] for d in range(3)]

        def cells(t):
            return [(2 * t + h, h, slice(h * LANES, (h + 1) * LANES)) for h in range(2)]

        z1, z2, z3, direct, sums, lefts, got5, v3, d1 = ({} for _ in range(9))

        def stage_basis(ts):
            for t in ts:
                cols = []
                for r, h, cell in cells(t):
                    hit = sub8.astype(F32) == kinds_s[r : r + 1, :]
                    onehot = jnp.where(hit, 1.0, 0.0)
                    onehot = jnp.concatenate([onehot, onehot], axis=0).astype(BF16)
                    cols.append(stack(basis_s[r * 16 : r * 16 + 16, :], onehot))
                z1[t] = mm(w1, jnp.concatenate(cols, axis=1))

        def stage_units(ts):
            for t in ts:
                for r, h, cell in cells(t):
                    a, b = pieces(0, r), pieces(3, r)
                    ua = jnp.concatenate([*a, *b, *a, zero8], axis=0)
                    ua_s[t, :, cell] = ua.astype(BF16)
                    a, b = pieces(6, r), pieces(9, r)
                    ub = jnp.concatenate([*a, *b], axis=0)
                    ub_s[t, :, cell] = ub.astype(BF16)

        def stage_first(ts):
            for t in ts:
                u = 1.0 + jnp.tanh(z1[t])
                f = z1[t] * u
                df1_s[t] = slope2(u, f)
                z2[t] = mm(w2, stack(f))

        def stage_second(ts):
            for t in ts:
                u = 1.0 + jnp.tanh(z2[t])
                f = z2[t] * u
                df2_s[t] = slope2(u, f)
                top, rest = halves(f)
                both_parts = jnp.concatenate([top, rest], axis=0)
                f2_s[t] = both_parts
                sums[t] = centre_sum(both_parts, t)
                direct[t] = mm(w3, jnp.concatenate([top, rest, top], axis=0))

        def stage_env(ts):
            for t, g in zip(ts, spread_rows([sums[t] for t in ts], w4)):
                lefts[t] = terms(*parted(g))
                top, rest = halves(jnp.concatenate([g * out_row2, zero8], axis=0))
                rest = jnp.where(lower, rest, 0.0)[:, :80]
                lefts[t, 1] = jnp.concatenate([w5, jnp.concatenate([top, rest], axis=1)], axis=0)

        def stage_mix(ts):
            for t in ts:
                z3[t] = mm(lefts[t], ua_s[t])

        def stage_third(ts):
            for t in ts:
                for r, h, cell in cells(t):
                    outf_s[r : r + 1, :] = direct[t][chan : chan + 1, cell]
                z = direct[t][:chan] + z3[t]
                u = 1.0 + jnp.tanh(z)
                f = z * u
                v = slope2(u, f)
                folded = fold8(f * out_s[...])
                for r, h, cell in cells(t):
                    red_s[6, 8 * r : 8 * r + 8, :] = folded[:, cell]
                top, rest = halves(v)
                sums[t] = centre_sum(jnp.concatenate([top, rest], axis=0), t)
                got5[t] = mm(lefts[t, 1], jnp.concatenate([top, rest, top, ones], axis=0))

        def stage_denv(ts):
            for t, g in zip(ts, spread_rows([sums[t] for t in ts], w6)):
                top, rest = parted(g)
                lefts[t] = terms(top, rest)
                lefts[t, 1] = jnp.concatenate([top, rest], axis=0).astype(BF16)
                for r, h, cell in cells(t):
                    for d in range(3):
                        part = got5[t][chan + 8 * d : chan + 8 * d + 8, cell]
                        red_s[d, 8 * r : 8 * r + 8, :] = part * masks[h]

        def stage_back(ts):
            for t in ts:
                v3[t] = mm(lefts[t], ua_s[t])

        def stage_slope2(ts):
            for t in ts:
                v = got5[t][:chan] + v3[t]
                d1[t] = mm(w7, stack(v * df2_s[t]))

        def stage_pull(ts):
            for t in ts:
                pulled = mm(lefts[t, 1], f2_s[t])
                for r, h, cell in cells(t):
                    for d in range(3):
                        part = pulled[8 * d : 8 * d + 8, cell] + pulled[24 + 8 * d : 32 + 8 * d, cell]
                        red_s[3 + d, 8 * r : 8 * r + 8, :] = part * masks[h]

        def stage_slope1(ts):
            for t in ts:
                top, rest = halves(d1[t] * df1_s[t])
                v = mm(w8, jnp.concatenate([top, rest], axis=0))
                v = v[:8] + v[16:24]
                for r, h, cell in cells(t):
                    db_s[8 * r : 8 * r + 8, :] = v[:, cell]

        stages = [
            stage_basis,
            stage_units,
            stage_first,
            stage_second,
            stage_env,
            stage_mix,
            stage_third,
            stage_denv,
            stage_pull,
            stage_back,
            stage_slope2,
            stage_slope1,
        ]
        groups = [range(t0, t0 + batch) for t0 in range(0, NBR // 2, batch)]
        for turn in range(len(stages) + (len(groups) - 1) * lag):
            for i, ts in enumerate(groups):
                if 0 <= turn - i * lag < len(stages):
                    stages[turn - i * lag](ts)

        for q, value in enumerate([*sins, *coss, *unit, envelope, x, inv_x, gap, inv_dist, here[4], occupied]):
            keep_s[q] = value
        return which, kb, odd

    zero = jnp.int32(0)
    last = lax.fori_loop(0, keep_even + my_odd + take, block, (zero, zero, zero))
    finish(*last)

    for d in range(3):
        for which in range(2):
            a = acc_s[which, 32 * d : 32 * d + 16, :] + acc_s[which, 32 * d + 16 : 32 * d + 32, :]
            a = own_s[which, d] - a
            for t in range(own_tiles):
                if which:
                    mate_out[4 * t + d : 4 * t + d + 1, :] = a[t : t + 1]
                else:
                    own_out[d : d + 1, t * LANES : (t + 1) * LANES] = a[t : t + 1]
            if which == 0:
                outf_s[0:16, :] = a
                for c, step in enumerate(steps):
                    par = parity(step)
                    for flip in range(2):
                        row = outf_s[pl.ds(own_tiles + 2 * c + jnp.where(par == flip, 1, 0), 1), :]
                        if c == 0 and flip == 0:
                            mate_out[4 * d + 3 : 4 * d + 4, :] = row
                        else:
                            ref, first = face_slot(ghost_out, c, flip, steps)
                            ref[first + d : first + d + 1, :] = row


def fold_kernel(own, back, ghost_index, *refs, steps):
    returned, out = refs[:-1], refs[-1]
    tiles = own.shape[1] // LANES
    lefts, rights = [], []
    for a, step in enumerate(steps):
        par = parity(step)
        for flip in range(2):
            index = ghost_index[pl.ds(2 * a + jnp.where(par == flip, 0, 1), 1), :]
            low, high = index & (LANES - 1), index >> 7
            hit = lax.broadcasted_iota(jnp.int32, (LANES, LANES), 0) == low
            rights.append(jnp.where(hit, 1.0, 0.0).astype(BF16))
            tile_hit = lax.broadcasted_iota(jnp.int32, (16, LANES), 0) == high
            rows = []
            for d in range(3):
                if a == 0 and flip == 0:
                    value = back[4 * d + 3 : 4 * d + 4, :]
                else:
                    ref, first = face_slot(returned, a, flip, steps)
                    value = ref[first + d : first + d + 1, :]
                rows.extend(halves(jnp.where(tile_hit, value, 0.0)))
            lefts.append(jnp.concatenate(rows, axis=0))
    total = mm_nt(jnp.concatenate(lefts, axis=1), jnp.concatenate(rights, axis=1))
    for d in range(3):
        a = total[32 * d : 32 * d + 16] + total[32 * d + 16 : 32 * d + 32]
        for t in range(tiles):
            lane = slice(t * LANES, (t + 1) * LANES)
            out[d : d + 1, lane] = own[d : d + 1, lane] + back[4 * t + d : 4 * t + d + 1, :] + a[t : t + 1]


VM = functools.partial(pl.BlockSpec, memory_space=pltpu.VMEM)
SM = functools.partial(pl.BlockSpec, memory_space=pltpu.SMEM)
SMALL = pltpu.CompilerParams(vmem_limit_bytes=4 * 1024 * 1024)


def shards(
    positions,
    species,
    live_bins,
    edge_nbr,
    ghost_index,
    zeta_table,
    energy_scale,
    center_embed,
    nbr_embed,
    radial_weight,
    latent_weight,
    env_weight,
    mix_weight,
    out_weight,
):
    size = lax.axis_size("dom")
    atoms = species.shape[0]
    chan = latent_weight.shape[0]
    ghosts = ghost_index.shape[1]
    steps = tuple(o for o, _, s in FACES if s < 0)
    shape = jax.ShapeDtypeStruct

    nbr = edge_nbr.reshape(atoms * NBR // LANES, LANES)
    tiles = atoms // LANES
    swaps = [(steps[a], flip) for a, flip in swap_order(steps)]
    buffers = [shape((8 if 2 * step == size else 4, ghosts), F32) for step, _ in swaps[1:]]

    def exchange(parts):
        return [swap(part, size, step, flip) for part, (step, flip) in zip(parts, swaps)]

    pack, *sends = pl.pallas_call(
        functools.partial(prep_kernel, steps=steps),
        out_shape=[shape((8 * tiles + nbr.shape[0], LANES), F32)] + buffers,
        in_specs=[SM(), SM(), SM()] + [VM()] * 6,
        out_specs=[VM()] * (1 + len(buffers)),
        name="prep",
    )(
        zeta_table,
        energy_scale,
        live_bins,
        positions,
        species.reshape(1, atoms),
        ghost_index,
        nbr,
        nbr_embed.reshape(1, chan),
        out_weight.reshape(1, chan),
    )
    mate, *arrived = exchange([pack, *sends])

    heights = [(chan, 64), (chan, 3 * chan), (chan + 16, 3 * chan), (6 * chan, LANES)]
    heights += [(chan, 3 * chan + 16), (6 * chan, LANES), (chan, 3 * chan), (32, LANES)]
    pack_here, out_wide, out_row2, *weights = pl.pallas_call(
        weights_kernel,
        out_shape=[shape(pack.shape, F32), shape((chan, 2 * LANES), F32), shape((1, 2 * chan), F32)]
        + [shape(h, BF16) for h in heights],
        in_specs=[VM()] * 6,
        out_specs=[VM()] * (3 + len(heights)),
        compiler_params=SMALL,
        name="weights",
    )(
        pack,
        center_embed.T,
        radial_weight.T,
        latent_weight,
        env_weight,
        mix_weight,
    )

    pairs = NBR // 2
    big = pltpu.VMEM((pairs, chan, 2 * LANES), F32)
    own, mate_part, *parts = pl.pallas_call(
        functools.partial(edge_kernel, steps=steps, batch=8, lag=1, basis_count=radial_weight.shape[1]),
        out_shape=[shape((3, atoms), F32), shape((4 * tiles, LANES), F32)] + buffers,
        in_specs=[SM()] + [VM()] * (4 + len(buffers) + len(weights)),
        out_specs=[VM()] * (2 + len(buffers)),
        scratch_shapes=[
            pltpu.VMEM((2, 16, 8, LANES), F32),
            pltpu.VMEM((2 * nbr.shape[0], LANES), F32),
            pltpu.VMEM((NBR, LANES), F32),
            pltpu.VMEM((2 * radial_weight.shape[1] + 10, NBR, LANES), F32),
            pltpu.VMEM((NBR * 16, LANES), F32),
            pltpu.VMEM((NBR, LANES), F32),
            pltpu.VMEM((12, NBR, LANES), F32),
            pltpu.VMEM((6, NBR, LANES), F32),
            pltpu.VMEM((7, NBR * 8, LANES), F32),
            pltpu.VMEM((NBR, LANES), F32),
            pltpu.VMEM((NBR * 8, LANES), F32),
            pltpu.VMEM((2, 96, LANES), F32),
            pltpu.VMEM((2, 3, 16, LANES), F32),
            big,
            big,
            pltpu.VMEM((pairs, 2 * chan, 2 * LANES), BF16),
            pltpu.VMEM((pairs, 80, 2 * LANES), BF16),
            pltpu.VMEM((pairs, 48, 2 * LANES), BF16),
            pltpu.VMEM((LANES, LANES), BF16),
        ],
        compiler_params=pltpu.CompilerParams(vmem_limit_bytes=24 * 1024 * 1024),
        name="edges",
    )(live_bins, pack_here, mate, out_wide, out_row2, *arrived, *weights)
    back, *returned = exchange([mate_part, *parts])
    return pl.pallas_call(
        functools.partial(fold_kernel, steps=steps),
        out_shape=shape((3, atoms), F32),
        in_specs=[VM()] * (3 + len(buffers)),
        out_specs=VM(),
        compiler_params=SMALL,
        name="fold",
    )(own, back, ghost_index, *returned)


def solution(mesh):
    in_specs = (
        P(None, ("rep", "dom")),
        P(("rep", "dom")),
        P(("rep", "dom")),
        P(("rep", "dom")),
        P(None, ("rep", "dom")),
        P(),
        P(),
        P(),
        P(),
        P(),
        P(),
        P(),
        P(),
        P(),
    )
    out_specs = P(None, ("rep", "dom"))
    return jax.shard_map(shards, mesh=mesh, in_specs=in_specs, out_specs=out_specs, check_vma=False)
```

```python
import functools
import math

import jax
import jax.numpy as jnp
from jax import lax
from jax.experimental import pallas as pl
from jax.experimental.pallas import tpu as pltpu
from jax.sharding import PartitionSpec as P

NBR = 32
BIN_ATOMS = 16
LANES = 128

FACES = ((1, 0, -1.0), (-1, 0, 1.0), (2, 1, -1.0), (-2, 1, 1.0), (8, 2, -1.0), (-8, 2, 1.0))
CUTOFF = 6.0
SOFTEN = 0.5
BOX_SHIFT = 3.0
F32 = jnp.float32
BF16 = jnp.bfloat16

SIN_TERMS = [(-1.0) ** i / math.factorial(2 * i + 1) for i in range(8)]
COS_TERMS = [(-1.0) ** i / math.factorial(2 * i) for i in range(8)]


def swap(block, size, step, flip):
    def partner(i):
        return (i + step if (i // step) % 2 == flip else i - step) % size

    return lax.ppermute(block, "dom", [(i, partner(i)) for i in range(size)])


def poly(terms, square):
    total = jnp.full_like(square, terms[-1])
    for term in terms[-2::-1]:
        total = total * square + term
    return total


def halves(x):
    top = x.astype(BF16)
    return top, (x - top.astype(F32)).astype(BF16)


def wide(x):
    top, rest = halves(x)
    return jnp.concatenate([top, top, rest], axis=1)


def stack(x, *more):
    top, rest = halves(x)
    return jnp.concatenate([top, rest, top, *more], axis=0)


def mm(left, right):
    return jnp.dot(left, right, preferred_element_type=F32)


def mm_nt(left, right):
    return lax.dot_general(left, right, (((1,), (1,)), ((), ())), preferred_element_type=F32)


def lookup(row, index):
    return jnp.take_along_axis(
        jnp.broadcast_to(row, index.shape), index, axis=1, mode="promise_in_bounds"
    )


def parity(step):
    return (lax.axis_index("dom") // step) % 2


def merged(step):
    return 2 * step == lax.axis_size("dom")


def swap_order(steps):
    pairs = [(a, f) for a, step in enumerate(steps) for f in range(1 if merged(step) else 2)]
    return sorted(pairs, key=lambda p: (p != (0, 0), merged(steps[p[0]]), -p[1], -p[0]))


def face_slot(refs, a, flip, steps):
    both = merged(steps[a])
    place = swap_order(steps).index((a, 0 if both else flip))
    return refs[place - 1], 4 * flip if both else 0


def prep_kernel(
    zeta_table, escale, live, pos, species, ghost_index, nbr, nbr_row, out_row, pack, *sends, steps
):
    kinds = species[...]
    zeta = scale = jnp.zeros(kinds.shape, F32)
    for k in range(zeta_table.shape[0]):
        zeta = jnp.where(kinds == k, zeta_table[k], zeta)
        scale = jnp.where(kinds == k, escale[k], scale)
    width = kinds.shape[1]
    tiles = width // LANES
    live_row = jnp.full((1, LANES), live[0].astype(F32))
    for t in range(tiles):
        lane = slice(t * LANES, (t + 1) * LANES)
        parts = [pos[:, lane], zeta[:, lane], kinds[:, lane].astype(F32), live_row]
        pack[8 * t : 8 * t + 6, :] = jnp.concatenate(parts, axis=0)
        pack[8 * t + 6 : 8 * t + 7, :] = jnp.zeros((1, LANES), F32)
        pack[8 * t + 7 : 8 * t + 8, :] = scale[:, lane]
    chan = nbr_row.shape[1]
    pack[38:39, :chan] = nbr_row[...]
    pack[38:39, chan : 2 * chan] = out_row[...]
    pack[8 * tiles :, :] = nbr[...].astype(F32)
    index = ghost_index[...]
    index = jnp.concatenate([index, index[:2]], axis=0)
    low, high = index & (LANES - 1), index >> 7
    got = []
    for d in range(4):
        value = jnp.zeros(index.shape, F32)
        for t in range(tiles):
            row = pack[8 * t + d : 8 * t + d + 1, :]
            value = jnp.where(high == t, lookup(row, low), value)
        got.append(value)
    for a, step in enumerate(steps):
        par = parity(step)
        for flip in range(2):
            ahead = par == flip
            for d in range(4):
                first, second = got[d][2 * a : 2 * a + 1], got[d][2 * a + 1 : 2 * a + 2]
                if d == a:
                    first, second = first - BOX_SHIFT, second + BOX_SHIFT
                part = jnp.where(ahead, first, second)
                if a == 0 and flip == 0:
                    pack[8 * d + 6 : 8 * d + 7, :] = part
                else:
                    ref, row = face_slot(sends, a, flip, steps)
                    ref[row + d : row + d + 1, :] = part


def weights_kernel(pack, center_t, radial_t, latent, env, mix, *outs):
    pack_o, out_wide_o, out_row2_o = outs[:3]
    pack_o[...] = pack[...]
    chan = latent.shape[0]
    kinds_total = center_t.shape[0]
    nbr_row, row = pack[38:39, :chan], pack[38:39, chan : 2 * chan]
    norm = NBR ** (-0.5)
    nb = radial_t.shape[0]
    first = jnp.concatenate(
        [radial_t[...], nbr_row, jnp.zeros((LANES - nb - 1, chan), F32)], axis=0
    ).T
    centers = jnp.concatenate([center_t[...], jnp.zeros((LANES - kinds_total, chan), F32)], axis=0).T
    top, rest = halves(0.5 * centers[:, :8])
    w1 = jnp.concatenate([wide(0.5 * first[:, :16]), top, rest], axis=1)
    w2 = wide(0.5 * latent[...])
    mix_a = mix[:, :chan]
    mix_b = mix[:, chan:]
    w3 = wide(jnp.concatenate([0.5 * mix_a, row, jnp.zeros((15, chan), F32)], axis=0))
    both = (0.5 * norm) * mm(wide(mix_b), stack(env[...]))
    out_col = jnp.broadcast_to(row, (LANES, chan)).T
    out_wide_o[...] = jnp.concatenate([out_col, out_col], axis=1)
    _, orest = halves(out_col)
    lane16 = lax.broadcasted_iota(jnp.int32, (chan, 16), 1)
    extra = jnp.where(lane16 == 0, out_col[:, :16], 0.0).astype(BF16)
    extra = extra + jnp.where(lane16 == 1, orest[:, :16].astype(F32), 0.0).astype(BF16)
    w5 = jnp.concatenate([wide(mix_a.T * (0.5 * row)), extra], axis=1)
    out_row2_o[...] = jnp.concatenate([row, row], axis=1)

    def doubled(x):
        top, rest = halves(jnp.concatenate([jnp.concatenate([x, x], axis=0)] * 2, axis=1))
        return jnp.concatenate([top, top, rest], axis=0)

    w4 = doubled(both.T)
    w6 = doubled(out_col[:, :chan] * both)
    w7 = wide(0.5 * latent[...].T)
    last = jnp.concatenate([0.5 * radial_t[...], jnp.zeros((16 - nb, chan), F32)], axis=0)
    top, rest = halves(jnp.concatenate([last, last], axis=1))
    w8 = jnp.concatenate([top, rest], axis=0)
    for ref, value in zip(outs[3:], (w1, w2, w3, w4, w5, w6, w7, w8)):
        ref[...] = value


def edge_kernel(
    live,
    pack,
    mate,
    out_s,
    row2,
    *refs,
    steps,
    batch,
    basis_count,
    lag,
):
    nfaces = 2 * len(steps)
    nsends = sum(1 if merged(step) else 2 for step in steps) - 1
    ghosts = refs[:nsends]
    weights = refs[nsends : nsends + 8]
    own_out, mate_out = refs[nsends + 8 : nsends + 10]
    ghost_out = refs[nsends + 10 : 2 * nsends + 10]
    (
        table,
        lists,
        index_s,
        keep_s,
        basis_s,
        kinds_s,
        geo_s,
        force_s,
        red_s,
        outf_s,
        db_s,
        acc_s,
        own_s,
        df1_s,
        df2_s,
        f2_s,
        ua_s,
        ub_s,
        sel_s,
    ) = refs[2 * nsends + 10 :]
    chan = out_s.shape[0]
    nb = basis_count
    own_tiles = pack.shape[0] // (8 + NBR)
    tiles = own_tiles + nfaces
    group = LANES // BIN_ATOMS
    wide_row = 2 * LANES

    for t in range(own_tiles):
        table[0, t] = pack[8 * t : 8 * t + 8, :]
        table[1, t] = mate[8 * t : 8 * t + 8, :]
    edge_rows = pack.shape[0] - 8 * own_tiles
    lists[:edge_rows, :] = pack[8 * own_tiles :, :]
    lists[edge_rows:, :] = mate[8 * own_tiles :, :]
    for a, step in enumerate(steps):
        par = parity(step)
        for flip in range(2):
            tile = own_tiles + 2 * a + jnp.where(par == flip, 1, 0)
            for d in range(4):
                if a == 0 and flip == 0:
                    row = mate[8 * d + 6 : 8 * d + 7, :]
                else:
                    ref, first = face_slot(ghosts, a, flip, steps)
                    row = ref[first + d : first + d + 1, :]
                table[0, tile, d : d + 1, :] = row
    acc_s[...] = jnp.zeros(acc_s.shape, F32)
    own_s[...] = jnp.zeros(own_s.shape, F32)
    keep_s[keep_s.shape[0] - 1] = jnp.zeros((NBR, LANES), F32)

    w1, w2, w3, w4, w5, w6, w7, w8 = [ref[...] for ref in weights]
    out_row2 = row2[...]
    sub16 = lax.broadcasted_iota(jnp.int32, (16, LANES), 0)
    sub16w = lax.broadcasted_iota(jnp.int32, (16, wide_row), 0)
    ones = jnp.where(sub16w < 2, 1.0, 0.0).astype(BF16)
    from_lane = lax.broadcasted_iota(jnp.int32, (LANES, LANES), 0)
    to_lane = lax.broadcasted_iota(jnp.int32, (LANES, LANES), 1)
    per_row = LANES // NBR
    lane_bf = from_lane.astype(F32).astype(BF16)
    one_bf, zero_bf = jnp.ones((), BF16), jnp.zeros((), BF16)
    sel_s[...] = jnp.where(from_lane // NBR == to_lane % per_row, 1.0, 0.0).astype(BF16)
    sub8 = lax.broadcasted_iota(jnp.int32, (8, LANES), 0)
    lane8 = lax.broadcasted_iota(jnp.int32, (8, LANES), 1)
    masks = [jnp.where(sub8 == h * per_row + lane8 // NBR, 1.0, 0.0) for h in range(2)]
    zero8 = jnp.zeros((8, LANES), F32)
    lower = lax.broadcasted_iota(jnp.int32, (NBR, LANES), 1) < chan

    mine = live[0]
    theirs = jnp.max(mate[5:6, :]).astype(jnp.int32)

    def counts(bins):
        even = ((bins + 1) // 2 + group - 1) // group
        odd = (bins // 2 + group - 1) // group
        return even, odd

    my_even, my_odd = counts(mine)
    their_even, their_odd = counts(theirs)
    excess = my_even + my_odd - their_even - their_odd
    give = jnp.minimum(jnp.maximum(excess, 0) // 2, my_even)
    take = jnp.minimum(jnp.maximum(-excess, 0) // 2, their_even)
    keep_even = my_even - give

    def slope2(u, f):
        return u + f * (2.0 - u)

    def finish(which, kb, odd):
        index = index_s[...].astype(jnp.int32)
        low, high = index & (LANES - 1), index >> 7
        local = 2 * sub8 + odd
        upper = sub8 < 4
        kept = [keep_s[q] for q in range(keep_s.shape[0])]
        sins, coss, unit = kept[:nb], kept[nb : 2 * nb], kept[2 * nb : 2 * nb + 3]
        envelope, x, inv_x, gap, inv_dist, scale_of, occupied = kept[2 * nb + 3 :]

        def collect(ref, q):
            total = ref[q, pl.ds(0, NBR, stride=8), :]
            for k in range(1, 8):
                total = total + ref[q, pl.ds(k, NBR, stride=8), :]
            return total

        pulls = [collect(red_s, 3 + d) for d in range(3)]
        d_unit = [envelope * (collect(red_s, d) + pulls[d]) for d in range(3)]
        d_env = collect(red_s, 6) + outf_s[...]
        for d in range(3):
            d_env = d_env + unit[d] * pulls[d]
        along = jnp.zeros((NBR, LANES), F32)
        level = jnp.zeros((NBR, LANES), F32)
        for k in range(nb):
            g = db_s[pl.ds(k, NBR, stride=8), :]
            ratio = sins[k] * inv_x
            level = level + g * ratio
            along = along + g * ((k + 1) * math.pi * coss[k] - ratio)
        d_env = d_env + envelope * level
        d_x = envelope * envelope * inv_x * along - 4.0 * x * gap * d_env
        radial = d_x * (1.0 / CUTOFF)
        for d in range(3):
            radial = radial - d_unit[d] * unit[d] * inv_dist
        lefts = []
        for d in range(3):
            g = jnp.where(occupied > 0.0, (d_unit[d] * inv_dist + radial * unit[d]) * scale_of, 0.0)
            top = g.astype(BF16).astype(F32)
            force_s[2 * d] = top
            force_s[2 * d + 1] = g - top
            lefts += [top, g - top]
        sums = mm(jnp.concatenate(lefts, axis=0).astype(BF16), sel_s[...])
        own_rows = []
        for d in range(3):
            total = jnp.zeros((8, LANES), F32)
            for part in range(4):
                row = 64 * d + 8 * part
                value = sums[row : row + 8] + sums[row + NBR : row + NBR + 8]
                total = total + jnp.where((lane8 % BIN_ATOMS) // per_row == part, value, 0.0)
            total = jnp.where(lane8 // BIN_ATOMS == local % group, total, 0.0)
            for h in range(2):
                own_rows.append(jnp.sum(jnp.where(upper == (h == 0), total, 0.0), axis=0, keepdims=True))
        for d in range(3):
            for h in range(2):
                own_s[which, d, pl.ds(2 * kb + h, 1), :] += own_rows[2 * d + h]

        lefts, rights = [], []
        index_s[...] = low.astype(F32)
        for n in range(NBR):
            highs = high[n : n + 1]
            lows = jnp.broadcast_to(index_s[n : n + 1, :], (16, LANES)).astype(BF16)
            lows = jnp.concatenate([lows] * (LANES // 16), axis=0)
            rights.append(jnp.where(lane_bf == lows, one_bf, zero_bf))
            hit = sub16 == highs
            rows = [jnp.where(hit, force_s[q, n : n + 1, :], 0.0) for q in range(6)]
            lefts.append(jnp.concatenate(rows, axis=0).astype(BF16))
        for c in range(0, NBR, 8):
            acc_s[which] += mm_nt(jnp.concatenate(lefts[c : c + 8], axis=1), jnp.concatenate(rights[c : c + 8], axis=1))

    def block(i, carry):
        finish(*carry)
        is_mate = i >= keep_even + my_odd
        is_odd = jnp.logical_and(i >= keep_even, jnp.logical_not(is_mate))
        which = jnp.where(is_mate, 1, 0)
        odd = jnp.where(is_odd, 1, 0)
        kb = jnp.where(
            is_mate, their_even - take + i - keep_even - my_odd, jnp.where(is_odd, i - keep_even, i)
        )
        bins = jnp.where(is_mate, theirs, mine)
        start = edge_rows * which + 64 * kb + 4 * odd
        rows = [lists[pl.ds(start + part, 8, stride=8), :] for part in range(4)]
        index = jnp.concatenate(rows, axis=0)
        index_s[...] = index
        index = index.astype(jnp.int32)
        low, high = index & (LANES - 1), index >> 7

        local = 2 * sub8 + odd
        bin_of = 16 * kb + local
        upper = sub8 < 4
        here = []
        for d in (0, 1, 2, 4, 7):
            source = jnp.where(
                upper,
                jnp.broadcast_to(table[which, 2 * kb, d : d + 1, :], (8, LANES)),
                jnp.broadcast_to(table[which, 2 * kb + 1, d : d + 1, :], (8, LANES)),
            )
            found = []
            for part in range(4):
                pick = (local % group) * BIN_ATOMS + part * per_row + lane8 // NBR
                found.append(jnp.take_along_axis(source, pick, axis=1, mode="promise_in_bounds"))
            here.append(jnp.concatenate(found, axis=0))
        kinds = here[3]
        kinds_s[...] = kinds
        occupied = jnp.concatenate([jnp.where(bin_of < bins, 1.0, 0.0)] * 4, axis=0)

        got = []
        for d in range(4):
            value = jnp.zeros((NBR, LANES), F32)
            for t in range(tiles):
                value = jnp.where(high == t, lookup(table[which, t, d : d + 1, :], low), value)
            got.append(value)
        disp = [got[d] - here[d] for d in range(3)]
        square = disp[0] * disp[0] + disp[1] * disp[1] + disp[2] * disp[2]
        dist = jnp.sqrt(square + SOFTEN * SOFTEN)
        inv_dist = 1.0 / dist
        unit = [disp[d] * inv_dist for d in range(3)]
        x = jnp.minimum(dist * (1.0 / CUTOFF), 1.0)
        inv_x = 1.0 / x
        gap = 1.0 - x * x
        envelope = gap * gap
        t = math.pi * (x - 0.5)
        tt = t * t
        s1 = poly(COS_TERMS, tt)
        c1 = -(t * poly(SIN_TERMS, tt))
        sins, coss = [s1], [c1]
        for k in range(2, nb + 1):
            p, q = k // 2 - 1, k - k // 2 - 1
            sins.append(sins[p] * coss[q] + coss[p] * sins[q])
            coss.append(coss[p] * coss[q] - sins[p] * sins[q])
        scale = envelope * inv_x
        for k in range(nb):
            basis_s[pl.ds(k, NBR, stride=16), :] = sins[k] * scale
        basis_s[pl.ds(nb, NBR, stride=16), :] = got[3]
        for k in range(nb + 1, 16):
            basis_s[pl.ds(k, NBR, stride=16), :] = jnp.zeros((NBR, LANES), F32)
        for d in range(3):
            for q, value in ((d, unit[d]), (6 + d, unit[d] * envelope)):
                top = value.astype(BF16).astype(F32)
                geo_s[q] = top
                geo_s[q + 3] = value - top

        def fold8(v):
            return sum(v[8 * j : 8 * j + 8] for j in range(1, chan // 8)) + v[:8]

        def parted(x):
            top = x.astype(BF16).astype(F32)
            return top, x - top

        def terms(top, rest):
            rows = jnp.concatenate([top[:24], top[:24], rest[:24], zero8], axis=0)
            return rows.T[:chan].astype(BF16)

        def centre_sum(both_parts, t):
            found = mm_nt(ub_s[t], both_parts)
            return found[:24] + jnp.where(lower[:24], found[24:], 0.0)

        def spread_rows(sums, weight):
            top, rest = halves(jnp.concatenate(sums, axis=0))
            out = mm(jnp.concatenate([top, rest, top], axis=1), weight)
            return [out[24 * i : 24 * i + 24] for i in range(len(sums))]

        def pieces(q, r):
            return [geo_s[q + d, r : r + 1, :] * masks[r % 2] for d in range(3)]

        def cells(t):
            return [(2 * t + h, h, slice(h * LANES, (h + 1) * LANES)) for h in range(2)]

        z1, z2, z3, direct, sums, lefts, got5, v3, d1 = ({} for _ in range(9))

        def stage_basis(ts):
            for t in ts:
                cols = []
                for r, h, cell in cells(t):
                    hit = sub8.astype(F32) == kinds_s[r : r + 1, :]
                    onehot = jnp.where(hit, 1.0, 0.0)
                    onehot = jnp.concatenate([onehot, onehot], axis=0).astype(BF16)
                    cols.append(stack(basis_s[r * 16 : r * 16 + 16, :], onehot))
                z1[t] = mm(w1, jnp.concatenate(cols, axis=1))

        def stage_units(ts):
            for t in ts:
                for r, h, cell in cells(t):
                    a, b = pieces(0, r), pieces(3, r)
                    ua = jnp.concatenate([*a, *b, *a, zero8], axis=0)
                    ua_s[t, :, cell] = ua.astype(BF16)
                    a, b = pieces(6, r), pieces(9, r)
                    ub = jnp.concatenate([*a, *b], axis=0)
                    ub_s[t, :, cell] = ub.astype(BF16)

        def stage_first(ts):
            for t in ts:
                u = 1.0 + jnp.tanh(z1[t])
                f = z1[t] * u
                df1_s[t] = slope2(u, f)
                z2[t] = mm(w2, stack(f))

        def stage_second(ts):
            for t in ts:
                u = 1.0 + jnp.tanh(z2[t])
                f = z2[t] * u
                df2_s[t] = slope2(u, f)
                top, rest = halves(f)
                both_parts = jnp.concatenate([top, rest], axis=0)
                f2_s[t] = both_parts
                sums[t] = centre_sum(both_parts, t)
                direct[t] = mm(w3, jnp.concatenate([top, rest, top], axis=0))

        def stage_env(ts):
            for t, g in zip(ts, spread_rows([sums[t] for t in ts], w4)):
                lefts[t] = terms(*parted(g))
                top, rest = halves(jnp.concatenate([g * out_row2, zero8], axis=0))
                rest = jnp.where(lower, rest, 0.0)[:, :80]
                lefts[t, 1] = jnp.concatenate([w5, jnp.concatenate([top, rest], axis=1)], axis=0)

        def stage_mix(ts):
            for t in ts:
                z3[t] = mm(lefts[t], ua_s[t])

        def stage_third(ts):
            for t in ts:
                for r, h, cell in cells(t):
                    outf_s[r : r + 1, :] = direct[t][chan : chan + 1, cell]
                z = direct[t][:chan] + z3[t]
                u = 1.0 + jnp.tanh(z)
                f = z * u
                v = slope2(u, f)
                folded = fold8(f * out_s[...])
                for r, h, cell in cells(t):
                    red_s[6, 8 * r : 8 * r + 8, :] = folded[:, cell]
                top, rest = halves(v)
                got5[t] = mm(lefts[t, 1], jnp.concatenate([top, rest, top, ones], axis=0))
                sums[t] = centre_sum(jnp.concatenate([top, rest], axis=0), t)

        def stage_denv(ts):
            for t, g in zip(ts, spread_rows([sums[t] for t in ts], w6)):
                top, rest = parted(g)
                lefts[t] = terms(top, rest)
                lefts[t, 1] = jnp.concatenate([top, rest], axis=0).astype(BF16)
                for r, h, cell in cells(t):
                    for d in range(3):
                        part = got5[t][chan + 8 * d : chan + 8 * d + 8, cell]
                        red_s[d, 8 * r : 8 * r + 8, :] = part * masks[h]

        def stage_back(ts):
            for t in ts:
                v3[t] = mm(lefts[t], ua_s[t])

        def stage_slope2(ts):
            for t in ts:
                v = got5[t][:chan] + v3[t]
                d1[t] = mm(w7, stack(v * df2_s[t]))

        def stage_pull(ts):
            for t in ts:
                pulled = mm(lefts[t, 1], f2_s[t])
                for r, h, cell in cells(t):
                    for d in range(3):
                        part = pulled[8 * d : 8 * d + 8, cell] + pulled[24 + 8 * d : 32 + 8 * d, cell]
                        red_s[3 + d, 8 * r : 8 * r + 8, :] = part * masks[h]

        def stage_slope1(ts):
            for t in ts:
                top, rest = halves(d1[t] * df1_s[t])
                v = mm(w8, jnp.concatenate([top, rest], axis=0))
                v = v[:8] + v[16:24]
                for r, h, cell in cells(t):
                    db_s[8 * r : 8 * r + 8, :] = v[:, cell]

        stages = [
            stage_basis,
            stage_units,
            stage_first,
            stage_second,
            stage_env,
            stage_mix,
            stage_third,
            stage_denv,
            stage_pull,
            stage_back,
            stage_slope2,
            stage_slope1,
        ]
        groups = [range(t0, t0 + batch) for t0 in range(0, NBR // 2, batch)]
        for turn in range(len(stages) + (len(groups) - 1) * lag):
            for i, ts in enumerate(groups):
                if 0 <= turn - i * lag < len(stages):
                    stages[turn - i * lag](ts)

        for q, value in enumerate([*sins, *coss, *unit, envelope, x, inv_x, gap, inv_dist, here[4], occupied]):
            keep_s[q] = value
        return which, kb, odd

    zero = jnp.int32(0)
    last = lax.fori_loop(0, keep_even + my_odd + take, block, (zero, zero, zero))
    finish(*last)

    for d in range(3):
        for which in range(2):
            a = acc_s[which, 32 * d : 32 * d + 16, :] + acc_s[which, 32 * d + 16 : 32 * d + 32, :]
            a = own_s[which, d] - a
            for t in range(own_tiles):
                if which:
                    mate_out[4 * t + d : 4 * t + d + 1, :] = a[t : t + 1]
                else:
                    own_out[d : d + 1, t * LANES : (t + 1) * LANES] = a[t : t + 1]
            if which == 0:
                outf_s[0:16, :] = a
                for c, step in enumerate(steps):
                    par = parity(step)
                    for flip in range(2):
                        row = outf_s[pl.ds(own_tiles + 2 * c + jnp.where(par == flip, 1, 0), 1), :]
                        if c == 0 and flip == 0:
                            mate_out[4 * d + 3 : 4 * d + 4, :] = row
                        else:
                            ref, first = face_slot(ghost_out, c, flip, steps)
                            ref[first + d : first + d + 1, :] = row


def fold_kernel(own, back, ghost_index, *refs, steps):
    returned, out = refs[:-1], refs[-1]
    tiles = own.shape[1] // LANES
    lefts, rights = [], []
    for a, step in enumerate(steps):
        par = parity(step)
        for flip in range(2):
            index = ghost_index[pl.ds(2 * a + jnp.where(par == flip, 0, 1), 1), :]
            low, high = index & (LANES - 1), index >> 7
            hit = lax.broadcasted_iota(jnp.int32, (LANES, LANES), 0) == low
            rights.append(jnp.where(hit, 1.0, 0.0).astype(BF16))
            tile_hit = lax.broadcasted_iota(jnp.int32, (16, LANES), 0) == high
            rows = []
            for d in range(3):
                if a == 0 and flip == 0:
                    value = back[4 * d + 3 : 4 * d + 4, :]
                else:
                    ref, first = face_slot(returned, a, flip, steps)
                    value = ref[first + d : first + d + 1, :]
                rows.extend(halves(jnp.where(tile_hit, value, 0.0)))
            lefts.append(jnp.concatenate(rows, axis=0))
    total = mm_nt(jnp.concatenate(lefts, axis=1), jnp.concatenate(rights, axis=1))
    for d in range(3):
        a = total[32 * d : 32 * d + 16] + total[32 * d + 16 : 32 * d + 32]
        for t in range(tiles):
            lane = slice(t * LANES, (t + 1) * LANES)
            out[d : d + 1, lane] = own[d : d + 1, lane] + back[4 * t + d : 4 * t + d + 1, :] + a[t : t + 1]


VM = functools.partial(pl.BlockSpec, memory_space=pltpu.VMEM)
SM = functools.partial(pl.BlockSpec, memory_space=pltpu.SMEM)
SMALL = pltpu.CompilerParams(vmem_limit_bytes=4 * 1024 * 1024)


def shards(
    positions,
    species,
    live_bins,
    edge_nbr,
    ghost_index,
    zeta_table,
    energy_scale,
    center_embed,
    nbr_embed,
    radial_weight,
    latent_weight,
    env_weight,
    mix_weight,
    out_weight,
):
    size = lax.axis_size("dom")
    atoms = species.shape[0]
    chan = latent_weight.shape[0]
    ghosts = ghost_index.shape[1]
    steps = tuple(o for o, _, s in FACES if s < 0)
    shape = jax.ShapeDtypeStruct

    nbr = edge_nbr.reshape(atoms * NBR // LANES, LANES)
    tiles = atoms // LANES
    swaps = [(steps[a], flip) for a, flip in swap_order(steps)]
    buffers = [shape((8 if 2 * step == size else 4, ghosts), F32) for step, _ in swaps[1:]]

    def exchange(parts):
        return [swap(part, size, step, flip) for part, (step, flip) in zip(parts, swaps)]

    pack, *sends = pl.pallas_call(
        functools.partial(prep_kernel, steps=steps),
        out_shape=[shape((8 * tiles + nbr.shape[0], LANES), F32)] + buffers,
        in_specs=[SM(), SM(), SM()] + [VM()] * 6,
        out_specs=[VM()] * (1 + len(buffers)),
        name="prep",
    )(
        zeta_table,
        energy_scale,
        live_bins,
        positions,
        species.reshape(1, atoms),
        ghost_index,
        nbr,
        nbr_embed.reshape(1, chan),
        out_weight.reshape(1, chan),
    )
    mate, *arrived = exchange([pack, *sends])

    heights = [(chan, 64), (chan, 3 * chan), (chan + 16, 3 * chan), (6 * chan, LANES)]
    heights += [(chan, 3 * chan + 16), (6 * chan, LANES), (chan, 3 * chan), (32, LANES)]
    pack_here, out_wide, out_row2, *weights = pl.pallas_call(
        weights_kernel,
        out_shape=[shape(pack.shape, F32), shape((chan, 2 * LANES), F32), shape((1, 2 * chan), F32)]
        + [shape(h, BF16) for h in heights],
        in_specs=[VM()] * 6,
        out_specs=[VM()] * (3 + len(heights)),
        compiler_params=SMALL,
        name="weights",
    )(
        pack,
        center_embed.T,
        radial_weight.T,
        latent_weight,
        env_weight,
        mix_weight,
    )

    pairs = NBR // 2
    big = pltpu.VMEM((pairs, chan, 2 * LANES), F32)
    own, mate_part, *parts = pl.pallas_call(
        functools.partial(edge_kernel, steps=steps, batch=8, lag=1, basis_count=radial_weight.shape[1]),
        out_shape=[shape((3, atoms), F32), shape((4 * tiles, LANES), F32)] + buffers,
        in_specs=[SM()] + [VM()] * (4 + len(buffers) + len(weights)),
        out_specs=[VM()] * (2 + len(buffers)),
        scratch_shapes=[
            pltpu.VMEM((2, 16, 8, LANES), F32),
            pltpu.VMEM((2 * nbr.shape[0], LANES), F32),
            pltpu.VMEM((NBR, LANES), F32),
            pltpu.VMEM((2 * radial_weight.shape[1] + 10, NBR, LANES), F32),
            pltpu.VMEM((NBR * 16, LANES), F32),
            pltpu.VMEM((NBR, LANES), F32),
            pltpu.VMEM((12, NBR, LANES), F32),
            pltpu.VMEM((6, NBR, LANES), F32),
            pltpu.VMEM((7, NBR * 8, LANES), F32),
            pltpu.VMEM((NBR, LANES), F32),
            pltpu.VMEM((NBR * 8, LANES), F32),
            pltpu.VMEM((2, 96, LANES), F32),
            pltpu.VMEM((2, 3, 16, LANES), F32),
            big,
            big,
            pltpu.VMEM((pairs, 2 * chan, 2 * LANES), BF16),
            pltpu.VMEM((pairs, 80, 2 * LANES), BF16),
            pltpu.VMEM((pairs, 48, 2 * LANES), BF16),
            pltpu.VMEM((LANES, LANES), BF16),
        ],
        compiler_params=pltpu.CompilerParams(vmem_limit_bytes=24 * 1024 * 1024),
        name="edges",
    )(live_bins, pack_here, mate, out_wide, out_row2, *arrived, *weights)
    back, *returned = exchange([mate_part, *parts])
    return pl.pallas_call(
        functools.partial(fold_kernel, steps=steps),
        out_shape=shape((3, atoms), F32),
        in_specs=[VM()] * (3 + len(buffers)),
        out_specs=VM(),
        compiler_params=SMALL,
        name="fold",
    )(own, back, ghost_index, *returned)


def solution(mesh):
    in_specs = (
        P(None, ("rep", "dom")),
        P(("rep", "dom")),
        P(("rep", "dom")),
        P(("rep", "dom")),
        P(None, ("rep", "dom")),
        P(),
        P(),
        P(),
        P(),
        P(),
        P(),
        P(),
        P(),
        P(),
    )
    out_specs = P(None, ("rep", "dom"))
    return jax.shard_map(shards, mesh=mesh, in_specs=in_specs, out_specs=out_specs, check_vma=False)
```
